32 devices in a mesh: dp: 8 (over z, x), tp: 4 (over y, core).
Axes of the slice: x: 2, y: 2, z: 4, core: 2. Of those that a mesh axis runs over, the one named last changes fastest.
Arguments:
- images: float32 [8, 96, 96, 180], P('dp', 'tp'), may hold values from -6 to 6
- item_sizes: int32 [8], P('dp'), may hold values from 48 to 96, as said below
- cotangent: float32 [8, 96, 96, 180], P('dp', 'tp'), may hold values from -6 to 6
- pre_gain: float32 [180], P('tp'), may hold values from 0.1 to 1.9
- pre_shift: float32 [180], P('tp'), may hold values from -3 to 3
- qkv_weight: float32 [180, 540], P(None, 'tp'), may hold values from -0.4375 to 0.4375
- qv_bias: float32 [360], P('tp'), may hold values from -3 to 3
- rel_table: float32 [225, 6], replicated, may hold values from -3 to 3
- proj_weight: float32 [180, 180], P('tp'), may hold values from -1.75 to 1.75
- proj_bias: float32 [180], P('tp'), may hold values from -3 to 3
- mid_gain: float32 [180], P('tp'), may hold values from 0.1 to 1.9
- mid_shift: float32 [180], P('tp'), may hold values from -3 to 3
- up_weight: float32 [180, 360], P(None, 'tp'), may hold values from -0.4375 to 0.4375
- up_bias: float32 [360], P('tp'), may hold values from -3 to 3
- down_weight: float32 [360, 180], P('tp'), may hold values from -0.3125 to 0.3125
- down_bias: float32 [180], P('tp'), may hold values from -3 to 3
- conv_kernel: float32 [3, 3, 180, 180], P(None, None, None, 'tp'), may hold values from -0.15625 to 0.15625
- conv_bias: float32 [180], P('tp'), may hold values from -3 to 3
Outputs:
- block_out: float32 [8, 96, 96, 180], P('dp', 'tp')
- grad_images: float32 [8, 96, 96, 180], P('dp', 'tp')
- grad_pre_gain: float32 [180], P('tp')
- grad_pre_shift: float32 [180], P('tp')
- grad_qkv_weight: float32 [180, 540], P(None, 'tp')
- grad_qv_bias: float32 [360], P('tp')
- grad_rel_table: float32 [225, 6], replicated
- grad_proj_weight: float32 [180, 180], P('tp')
- grad_proj_bias: float32 [180], P('tp')
- grad_mid_gain: float32 [180], P('tp')
- grad_mid_shift: float32 [180], P('tp')
- grad_up_weight: float32 [180, 360], P(None, 'tp')
- grad_up_bias: float32 [360], P('tp')
- grad_down_weight: float32 [360, 180], P('tp')
- grad_down_bias: float32 [180], P('tp')
- grad_conv_kernel: float32 [3, 3, 180, 180], P(None, None, None, 'tp')
- grad_conv_bias: float32 [180], P('tp')
The draws below stay inside these ranges and needn't reach their ends.
Inputs may be any that keep to these rules, and one draw needn't show every extreme that they name: `item_sizes`: each image's valid side is 48, 64 or 96; in each aligned group of 4 consecutive images at least one has the full side 96.
All inputs are finite; a program needn't handle non-finite values.
Results may differ from the reference program's by a relative error of at most 0.0003.
Values sent between devices are 32-bit elements; how exact they have to be, the bound alone decides.
No kernel may reach another device: no remote copies, remote signals or barrier semaphores. Data moves between devices by JAX's collectives and lax.ppermute only.
A program may use at most 192 MiB of HBM per device.

```python
import jax
import jax.numpy as jnp
from jax import lax

D = 180
HEADS = 6
HID = 360
WIN = 8
IMG = 96
HD = 30
SHIFT = 4
RPOS = 225
N_IMG = 8


def draw_item_sizes(key, part):
    key = jax.random.fold_in(key, 11)
    first, second = jax.random.split(key)
    levels = jnp.array([IMG // 2, 2 * IMG // 3, IMG], dtype=jnp.int32)
    picks = jax.random.randint(first, (N_IMG,), 0, 3)
    chosen = levels[picks]
    groups = N_IMG // 4
    leader = jax.random.randint(second, (groups,), 0, 4)
    slot = jnp.arange(N_IMG, dtype=jnp.int32) % 4
    owner = jnp.repeat(leader, 4)
    return jnp.where(slot == owner, IMG, chosen).astype(jnp.int32)


def block_scale(key, shape, shards, least, top_value):
    def one(axis_at, parts):
        draws = jax.random.uniform(jax.random.fold_in(jax.random.fold_in(key, 6), axis_at), (parts,), jnp.float32, least / len(shards), top_value / len(shards))
        return jnp.repeat(jnp.exp(draws), shape[axis_at] // parts).reshape((-1,) + (1,) * (len(shape) - axis_at - 1))

    level = one(*shards[0])
    for cut in shards[1:]:
        level = level * one(*cut)
    return level


def scatter_about(rng, extent, deviation, limit, cuts=(), kind=jnp.bfloat16):
    level = block_scale(rng, extent, cuts, -0.22, 0.18) if cuts else 1.0
    result = jax.random.normal(rng, extent, jnp.float32) * deviation * level
    return jnp.minimum(jnp.maximum(result, -limit), limit).astype(kind)


def setup_inputs(seed: int = 0) -> dict:
    key_list = jax.random.split(jax.random.key(seed), 19)
    images = scatter_about(key_list[0], (N_IMG, IMG, IMG, D), 1.0, 6.0, ((0, 8), (1, 4)), jnp.float32)
    item_sizes = draw_item_sizes(jax.random.fold_in(key_list[18], 71), 0)
    cotangent = scatter_about(key_list[2], (N_IMG, IMG, IMG, D), 1.0, 6.0, ((0, 8), (1, 4)), jnp.float32)
    pre_gain = jnp.clip(1.0 + 0.18 * jax.random.normal(key_list[3], (D,), jnp.float32), 0.1, 1.9)
    pre_shift = scatter_about(key_list[4], (D,), 0.3, 3.0, ((0, 4),), jnp.float32)
    qkv_weight = scatter_about(key_list[5], (D, 3 * D), D ** -0.5, 0.4375, ((1, 4),), jnp.float32)
    qv_bias = scatter_about(key_list[6], (2 * D,), 0.5, 3.0, ((0, 4),), jnp.float32)
    rel_table = scatter_about(key_list[7], (RPOS, HEADS), 0.5, 3.0, (), jnp.float32)
    proj_weight = scatter_about(key_list[8], (D, D), (D // 16) ** -0.5, 1.75, ((0, 4),), jnp.float32)
    proj_bias = scatter_about(key_list[9], (D,), 0.3, 3.0, ((0, 4),), jnp.float32)
    mid_gain = jnp.clip(1.0 + 0.18 * jax.random.normal(key_list[10], (D,), jnp.float32), 0.1, 1.9)
    mid_shift = scatter_about(key_list[11], (D,), 0.3, 3.0, ((0, 4),), jnp.float32)
    up_weight = scatter_about(key_list[12], (D, HID), D ** -0.5, 0.4375, ((1, 4),), jnp.float32)
    up_bias = scatter_about(key_list[13], (HID,), 0.5, 3.0, ((0, 4),), jnp.float32)
    down_weight = scatter_about(key_list[14], (HID, D), HID ** -0.5, 0.3125, ((0, 4),), jnp.float32)
    down_bias = scatter_about(key_list[15], (D,), 0.3, 3.0, ((0, 4),), jnp.float32)
    conv_kernel = scatter_about(key_list[16], (3, 3, D, D), (9 * D) ** -0.5, 0.15625, ((3, 4),), jnp.float32)
    conv_bias = scatter_about(key_list[17], (D,), 0.3, 3.0, ((0, 4),), jnp.float32)
    return {"images": images, "item_sizes": item_sizes, "cotangent": cotangent, "pre_gain": pre_gain, "pre_shift": pre_shift, "qkv_weight": qkv_weight, "qv_bias": qv_bias, "rel_table": rel_table, "proj_weight": proj_weight, "proj_bias": proj_bias, "mid_gain": mid_gain, "mid_shift": mid_shift, "up_weight": up_weight, "up_bias": up_bias, "down_weight": down_weight, "down_bias": down_bias, "conv_kernel": conv_kernel, "conv_bias": conv_bias}


HIGHEST = lax.Precision.HIGHEST
EPSILON = 1e-05
NEG_FILL = -1e+30

def matmul(left, right):
    return jnp.dot(left, right, precision=HIGHEST, preferred_element_type=jnp.float32)

def layer_norm(value, gain, offset):
    centre = value - lax.optimization_barrier(jnp.mean(value, axis=-1, keepdims=True))
    spread = lax.optimization_barrier(jnp.mean(centre * centre, axis=-1, keepdims=True))
    return centre * lax.rsqrt(spread + EPSILON) * gain + offset

def to_windows(value):
    batch, height, breadth, chans = value.shape
    value = value.reshape(batch, height // WIN, WIN, breadth // WIN, WIN, chans)
    return value.transpose(0, 1, 3, 2, 4, 5).reshape(-1, WIN * WIN, chans)

def from_windows(value, batch, height, breadth):
    chans = value.shape[-1]
    value = value.reshape(batch, height // WIN, breadth // WIN, WIN, WIN, chans)
    return value.transpose(0, 1, 3, 2, 4, 5).reshape(batch, height, breadth, chans)

def bands(position):
    return (position >= IMG - WIN).astype(jnp.int32) + (position >= IMG - SHIFT).astype(jnp.int32)

def position_table():
    cells = jnp.arange(WIN * WIN, dtype=jnp.int32)
    down = cells // WIN
    across = cells % WIN
    rel_down = down[:, None] - down[None, :] + WIN - 1
    rel_across = across[:, None] - across[None, :] + WIN - 1
    return rel_down * (2 * WIN - 1) + rel_across

def block_forward(image, mask, params):
    pre_gain, pre_shift, qkv_weight, qv_bias, rel_table, proj_weight, proj_bias, mid_gain, mid_shift, up_weight, up_bias, down_weight, down_bias, conv_kernel, conv_bias = params
    mask_full = mask[:, :, None]
    start = mask_full * image
    shifted = jnp.roll(start, (-SHIFT, -SHIFT), axis=(0, 1))
    keep = jnp.roll(mask, (-SHIFT, -SHIFT), axis=(0, 1))
    positions = jnp.arange(IMG, dtype=jnp.int32)
    region = bands(positions)[:, None] * 3 + bands(positions)[None, :]
    region_windows = to_windows(region[None, :, :, None])[:, :, 0]
    keep_windows = to_windows(keep[None, :, :, None])[:, :, 0]
    allowed = (region_windows[:, :, None] == region_windows[:, None, :]) & (keep_windows[:, None, :] > 0.5)
    normed = layer_norm(shifted, pre_gain, pre_shift).reshape(-1, D)
    mixed = matmul(normed, qkv_weight)
    query = mixed[:, :D] + qv_bias[:D]
    keys = mixed[:, D:2 * D]
    values = mixed[:, 2 * D:] + qv_bias[D:]

    def heads_of(part):
        return to_windows(part.reshape(1, IMG, IMG, D)).reshape(-1, WIN * WIN, HEADS, HD)
    table = rel_table[position_table()].transpose(2, 0, 1)
    scores = jnp.einsum('wihd,wjhd->whij', heads_of(query), heads_of(keys), precision=HIGHEST) * HD ** (-0.5) + table
    scores = jnp.where(allowed[:, None], scores, NEG_FILL)
    probs = jax.nn.softmax(scores, axis=-1)
    attended = jnp.einsum('whij,wjhd->wihd', probs, heads_of(values), precision=HIGHEST)
    attended = from_windows(attended.reshape(-1, WIN * WIN, D), 1, IMG, IMG).reshape(-1, D)
    proj = (matmul(attended, proj_weight) + proj_bias).reshape(IMG, IMG, D)
    after_attn = start + mask_full * jnp.roll(proj, (SHIFT, SHIFT), axis=(0, 1))
    normed_mid = layer_norm(after_attn, mid_gain, mid_shift).reshape(-1, D)
    hidden = jax.nn.gelu(matmul(normed_mid, up_weight) + up_bias, approximate=False)
    after_mlp = after_attn + mask_full * (matmul(hidden, down_weight) + down_bias).reshape(IMG, IMG, D)
    padded = jnp.pad(after_mlp, ((1, 1), (1, 1), (0, 0)))
    total = jnp.zeros((IMG * IMG, D), jnp.float32)
    for down in range(3):
        for across in range(3):
            total = total + matmul(padded[down:down + IMG, across:across + IMG].reshape(-1, D), conv_kernel[down, across])
    conv = total.reshape(IMG, IMG, D) + conv_bias
    return start + mask_full * conv

def reference(images, item_sizes, cotangent, pre_gain, pre_shift, qkv_weight, qv_bias, rel_table, proj_weight, proj_bias, mid_gain, mid_shift, up_weight, up_bias, down_weight, down_bias, conv_kernel, conv_bias):
    params = (pre_gain, pre_shift, qkv_weight, qv_bias, rel_table, proj_weight, proj_bias, mid_gain, mid_shift, up_weight, up_bias, down_weight, down_bias, conv_kernel, conv_bias)

    def step(totals, item):
        image, size, cot = item
        positions = jnp.arange(IMG, dtype=jnp.int32)
        inside = positions < size
        mask = (inside[:, None] & inside[None, :]).astype(jnp.float32)

        def forward(image_in, weights):
            return block_forward(image_in, mask, weights)
        out, pull = jax.vjp(forward, image, params)
        d_image, d_params = pull(cot)
        totals = jax.tree.map(jnp.add, totals, d_params)
        return (totals, (out, d_image))
    zeros = jax.tree.map(jnp.zeros_like, params)
    totals, (outs, d_images) = lax.scan(step, zeros, (images, item_sizes, cotangent))
    return (outs, d_images, totals[0], totals[1], totals[2], totals[3], totals[4], totals[5], totals[6], totals[7], totals[8], totals[9], totals[10], totals[11], totals[12], totals[13], totals[14])
```

```python
import functools

import jax
import jax.numpy as jnp
from jax import lax
from jax.experimental import pallas as pl
from jax.experimental.pallas import tpu as pltpu
from jax.sharding import PartitionSpec as P

WIN = 8
IMG = 96
SHIFT = 4
EPSILON = 1e-05
NEG_FILL = -1e30
HEADS = 6
HD = 30
SLOT = 32
LANES = 256
HIGH = lax.Precision.HIGH
HIGHEST = lax.Precision.HIGHEST
F32 = jnp.float32
BF16 = jnp.bfloat16
BLOCK = WIN * IMG
PAIRS = IMG // WIN // 2
VMEM_BYTES = 60 * 2**20


def flip(axis, bit):
    return [(i, i ^ bit) for i in range(lax.axis_size(axis))]


def from_behind(block, axis, distance):
    n = lax.axis_size(axis)
    return lax.ppermute(block, axis, [((i - distance) % n, i) for i in range(n)])


def power_of_two(n):
    return n & (n - 1) == 0


def gather_tp(block):
    n = lax.axis_size("tp")
    if not power_of_two(n):
        return lax.all_gather(block, "tp")
    me = lax.axis_index("tp")
    got = block[None]
    bit = n // 2
    while bit:
        other = lax.ppermute(got, "tp", flip("tp", bit))
        mine_first = (me & bit) == 0
        got = jnp.stack([jnp.where(mine_first, got, other), jnp.where(mine_first, other, got)], 0)
        bit //= 2
    depth = n.bit_length() - 1
    got = got.reshape((2,) * depth + block.shape)
    return got.transpose(tuple(reversed(range(depth))) + tuple(range(depth, got.ndim))).reshape(
        (n,) + block.shape
    )


def scatter_sum_tp(parts):
    n = lax.axis_size("tp")
    if not power_of_two(n):
        return lax.psum_scatter(parts, "tp", scatter_dimension=0, tiled=False)
    me = lax.axis_index("tp")
    depth = n.bit_length() - 1
    rest = parts.shape[1:]
    held = parts
    for level in range(depth):
        bit = 1 << level
        held = held.reshape((-1, 2) + rest)
        upper = (me & bit) != 0
        send = jnp.where(upper, held[:, 0], held[:, 1])
        keep = jnp.where(upper, held[:, 1], held[:, 0])
        held = keep + lax.ppermute(send, "tp", flip("tp", bit))
    return held[0]


def radix_groups(n):
    groups = []
    while n > 1:
        for radix in (8, 4, 2):
            if n % radix == 0:
                groups.append(radix)
                n //= radix
                break
        else:
            groups.append(n)
            n = 1
    return groups


def sum_dp(value):
    n = lax.axis_size("dp")
    if not power_of_two(n):
        return lax.psum(value, "dp")
    me = lax.axis_index("dp")
    rows, lanes = value.shape
    unit = 8 * n
    padded = -(-rows // unit) * unit
    held = jnp.pad(value, ((0, padded - rows), (0, 0)))
    stride = 1
    steps = []
    for radix in radix_groups(n):
        digit = (me // stride) % radix
        chunks = held.reshape(radix, -1, lanes)
        total = lax.dynamic_index_in_dim(chunks, digit, 0, False)
        for k in range(1, radix):
            piece = lax.dynamic_index_in_dim(chunks, digit ^ k, 0, False)
            total = total + lax.ppermute(piece, "dp", flip("dp", k * stride))
        held = total
        steps.append((radix, stride, digit))
        stride *= radix
    for radix, stride, digit in reversed(steps):
        blocks = [held] + [lax.ppermute(held, "dp", flip("dp", k * stride)) for k in range(1, radix)]
        stacked = jnp.stack(blocks, 0)
        ordered = [lax.dynamic_index_in_dim(stacked, digit ^ k, 0, False) for k in range(radix)]
        held = jnp.concatenate(ordered, 0)
    return held[:rows]


def dot(left, right, left_dim, right_dim, precision=None):
    return lax.dot_general(
        left,
        right,
        (((left_dim,), (right_dim,)), ((), ())),
        precision=precision,
        preferred_element_type=F32,
    )


def nn(left, right):
    return dot(left, right, 1, 0, HIGH)


def nt(left, right):
    return dot(left, right, 1, 1, HIGH)


def tn(left, right):
    return dot(left, right, 0, 0, HIGH)


def iota(shape, dim):
    return lax.broadcasted_iota(jnp.int32, shape, dim)


def wrapped(position):
    return jnp.where(position >= IMG, position - IMG, position)


def frame_mask(size, first, shape):
    rows = wrapped(first + iota(shape, 0))
    cols = wrapped(iota(shape, 1) + SHIFT)
    return ((rows < size) & (cols < size)).astype(F32)


def normalize(value):
    centre = value - jnp.mean(value, axis=-1, keepdims=True)
    scale = lax.rsqrt(jnp.mean(centre * centre, axis=-1, keepdims=True) + EPSILON)
    return centre * scale, scale


def normalize_back(grad, unit, scale):
    return scale * (
        grad
        - jnp.mean(grad, axis=-1, keepdims=True)
        - unit * jnp.mean(grad * unit, axis=-1, keepdims=True)
    )


def upper(value):
    return value.astype(BF16).astype(F32)


def parted(value):
    high = upper(value)
    return jnp.where(iota(value.shape, 1) < 64, high, value - high)


def doubled(first, second):
    left = iota(first.shape, 1) < 64
    turned0 = pltpu.roll(first, 64, 1)
    turned1 = pltpu.roll(second, 64, 1)
    return (
        jnp.where(left, first, turned0),
        jnp.where(left, turned0, first),
        jnp.where(left, second, turned1),
    )


def head_products(rows, cols):
    lanes = iota((128, 128), 1)
    even = (lanes & 63) < SLOT
    outs = []
    for moving, fixed in zip(doubled(*rows), doubled(*cols)):
        high = fixed.astype(BF16)
        low = (fixed - high.astype(F32)).astype(BF16)
        held = jnp.concatenate([high, low], 1)
        pieces = parted(moving)
        ones = jnp.where(even, pieces, 0.0).astype(BF16)
        twos = jnp.where(even, 0.0, pieces).astype(BF16)
        both = []
        for w in range(2):
            part = slice(64 * w, 64 * w + 64)
            stream = jnp.concatenate([ones[part], twos[part]], 0)
            both.append(dot(jnp.concatenate([stream, stream], 1), held, 1, 1))
        outs.append(jnp.where(lanes < 64, both[0], both[1]))
    return jnp.concatenate(outs, 0)


def mix(tiles, first, second):
    lanes = iota((64, 128), 1)

    def product(part, block):
        high = block.astype(BF16)
        low = (block - high.astype(F32)).astype(BF16)
        held = jnp.concatenate([high, high, low, low], 0)
        stream = jnp.concatenate(part, 0)
        return dot(jnp.concatenate([stream, stream], 1), held, 1, 0)

    a = product(tiles[:4], first)
    b = product(tiles[4:], second)
    one = jnp.where(
        lanes < 64,
        jnp.where(lanes < 32, a[0:64], a[64:128]),
        jnp.where(lanes < 96, a[128:192], a[192:256]),
    )
    two = jnp.where(lanes < 32, b[0:64], b[64:128])
    return one, two


def straight_tiles(table):
    left = iota(table.shape, 1) < 64
    turned = pltpu.roll(table, 64, 1)
    outs = []
    for w in range(2):
        one = jnp.where(left, table, turned) if w == 0 else jnp.where(left, turned, table)
        both = parted(one).astype(BF16)
        outs.append([both[64 * h : 64 * h + 64] for h in range(HEADS)])
    return outs


def turned_tiles(table):
    high = upper(table)
    low = table - high
    outs = [[], []]
    for h in range(HEADS):
        part = slice(64 * h, 64 * h + 64)
        both = jnp.concatenate([high[part], low[part]], 0).astype(BF16).T
        for w in range(2):
            outs[w].append(both[64 * w : 64 * w + 64])
    return outs


def window_pair(ref, pair, start):
    cols = pl.ds(pl.multiple_of(pair * 2 * WIN, 2 * WIN), 2 * WIN)
    tiles = []
    for tile in range(2):
        block = ref[:, cols, start + 128 * tile : start + 128 * tile + 128]
        tiles.append(
            jnp.concatenate(
                [block[:, :WIN].reshape(64, 128), block[:, WIN:].reshape(64, 128)], 0
            )
        )
    return tiles


def put_window(ref, pair, w, start, tiles):
    cols = pl.ds(pl.multiple_of(pair * 2 * WIN + w * WIN, WIN), WIN)
    for tile in range(2):
        ref[:, cols, start + 128 * tile : start + 128 * tile + 128] = tiles[tile].reshape(
            WIN, WIN, 128
        )


def pair_fill(size, first, pair):
    shape = (64, 128)
    j, lane = iota(shape, 0), iota(shape, 1)
    i, window = lane & 63, 2 * pair + (lane >> 6)
    rows = wrapped(first + (j >> 3))
    cols = wrapped(window * WIN + (j & 7) + SHIFT)
    apart_rows = (first == IMG - WIN + SHIFT) & ((j >> 5) != (i >> 5))
    apart_cols = (window == IMG // WIN - 1) & (((j & 7) >> 2) != ((i & 7) >> 2))
    keep = (rows < size) & (cols < size)
    return jnp.where(apart_rows | apart_cols | jnp.logical_not(keep), NEG_FILL, 0.0)


def block_first(scal, k):
    return wrapped(scal[1] + WIN * k)


def attend_kernel(
    scal, x, gain, offset, weight, bias, table, proj, proj_bias, mixed, probs, attended, after
):
    chans = x.shape[-1]
    size, first = scal[0], block_first(scal, pl.program_id(0))
    mask = frame_mask(size, first, x.shape)
    start = mask * x[...]
    unit, _ = normalize(start)
    normed = unit * gain[...] + offset[...]
    mixed[...] = (nt(normed.reshape(BLOCK, chans), weight[...]) + bias[...]).reshape(mixed.shape)

    def step(pair, carry):
        query = window_pair(mixed, pair, 0)
        keys = window_pair(mixed, pair, LANES)
        values = window_pair(mixed, pair, 2 * LANES)
        scores = head_products(keys, [q * HD**-0.5 for q in query]) + table[...]
        scores = scores.reshape(HEADS, 64, 128) + pair_fill(size, first, pair)[None]
        scores = jnp.exp(scores - jnp.max(scores, 1, keepdims=True))
        prob = (scores * (1.0 / jnp.sum(scores, 1, keepdims=True))).reshape(HEADS * 64, 128)
        probs[0, pair] = prob
        for w, tiles in enumerate(turned_tiles(prob)):
            part = slice(64 * w, 64 * w + 64)
            put_window(attended, pair, w, 0, mix(tiles, values[0][part], values[1][part]))
        return carry

    lax.fori_loop(0, PAIRS, step, 0)
    out = nn(attended[...].reshape(BLOCK, LANES), proj[...]) + proj_bias[...]
    after[...] = start + mask * out.reshape(x.shape)


def feed_kernel(scal, value, gain, offset, up, up_bias, down, down_bias, pre, after):
    chans = value.shape[-1]
    size, first = scal[0], block_first(scal, pl.program_id(0))
    mask = frame_mask(size, first, value.shape)
    unit, _ = normalize(value[...])
    normed = unit * gain[...] + offset[...]
    hidden = nt(normed.reshape(BLOCK, chans), up[...]) + up_bias[...]
    pre[...] = hidden.reshape(pre.shape)
    act = hidden * (0.5 * (1.0 + lax.erf(hidden * 0.5**0.5)))
    out = nn(act, down[...]) + down_bias[...]
    after[...] = value[...] + mask * out.reshape(value.shape)


def conv_kernel_body(
    scal, after, cot, images, weight, bias, out, d_mid, grad, grad_bias, spread, d_spread, wide, tall
):
    chans = after.shape[-1]
    height = images.shape[0]
    k = pl.program_id(0)
    size, base = scal[0], scal[1]

    @pl.when(k == 0)
    def _():
        wide[...] = jnp.zeros_like(wide)
        tall[...] = jnp.zeros_like(tall)
        for i in range(3):
            for j in range(3):
                wide[i, :, LANES * j : LANES * j + chans] = weight[3 * i + j]
                tall[i, LANES * j : LANES * j + chans, :] = weight[3 * i + 2 - j]
        spread[...] = jnp.zeros_like(spread)
        d_spread[...] = jnp.zeros_like(d_spread)
        shape = (1, IMG, chans)
        cols = iota(shape, 1)

        def fill(ref, row, value):
            ref[pl.ds(row, 1), :, LANES : LANES + chans] = value
            ref[pl.ds(row, 1), :, :chans] = jnp.where(cols == 0, 0.0, pltpu.roll(value, 1, 1))
            ref[pl.ds(row, 1), :, 2 * LANES : 2 * LANES + chans] = jnp.where(
                cols == IMG - 1, 0.0, pltpu.roll(value, IMG - 1, 1)
            )

        def one(row, carry):
            inside = (base + SHIFT - 1 + row == IMG - 1) & (row == 0)
            outside = (wrapped(wrapped(base + SHIFT - 1 + row)) == 0) & (row == height + 1)
            value = pltpu.roll(after[pl.ds(row + SHIFT - 1, 1)], SHIFT, 1)
            fill(spread, row, jnp.where(inside | outside, 0.0, value))
            return carry

        lax.fori_loop(0, height + 2, one, 0)

        def two(row, carry):
            where = wrapped(wrapped(base + IMG - 1 + row))
            mask = ((where < size) & (cols < size)).astype(F32)
            fill(d_spread, row, mask * cot[pl.ds(row, 1)])
            return carry

        lax.fori_loop(0, height + 2 * SHIFT + 2, two, 0)
        grad[...] = jnp.zeros_like(grad)
        grad_bias[...] = jnp.zeros_like(grad_bias)

    shape = (WIN, IMG, chans)
    first = wrapped(base + WIN * k)
    rows = wrapped(first + iota(shape, 0))
    total = jnp.zeros(shape, F32)
    for i in range(3):
        block = d_spread[pl.ds(WIN * k + 2 - i, WIN)].reshape(BLOCK, 3 * LANES)
        part = nn(block, tall[i]).reshape(shape)
        if i == 0:
            part = jnp.where(rows == IMG - 1, 0.0, part)
        if i == 2:
            part = jnp.where(rows == 0, 0.0, part)
        total = total + part
    d_mid[...] = pltpu.roll(total, IMG - SHIFT, 1)

    @pl.when(k < height // WIN)
    def _():
        own = pl.ds(WIN * k, WIN)
        total = jnp.zeros((BLOCK, chans), F32)
        d_conv = d_spread[pl.ds(WIN * k + SHIFT + 1, WIN), :, LANES : LANES + chans].reshape(
            BLOCK, chans
        )
        turned = d_conv.T
        for i in range(3):
            block = spread[pl.ds(WIN * k + i, WIN)].reshape(BLOCK, 3 * LANES)
            total = total + nt(block, wide[i])
            grad[i] += nn(turned, block)
        where = wrapped(first + SHIFT + iota(shape, 0))
        mask = ((where < size) & (iota(shape, 1) < size)).astype(F32)
        conv = (total + bias[...]).reshape(shape)
        out[own] = mask * (images[own] + conv)
        grad_bias[...] += jnp.sum(d_conv, 0, keepdims=True)


def feed_back_kernel(
    scal, d_mid, value, pre, gain, offset, up, down, d_attn, g_up, g_down, g_up_bias, g_vec
):
    chans = value.shape[-1]
    k = pl.program_id(0)
    steps = pl.num_programs(0)

    @pl.when(k == 0)
    def _():
        g_up[...] = jnp.zeros_like(g_up)
        g_down[...] = jnp.zeros_like(g_down)
        g_up_bias[...] = jnp.zeros_like(g_up_bias)
        g_vec[...] = jnp.zeros_like(g_vec)

    size, first = scal[0], block_first(scal, k)
    mask = frame_mask(size, first, value.shape)
    row = iota((WIN, IMG, 1), 0) + WIN * k
    own3 = ((row >= SHIFT) & (row < steps * WIN - SHIFT)).astype(F32)
    own = own3.reshape(BLOCK, 1)
    mid = d_mid[...]
    d_ff = (mask * mid).reshape(BLOCK, chans)
    hidden = pre[...].reshape(BLOCK, pre.shape[-1])
    phi = 0.5 * (1.0 + lax.erf(hidden * 0.5**0.5))
    act = hidden * phi
    slope = phi + hidden * (jnp.exp(-0.5 * hidden * hidden) * 0.3989422804014327)
    d_pre = nt(d_ff, down[...]) * slope
    d_normed = nn(d_pre, up[...])
    unit3, scale = normalize(value[...])
    unit = unit3.reshape(BLOCK, chans)
    normed = unit * gain[...] + offset[...]
    grad = (d_normed * gain[...]).reshape(value.shape)
    d_attn[...] = mid + normalize_back(grad, unit3, scale)
    d_ff_own = own * d_ff
    d_pre_own = own * d_pre
    d_normed_own = own * d_normed
    g_down[...] += nn(d_ff_own.T, act)
    g_up[...] += nn(normed.T, d_pre_own)
    g_up_bias[...] += jnp.sum(d_pre_own, 0, keepdims=True)
    g_vec[0:1] += jnp.sum(d_normed_own * unit, 0, keepdims=True)
    g_vec[1:2] += jnp.sum(d_normed_own, 0, keepdims=True)
    g_vec[2:3] += jnp.sum(d_ff_own, 0, keepdims=True)


def attend_back_kernel(
    scal,
    x,
    mixed,
    probs,
    attended,
    d_attn,
    cot,
    gain,
    offset,
    weight,
    proj,
    out,
    g_qkv,
    g_proj,
    g_table,
    g_mixed,
    g_vec,
    d_att,
    d_mixed,
):
    chans = x.shape[-1]
    k = pl.program_id(0)
    height = out.shape[0]

    @pl.when(k == 0)
    def _():
        for ref in (g_qkv, g_proj, g_table, g_mixed, g_vec):
            ref[...] = jnp.zeros_like(ref)

    size, first = scal[0], block_first(scal, k)
    mask = frame_mask(size, first, x.shape)
    d_out = d_attn[...]
    d_proj = (mask * d_out).reshape(BLOCK, chans)
    d_att[...] = nt(d_proj, proj[...]).reshape(d_att.shape)
    counted = (k > 0).astype(F32)

    def step(pair, carry):
        query = [q * HD**-0.5 for q in window_pair(mixed, pair, 0)]
        keys = window_pair(mixed, pair, LANES)
        values = window_pair(mixed, pair, 2 * LANES)
        d_rows = window_pair(d_att, pair, 0)
        prob = probs[0, pair]
        d_prob = head_products(values, d_rows).reshape(HEADS, 64, 128)
        prob3 = prob.reshape(HEADS, 64, 128)
        d_score = prob3 * (d_prob - jnp.sum(prob3 * d_prob, 1, keepdims=True))
        d_score = d_score.reshape(HEADS * 64, 128)
        g_table[...] += counted * d_score
        prob_tiles = straight_tiles(prob)
        score_tiles = straight_tiles(d_score)
        turned = turned_tiles(d_score)
        for w in range(2):
            part = slice(64 * w, 64 * w + 64)
            d_query = mix(turned[w], keys[0][part], keys[1][part])
            put_window(d_mixed, pair, w, 0, [d * HD**-0.5 for d in d_query])
            put_window(
                d_mixed, pair, w, LANES, mix(score_tiles[w], query[0][part], query[1][part])
            )
            put_window(
                d_mixed, pair, w, 2 * LANES, mix(prob_tiles[w], d_rows[0][part], d_rows[1][part])
            )
        return carry

    lax.fori_loop(0, PAIRS, step, 0)
    start = mask * x[...]
    unit3, scale = normalize(start)
    unit = unit3.reshape(BLOCK, chans)
    d_all = d_mixed[...].reshape(BLOCK, 3 * LANES)
    d_normed = nn(d_all, weight[...])
    grad = (d_normed * gain[...]).reshape(x.shape)
    d_image = mask * (d_out + normalize_back(grad, unit3, scale))
    d_image = pltpu.roll(d_image, SHIFT, 1)

    shape = x.shape
    rows = wrapped(first + iota(shape, 0))
    plain = ((rows < size) & (iota(shape, 1) < size)).astype(F32)

    @pl.when(k == 0)
    def _():
        half = slice(SHIFT, WIN)
        out[:SHIFT] = d_image[half] + plain[half] * cot[:SHIFT]

    @pl.when((k > 0) & (k < pl.num_programs(0) - 1))
    def _():
        own = pl.ds(WIN * k - SHIFT, WIN)
        out[own] = d_image + plain * cot[own]

    @pl.when(k == pl.num_programs(0) - 1)
    def _():
        half = slice(0, SHIFT)
        out[height - SHIFT :] = d_image[half] + plain[half] * cot[height - SHIFT :]

    @pl.when(k > 0)
    def _():
        normed = unit * gain[...] + offset[...]
        g_qkv[...] += nn(normed.T, d_all)
        g_proj[...] += nn(d_proj.T, attended[...].reshape(BLOCK, LANES))
        g_mixed[...] += jnp.sum(d_all, 0, keepdims=True)
        g_vec[0:1] += jnp.sum(d_normed * unit, 0, keepdims=True)
        g_vec[1:2] += jnp.sum(d_normed, 0, keepdims=True)
        g_vec[2:3] += jnp.sum(d_proj, 0, keepdims=True)


def whole(shape):
    return pl.BlockSpec(shape, lambda k, s: (0,) * len(shape))


def rows_of(shape):
    return pl.BlockSpec((WIN,) + tuple(shape[1:]), lambda k, s: (k,) + (0,) * (len(shape) - 1))


def one_of(shape):
    return pl.BlockSpec((1,) + tuple(shape[1:]), lambda k, s: (k,) + (0,) * (len(shape) - 1))


def call(kernel, steps, ins, outs, scratch=(), flops=0):
    scal, rest = ins[0], ins[1:]
    size = sum(4 * a.size for a, _ in rest) + sum(4 * functools.reduce(lambda p, q: p * q, s) for s, _ in outs)
    return pl.pallas_call(
        kernel,
        grid_spec=pltpu.PrefetchScalarGridSpec(
            num_scalar_prefetch=1,
            grid=(steps,),
            in_specs=[make(a.shape) for a, make in rest],
            out_specs=[make(s) for s, make in outs],
            scratch_shapes=list(scratch),
        ),
        out_shape=[jax.ShapeDtypeStruct(s, F32) for s, _ in outs],
        compiler_params=pltpu.CompilerParams(
            dimension_semantics=("arbitrary",), vmem_limit_bytes=VMEM_BYTES
        ),
        cost_estimate=pl.CostEstimate(flops=flops, bytes_accessed=size, transcendentals=0),
    )(scal, *[a for a, _ in rest])


def position_onehot(heads_table):
    cells = jnp.arange(WIN * WIN, dtype=jnp.int32)
    j, i = cells[:, None], cells[None, :]
    down = i // WIN - j // WIN + WIN - 1
    across = i % WIN - j % WIN + WIN - 1
    index = (down * (2 * WIN - 1) + across).reshape(-1)
    return (index[:, None] == jnp.arange(heads_table, dtype=jnp.int32)[None, :]).astype(F32)


def spread_heads(value):
    lead, n = value.shape[:-2], value.shape[-1]
    value = value.reshape(lead + (HEADS, HD, n))
    none = [(0, 0)] * len(lead)
    value = jnp.pad(value, none + [(0, 0), (0, SLOT - HD), (0, 0)])
    value = value.reshape(lead + (HEADS * SLOT, n))
    return jnp.pad(value, none + [(0, LANES - HEADS * SLOT), (0, 0)])


def close_heads(value):
    lead, n = value.shape[:-2], value.shape[-1]
    value = value[..., : HEADS * SLOT, :].reshape(lead + (HEADS, SLOT, n))
    return value[..., :HD, :].reshape(lead + (HEADS * HD, n))


def body(
    images,
    item_sizes,
    cotangent,
    pre_gain,
    pre_shift,
    qkv_weight,
    qv_bias,
    rel_table,
    proj_weight,
    proj_bias,
    mid_gain,
    mid_shift,
    up_weight,
    up_bias,
    down_weight,
    down_bias,
    conv_kernel,
    conv_bias,
):
    batch, height, breadth, chans = images.shape
    parts = lax.axis_size("tp")
    hid = up_weight.shape[1] * parts
    me = lax.axis_index("tp")
    strip = height + 2 * SHIFT
    steps = strip // WIN
    image, cot = images[0], cotangent[0]

    vectors = [pre_gain, pre_shift, qv_bias, proj_bias, mid_gain, mid_shift, up_bias, down_bias, conv_bias]
    lengths = [v.shape[0] for v in vectors]
    flat = jnp.concatenate(vectors)
    vec_rows = -(-flat.shape[0] // chans)
    flat = jnp.pad(flat, (0, vec_rows * chans - flat.shape[0])).reshape(vec_rows, chans)
    mine1 = jnp.concatenate([qkv_weight.T, proj_weight, flat], 0)
    conv_rows = conv_kernel.reshape(9, chans, -1).transpose(0, 2, 1)
    share = conv_rows.shape[1]
    mine2 = jnp.concatenate([up_weight.T, down_weight], 0)
    all1 = gather_tp(mine1)
    x_above = from_behind(image[-SHIFT:], "tp", 1)
    x_below = from_behind(image[:SHIFT], "tp", -1)
    all2 = gather_tp(mine2)
    all3 = gather_tp(conv_rows)
    c_above = from_behind(cot[-SHIFT - 1 :], "tp", 1)
    c_below = from_behind(cot[: SHIFT + 1], "tp", -1)

    nq = qkv_weight.shape[1]
    full_qkv = spread_heads(all1[:, :nq].reshape(3, chans, chans)).reshape(3 * LANES, chans)
    full_proj = spread_heads(all1[:, nq : nq + chans // parts].reshape(chans, chans))
    flat = all1[:, nq + chans // parts :].reshape(parts, -1)
    full_vectors = []
    at = 0
    for n in lengths:
        full_vectors.append(flat[:, at : at + n].reshape(1, n * parts))
        at += n
    v_pre_gain, v_pre_shift, v_qv, v_proj_bias, v_mid_gain, v_mid_shift, v_up_bias, v_down_bias, v_conv_bias = full_vectors
    zeros = jnp.zeros((1, chans), F32)
    qkv_bias = jnp.concatenate([v_qv[:, :chans], zeros, v_qv[:, chans:]], 0)
    qkv_bias = spread_heads(qkv_bias[:, :, None]).reshape(1, 3 * LANES)
    nu = up_weight.shape[1]
    full_up = all2[:, :nu].reshape(hid, chans)
    full_down = all2[:, nu:].reshape(hid, chans)
    full_conv = all3.transpose(1, 0, 2, 3).reshape(9, chans, chans)

    x = jnp.roll(jnp.concatenate([x_above, image, x_below], 0), -SHIFT, 1)
    cot_wide = jnp.concatenate([c_above, cot, c_below], 0)
    scal = jnp.stack([item_sizes[0], (me * height + IMG - SHIFT) % IMG]).astype(jnp.int32)

    onehot = position_onehot(rel_table.shape[0])
    table = jnp.dot(rel_table.T, onehot.T, precision=HIGHEST).reshape(HEADS * 64, 64)
    table = jnp.concatenate([table, table], 1)

    def frame(lanes):
        return (strip, breadth, lanes)

    mixed, probs, attended, after_attn = call(
        attend_kernel,
        steps,
        [scal, (x, rows_of), (v_pre_gain, whole), (v_pre_shift, whole), (full_qkv, whole), (qkv_bias, whole), (table, whole), (full_proj, whole), (v_proj_bias, whole)],
        [(frame(3 * LANES), rows_of), ((steps, PAIRS, HEADS * 64, 128), one_of), (frame(LANES), rows_of), (frame(chans), rows_of)],
        flops=10**10,
    )
    pre, after_mlp = call(
        feed_kernel,
        steps,
        [scal, (after_attn, rows_of), (v_mid_gain, whole), (v_mid_shift, whole), (full_up, whole), (v_up_bias, whole), (full_down, whole), (v_down_bias, whole)],
        [(frame(hid), rows_of), (frame(chans), rows_of)],
        flops=5 * 10**9,
    )
    block_out, d_mid, g_conv, g_conv_bias = call(
        conv_kernel_body,
        steps,
        [scal, (after_mlp, whole), (cot_wide, whole), (image, whole), (full_conv, whole), (v_conv_bias, whole)],
        [(image.shape, whole), (frame(chans), rows_of), ((3, chans, 3 * LANES), whole), ((1, chans), whole)],
        [
            pltpu.VMEM((height + 2, breadth, 3 * LANES), F32),
            pltpu.VMEM((strip + 2, breadth, 3 * LANES), F32),
            pltpu.VMEM((3, chans, 3 * LANES), F32),
            pltpu.VMEM((3, 3 * LANES, chans), F32),
        ],
        flops=3 * 10**10,
    )
    d_attn, g_up, g_down, g_up_bias, g_vec2 = call(
        feed_back_kernel,
        steps,
        [scal, (d_mid, rows_of), (after_attn, rows_of), (pre, rows_of), (v_mid_gain, whole), (v_mid_shift, whole), (full_up, whole), (full_down, whole)],
        [(frame(chans), rows_of), ((chans, hid), whole), ((chans, hid), whole), ((1, hid), whole), ((8, chans), whole)],
        flops=10**10,
    )
    grad_images, g_qkv, g_proj, g_table, g_mixed, g_vec1 = call(
        attend_back_kernel,
        steps,
        [scal, (x, rows_of), (mixed, rows_of), (probs, one_of), (attended, rows_of), (d_attn, rows_of), (cot, whole), (v_pre_gain, whole), (v_pre_shift, whole), (full_qkv, whole), (full_proj, whole)],
        [(image.shape, whole), ((chans, 3 * LANES), whole), ((chans, LANES), whole), ((HEADS * 64, 128), whole), ((1, 3 * LANES), whole), ((8, chans), whole)],
        [pltpu.VMEM((WIN, breadth, LANES), F32), pltpu.VMEM((WIN, breadth, 3 * LANES), F32)],
        flops=2 * 10**10,
    )

    conv_parts = g_conv.reshape(3, parts, share, 3, LANES)[..., :chans]
    conv_parts = conv_parts.transpose(1, 0, 3, 2, 4).reshape(parts, 9 * share, chans)
    sum_conv = sum_dp(scatter_sum_tp(conv_parts))
    feed_parts = jnp.concatenate(
        [g_up.T.reshape(parts, nu, chans), g_down.T.reshape(parts, nu, chans)], 1
    )
    sum_feed = sum_dp(scatter_sum_tp(feed_parts))
    qkv_parts = close_heads(g_qkv.T.reshape(3, LANES, chans)).reshape(parts, nq, chans)
    proj_parts = close_heads(g_proj.T).reshape(parts, chans // parts, chans)
    folded = (g_table[:, :64] + g_table[:, 64:]).reshape(HEADS, 64 * 64)
    table_grad = jnp.dot(folded, onehot, precision=HIGHEST).reshape(-1)
    mixed_bias = close_heads(g_mixed.reshape(3, LANES, 1))[:, :, 0]
    vec_grads = [
        g_vec1[0],
        g_vec1[1],
        jnp.concatenate([mixed_bias[0], mixed_bias[2]]),
        g_vec1[2],
        g_vec2[0],
        g_vec2[1],
        g_up_bias[0],
        g_vec2[2],
        g_conv_bias[0],
    ]
    flat = jnp.concatenate([v.reshape(parts, -1) for v in vec_grads], 1)
    flat = jnp.concatenate([flat, jnp.broadcast_to(table_grad[None], (parts, table_grad.shape[0]))], 1)
    rows = -(-flat.shape[1] // chans)
    flat = jnp.pad(flat, ((0, 0), (0, rows * chans - flat.shape[1]))).reshape(parts, rows, chans)
    last = sum_dp(scatter_sum_tp(jnp.concatenate([qkv_parts, proj_parts, flat], 1)))

    grad_conv_kernel = sum_conv.reshape(3, 3, share, chans).transpose(0, 1, 3, 2)
    grad_up = sum_feed[:nu].T
    grad_down = sum_feed[nu:]
    grad_qkv = last[:nq].T
    grad_proj = last[nq : nq + chans // parts]
    flat = last[nq + chans // parts :].reshape(-1)
    outs = []
    at = 0
    for n in lengths:
        outs.append(flat[at : at + n])
        at += n
    grad_rel = flat[at : at + table_grad.shape[0]].reshape(HEADS, -1).T
    return (
        block_out[None],
        grad_images[None],
        outs[0],
        outs[1],
        grad_qkv,
        outs[2],
        grad_rel,
        grad_proj,
        outs[3],
        outs[4],
        outs[5],
        grad_up,
        outs[6],
        grad_down,
        outs[7],
        grad_conv_kernel,
        outs[8],
    )


def solution(mesh):
    placed = (
        P("dp", "tp", None, None),
        P("dp"),
        P("dp", "tp", None, None),
        P("tp"),
        P("tp"),
        P(None, "tp"),
        P("tp"),
        P(),
        P("tp", None),
        P("tp"),
        P("tp"),
        P("tp"),
        P(None, "tp"),
        P("tp"),
        P("tp", None),
        P("tp"),
        P(None, None, None, "tp"),
        P("tp"),
    )
    return jax.shard_map(
        body,
        mesh=mesh,
        in_specs=placed,
        out_specs=(
            P("dp", "tp", None, None),
            P("dp", "tp", None, None),
            P("tp"),
            P("tp"),
            P(None, "tp"),
            P("tp"),
            P(),
            P("tp", None),
            P("tp"),
            P("tp"),
            P("tp"),
            P(None, "tp"),
            P("tp"),
            P("tp", None),
            P("tp"),
            P(None, None, None, "tp"),
            P("tp"),
        ),
        check_vma=False,
    )
```

```python
import functools

import jax
import jax.numpy as jnp
from jax import lax
from jax.experimental import pallas as pl
from jax.experimental.pallas import tpu as pltpu
from jax.sharding import PartitionSpec as P

WIN = 8
IMG = 96
SHIFT = 4
EPSILON = 1e-05
NEG_FILL = -1e30
CHANS = 180
HEADS = 6
HD = 30
HALF = 15
SLOT = 32
LANES = 256
INNER = 192
HID = 384
RPOS = 225
HIGH = lax.Precision.HIGH
HIGHEST = lax.Precision.HIGHEST
F32 = jnp.float32
BF16 = jnp.bfloat16
BLOCK = WIN * IMG
PAIRS = IMG // WIN // 2
PARTS = 4
VMEM_BYTES = 60 * 2**20

QKV_ROWS, PROJ_ROWS, VEC_ROWS = 144, 48, 16
FEED_ROWS = 96
CONV_ROWS = 48
REST_ROWS = 272
PRE_GAIN, PRE_SHIFT, PROJ_BIAS, MID_GAIN, MID_SHIFT, DOWN_BIAS, CONV_BIAS, QV_BIAS, UP_BIAS = range(9)


def flip(axis, bit):
    return [(i, i ^ bit) for i in range(lax.axis_size(axis))]


def from_behind(block, axis, distance):
    n = lax.axis_size(axis)
    return lax.ppermute(block, axis, [((i - distance) % n, i) for i in range(n)])


def gather_tp(block):
    got = {0: block}
    for bit in (2, 1):
        got.update({k | bit: lax.ppermute(b, "tp", flip("tp", bit)) for k, b in list(got.items())})
    return [got[k] for k in range(PARTS)]


def tp_stage(parts, level):
    bit = 1 << level
    parts = parts.reshape((-1, 2) + parts.shape[1:])
    odd = (lax.axis_index("tp") & bit) != 0
    send = jnp.where(odd, parts[:, 0], parts[:, 1])
    got = lax.ppermute(send, "tp", flip("tp", bit))
    return jnp.where(odd, parts[:, 1], parts[:, 0]) + got


def dp_bits():
    n = lax.axis_size("dp")
    return [1 << b for b in range(n.bit_length() - 1)]


def dp_halve(held, bit):
    half = held.shape[0] // 2
    odd = (lax.axis_index("dp") & bit) != 0
    send = jnp.where(odd, held[:half], held[half:])
    got = lax.ppermute(send, "dp", flip("dp", bit))
    return jnp.where(odd, held[half:], held[:half]) + got


def dp_join(held, bit):
    odd = (lax.axis_index("dp") & bit) != 0
    got = lax.ppermute(held, "dp", flip("dp", bit))
    return jnp.concatenate([jnp.where(odd, got, held), jnp.where(odd, held, got)], 0)


def dp_add(held, bit):
    return held + lax.ppermute(held, "dp", flip("dp", bit))


def dot(left, right, left_dim, right_dim, precision=None):
    return lax.dot_general(
        left,
        right,
        (((left_dim,), (right_dim,)), ((), ())),
        precision=precision,
        preferred_element_type=F32,
    )


def nn(left, right):
    return dot(left, right, 1, 0, HIGH)


def nt(left, right):
    return dot(left, right, 1, 1, HIGH)


def turn(value):
    return value.T[:184]


def iota(shape, dim):
    return lax.broadcasted_iota(jnp.int32, shape, dim)


def wrapped(position):
    return jnp.where(position >= IMG, position - IMG, position)


def frame_mask(size, first, rows=WIN):
    shape = (rows, IMG, LANES)
    row = wrapped(first + iota(shape, 0))
    col = wrapped(iota(shape, 1) + SHIFT)
    return ((row < size) & (col < size) & (iota(shape, 2) < CHANS)).astype(F32)


def plain_mask(size, first, rows):
    shape = (rows, IMG, LANES)
    row = wrapped(first + iota(shape, 0))
    return ((row < size) & (iota(shape, 1) < size) & (iota(shape, 2) < CHANS)).astype(F32)


def is_channel(shape):
    return iota(shape, len(shape) - 1) < CHANS


def mean(value):
    return jnp.sum(value, axis=-1, keepdims=True) * (1.0 / CHANS)


def normalize(value):
    centre = jnp.where(is_channel(value.shape), value - mean(value), 0.0)
    scale = lax.rsqrt(mean(centre * centre) + EPSILON)
    return centre * scale, scale


def normalize_back(grad, unit, scale):
    value = scale * (grad - mean(grad) - unit * mean(grad * unit))
    return jnp.where(is_channel(value.shape), value, 0.0)


def upper(value):
    return value.astype(BF16).astype(F32)


def parted(value):
    high = upper(value)
    return jnp.where(iota(value.shape, 1) < 64, high, value - high)


def doubled(first, second):
    left = iota(first.shape, 1) < 64
    turned0 = pltpu.roll(first, 64, 1)
    turned1 = pltpu.roll(second, 64, 1)
    return (
        jnp.where(left, first, turned0),
        jnp.where(left, turned0, first),
        jnp.where(left, second, turned1),
    )


def head_products(rows, cols):
    lanes = iota((128, 128), 1)
    even = (lanes & 63) < SLOT
    outs = []
    for moving, fixed in zip(doubled(*rows), doubled(*cols)):
        high = fixed.astype(BF16)
        low = (fixed - high.astype(F32)).astype(BF16)
        held = jnp.concatenate([high, low], 1)
        pieces = parted(moving)
        ones = jnp.where(even, pieces, 0.0).astype(BF16)
        twos = jnp.where(even, 0.0, pieces).astype(BF16)
        both = []
        for w in range(2):
            part = slice(64 * w, 64 * w + 64)
            stream = jnp.concatenate([ones[part], twos[part]], 0)
            both.append(dot(jnp.concatenate([stream, stream], 1), held, 1, 1))
        outs.append(jnp.where(lanes < 64, both[0], both[1]))
    return jnp.concatenate(outs, 0)


def mix(tiles, first, second):
    lanes = iota((64, 128), 1)

    def product(part, block):
        high = block.astype(BF16)
        low = (block - high.astype(F32)).astype(BF16)
        held = jnp.concatenate([high, high, low, low], 0)
        stream = jnp.concatenate(part, 0)
        return dot(jnp.concatenate([stream, stream], 1), held, 1, 0)

    a = product(tiles[:4], first)
    b = product(tiles[4:], second)
    one = jnp.where(
        lanes < 64,
        jnp.where(lanes < 32, a[0:64], a[64:128]),
        jnp.where(lanes < 96, a[128:192], a[192:256]),
    )
    two = jnp.where(lanes < 32, b[0:64], b[64:128])
    return one, two


def straight_tiles(table):
    left = iota(table.shape, 1) < 64
    turned = pltpu.roll(table, 64, 1)
    outs = []
    for w in range(2):
        one = jnp.where(left, table, turned) if w == 0 else jnp.where(left, turned, table)
        both = parted(one).astype(BF16)
        outs.append([both[64 * h : 64 * h + 64] for h in range(HEADS)])
    return outs


def turned_tiles(table):
    high = upper(table)
    low = table - high
    outs = [[], []]
    for h in range(HEADS):
        part = slice(64 * h, 64 * h + 64)
        both = jnp.concatenate([high[part], low[part]], 0).astype(BF16).T
        for w in range(2):
            outs[w].append(both[64 * w : 64 * w + 64])
    return outs


def window_pair(ref, pair, start):
    cols = pl.ds(pl.multiple_of(pair * 2 * WIN, 2 * WIN), 2 * WIN)
    tiles = []
    for tile in range(2):
        block = ref[:, cols, start + 128 * tile : start + 128 * tile + 128]
        tiles.append(
            jnp.concatenate(
                [block[:, :WIN].reshape(64, 128), block[:, WIN:].reshape(64, 128)], 0
            )
        )
    return tiles


def put_window(ref, pair, w, start, tiles):
    cols = pl.ds(pl.multiple_of(pair * 2 * WIN + w * WIN, WIN), WIN)
    for tile in range(2):
        ref[:, cols, start + 128 * tile : start + 128 * tile + 128] = tiles[tile].reshape(
            WIN, WIN, 128
        )


def pair_fill(size, first, pair):
    shape = (64, 128)
    j, lane = iota(shape, 0), iota(shape, 1)
    i, window = lane & 63, 2 * pair + (lane >> 6)
    rows = wrapped(first + (j >> 3))
    cols = wrapped(window * WIN + (j & 7) + SHIFT)
    apart_rows = (first == IMG - WIN + SHIFT) & ((j >> 5) != (i >> 5))
    apart_cols = (window == IMG // WIN - 1) & (((j & 7) >> 2) != ((i & 7) >> 2))
    keep = (rows < size) & (cols < size)
    return jnp.where(apart_rows | apart_cols | jnp.logical_not(keep), NEG_FILL, 0.0)


def block_first(scal, k):
    return wrapped(scal[1] + WIN * k)


def gelu_parts(hidden):
    return 0.5 * (1.0 + lax.erf(hidden * 0.5**0.5))


def prepare_kernel(scal, p0, p1, p2, p3, rel, qkv, proj, vec, table, spread):
    me = scal[2]
    for ref in (qkv, proj, vec, spread):
        ref[...] = jnp.zeros_like(ref)
    lanes = iota((VEC_ROWS, 3 * LANES), 1)
    row = iota((VEC_ROWS, 3 * LANES), 0)
    for k, piece in enumerate((p0, p1, p2, p3)):
        owner = me ^ k
        for m in range(3):
            at = owner * 3 + m
            start = pl.multiple_of((at // 4) * LANES + (at % 4) * 48, 16)
            qkv[pl.ds(start, 48), :CHANS] = piece[48 * m : 48 * m + 48]
        proj[pl.ds(pl.multiple_of(owner * PROJ_ROWS, 16), PROJ_ROWS), :CHANS] = piece[
            QKV_ROWS : QKV_ROWS + PROJ_ROWS
        ]
        spread[:VEC_ROWS, :CHANS] = piece[QKV_ROWS + PROJ_ROWS :]
        value = spread[:VEC_ROWS]
        small = jnp.where(lanes < CHANS // PARTS, value, 0.0)
        large = jnp.where(lanes < 96, value, 0.0)
        vec[...] += jnp.where(
            row < QV_BIAS,
            pltpu.roll(small, owner * (CHANS // PARTS), 1),
            jnp.where(
                row == QV_BIAS,
                pltpu.roll(large, (owner // 2) * 2 * LANES + (owner % 2) * 96, 1),
                pltpu.roll(large, owner * 96, 1),
            ),
        )
    spread[...] = jnp.zeros_like(spread)
    spread[:HEADS, :RPOS] = rel[...]
    pieces = []
    for h in range(HEADS):
        line = jnp.broadcast_to(spread[h : h + 1, :LANES], (WIN, LANES))
        for y in range(WIN):
            pieces.append(
                pltpu.roll(line, (15 * y - 112) % LANES, 1, stride=1, stride_axis=0)
            )
    lines = jnp.concatenate(pieces, 0)
    u, lane = iota((LANES, 128), 0), iota((LANES, 128), 1) & 63
    pick = (u == (lane >> 3) * 15 + (lane & 7)).astype(F32)
    table[...] = dot(lines, pick, 1, 0, HIGHEST)


def attend_kernel(
    place, scal, x_low, x_high, qkv, vec, table, proj, *refs
):
    mixed, probs, attended, after, start = refs[-6:-1]
    wide = refs[-1]
    k = place(pl.program_id(0))
    size, first = scal[0], block_first(scal, k)
    wide[...] = jnp.zeros_like(wide)
    wide[:4, :, :CHANS] = pltpu.roll(x_low[...], IMG - SHIFT, 1)
    wide[4:, :, :CHANS] = pltpu.roll(x_high[...], IMG - SHIFT, 1)
    mask = frame_mask(size, first)
    begin = mask * wide[...]
    start[...] = begin
    unit, _ = normalize(begin)
    normed = unit * vec[PRE_GAIN, :LANES] + vec[PRE_SHIFT, :LANES]
    mixed[...] = (
        nt(normed.reshape(BLOCK, LANES), qkv[...]) + vec[QV_BIAS : QV_BIAS + 1]
    ).reshape(mixed.shape)

    def step(pair, carry):
        query = window_pair(mixed, pair, 0)
        keys = window_pair(mixed, pair, LANES)
        values = window_pair(mixed, pair, 2 * LANES)
        scores = head_products(keys, [q * HD**-0.5 for q in query]) + table[...]
        scores = scores.reshape(HEADS, 64, 128) + pair_fill(size, first, pair)[None]
        scores = jnp.exp(scores - jnp.max(scores, 1, keepdims=True))
        prob = (scores * (1.0 / jnp.sum(scores, 1, keepdims=True))).reshape(HEADS * 64, 128)
        probs[0, pair] = prob
        for w, tiles in enumerate(turned_tiles(prob)):
            part = slice(64 * w, 64 * w + 64)
            put_window(attended, pair, w, 0, mix(tiles, values[0][part], values[1][part]))
        return carry

    lax.fori_loop(0, PAIRS, step, 0)
    out = nn(attended[...].reshape(BLOCK, LANES), proj[...]) + vec[PROJ_BIAS : PROJ_BIAS + 1, :LANES]
    after[...] = begin + mask * out.reshape(after.shape)


def feed_kernel(scal, value, vec, p0, p1, p2, p3, pre, after, up, down):
    @pl.when(pl.program_id(0) == 0)
    def _():
        up[...] = jnp.zeros_like(up)
        down[...] = jnp.zeros_like(down)
        for k, piece in enumerate((p0, p1, p2, p3)):
            rows = pl.ds(pl.multiple_of((scal[2] ^ k) * FEED_ROWS, 32), FEED_ROWS)
            up[rows, :CHANS] = piece[:FEED_ROWS]
            down[rows, :CHANS] = piece[FEED_ROWS:]

    size, first = scal[0], block_first(scal, pl.program_id(0))
    mask = frame_mask(size, first)
    unit, _ = normalize(value[...])
    normed = unit * vec[MID_GAIN, :LANES] + vec[MID_SHIFT, :LANES]
    hidden = nt(normed.reshape(BLOCK, LANES), up[...]) + vec[UP_BIAS : UP_BIAS + 1, :HID]
    pre[...] = hidden.reshape(pre.shape)
    act = hidden * gelu_parts(hidden)
    out = nn(act, down[...]) + vec[DOWN_BIAS : DOWN_BIAS + 1, :LANES]
    after[...] = value[...] + mask * out.reshape(value.shape)


def put_shifted(ref, row, value):
    cols = iota(value.shape, 1)
    ref[pl.ds(row, 1), :, LANES : 2 * LANES] = value
    ref[pl.ds(row, 1), :, :LANES] = jnp.where(cols == 0, 0.0, pltpu.roll(value, 1, 1))
    ref[pl.ds(row, 1), :, 2 * LANES :] = jnp.where(
        cols == IMG - 1, 0.0, pltpu.roll(value, IMG - 1, 1)
    )


def spread_rows(scal, after, spread, height):
    base = scal[1]

    def one(row, carry):
        above = (base + SHIFT - 1 + row == IMG - 1) & (row == 0)
        below = (wrapped(wrapped(base + SHIFT - 1 + row)) == 0) & (row == height + 1)
        value = pltpu.roll(after[pl.ds(row + SHIFT - 1, 1)], SHIFT, 1)
        put_shifted(spread, row, jnp.where(above | below, 0.0, value))
        return carry

    lax.fori_loop(0, height + 2, one, 0)


def conv_back_kernel(
    scal,
    after,
    cot,
    cot_above,
    cot_below,
    p0,
    p1,
    p2,
    p3,
    d_mid,
    grads,
    vec,
    wide,
    spread,
    d_spread,
    tall,
    gathered,
    padded,
    grad,
):
    height = cot.shape[0]
    share = CHANS // PARTS
    k = pl.program_id(0)
    size, base, me = scal[0], scal[1], scal[2]

    @pl.when(k == 0)
    def _():
        for ref in (wide, tall, padded, grad, vec):
            ref[...] = jnp.zeros_like(ref)
        for n, piece in enumerate((p0, p1, p2, p3)):
            gathered[me ^ n] = piece[...]
        for s in range(PARTS):
            rows = slice(share * s, share * s + share)
            for i in range(3):
                for j in range(3):
                    part = gathered[s, 3 * i + j]
                    wide[i, rows, LANES * j : LANES * j + CHANS] = part
                    at = LANES * (2 - j) + share * s
                    tall[i, at : at + share, :CHANS] = part
        spread_rows(scal, after, spread, height)

        def put(row, value, image_row):
            padded[0, :, :CHANS] = value
            shape = (1, IMG, LANES)
            mask = (image_row < size) & (iota(shape, 1) < size)
            put_shifted(d_spread, row, jnp.where(mask, padded[...], 0.0))

        for row in range(SHIFT + 1):
            put(row, cot_above[row], wrapped(base + IMG - 1 + row))
            below = height + SHIFT + 1 + row
            put(below, cot_below[row], wrapped(wrapped(base + IMG - 1 + below)))

        def two(row, carry):
            at = row + SHIFT + 1
            put(at, cot[row], wrapped(wrapped(base + IMG - 1 + at)))
            return carry

        lax.fori_loop(0, height, two, 0)

    shape = (WIN, IMG, LANES)
    first = wrapped(base + WIN * k)
    rows = wrapped(first + iota(shape, 0))
    total = jnp.zeros(shape, F32)
    for i in range(3):
        block = d_spread[pl.ds(WIN * k + 2 - i, WIN)].reshape(BLOCK, 3 * LANES)
        part = nn(block, tall[i]).reshape(shape)
        if i == 0:
            part = jnp.where(rows == IMG - 1, 0.0, part)
        if i == 2:
            part = jnp.where(rows == 0, 0.0, part)
        total = total + part
    d_mid[...] = pltpu.roll(total, IMG - SHIFT, 1)

    @pl.when(k < height // WIN)
    def _():
        d_conv = d_spread[pl.ds(WIN * k + SHIFT + 1, WIN), :, LANES : 2 * LANES].reshape(
            BLOCK, LANES
        )
        turned = turn(d_conv)
        for i in range(3):
            block = spread[pl.ds(WIN * k + i, WIN)].reshape(BLOCK, 3 * LANES)
            grad[i] += nn(turned, block)
        vec[CONV_BIAS : CONV_BIAS + 1, :LANES] += jnp.sum(d_conv, 0, keepdims=True)

    @pl.when(k == pl.num_programs(0) - 1)
    def _():
        for s in range(PARTS):
            for i in range(3):
                for j in range(3):
                    at = CONV_ROWS * (3 * i + j)
                    grads[s, at : at + share] = grad[
                        i, share * s : share * s + share, LANES * j : LANES * j + LANES
                    ]


def conv_kernel_body(scal, after, images, wide, vec, *refs):
    out, spread, padded = refs[-3:]
    height = images.shape[0]
    k = pl.program_id(0)

    @pl.when(k == 0)
    def _():
        padded[...] = jnp.zeros_like(padded)
        spread_rows(scal, after, spread, height)

    own = pl.ds(WIN * k, WIN)
    padded[:, :, :CHANS] = images[own]
    total = jnp.zeros((BLOCK, LANES), F32)
    for i in range(3):
        block = spread[pl.ds(WIN * k + i, WIN)].reshape(BLOCK, 3 * LANES)
        total = total + nt(block, wide[i])
    mask = plain_mask(scal[0], wrapped(scal[1] + SHIFT) + WIN * k, WIN)
    conv = (total + vec[CONV_BIAS : CONV_BIAS + 1, :LANES]).reshape(mask.shape)
    out[...] = (mask * (padded[...] + conv))[:, :, :CHANS]


def feed_back_kernel(
    scal, d_mid, value, pre, attended, up, down, proj, vec, *refs
):
    d_attn, d_att, grads, g_vec, g_up, g_down, g_proj = refs[-7:]
    k = pl.program_id(0)
    steps = pl.num_programs(0)

    @pl.when(k == 0)
    def _():
        for ref in (g_up, g_down, g_proj, g_vec):
            ref[...] = jnp.zeros_like(ref)

    size, first = scal[0], block_first(scal, k)
    mask = frame_mask(size, first)
    row = iota((WIN, IMG, LANES), 0) + WIN * k
    own = ((row >= SHIFT) & (row < steps * WIN - SHIFT)).reshape(BLOCK, LANES)
    mid = d_mid[...]
    d_ff = (mask * mid).reshape(BLOCK, LANES)
    hidden = pre[...].reshape(BLOCK, HID)
    phi = gelu_parts(hidden)
    act = hidden * phi
    slope = phi + hidden * (jnp.exp(-0.5 * hidden * hidden) * 0.3989422804014327)
    d_pre = nt(d_ff, down[...]) * slope
    d_normed = nn(d_pre, up[...])
    unit3, scale = normalize(value[...])
    unit = unit3.reshape(BLOCK, LANES)
    gain = vec[MID_GAIN : MID_GAIN + 1, :LANES]
    normed = unit * gain + vec[MID_SHIFT : MID_SHIFT + 1, :LANES]
    grad = (d_normed * gain).reshape(value.shape)
    d_out = mid + normalize_back(grad, unit3, scale)
    d_attn[...] = d_out
    d_proj = (mask * d_out).reshape(BLOCK, LANES)
    d_att[...] = nt(d_proj, proj[...]).reshape(d_att.shape)

    def gather(part):
        d_ff_own, d_pre_own = d_ff[part], d_pre[part]
        d_normed_own = d_normed[part]
        g_down[...] += nn(turn(d_ff_own), act[part])
        g_up[...] += nn(turn(normed[part]), d_pre_own)
        g_vec[UP_BIAS : UP_BIAS + 1, :HID] += jnp.sum(d_pre_own, 0, keepdims=True)
        for at, v in (
            (MID_GAIN, d_normed_own * unit[part]),
            (MID_SHIFT, d_normed_own),
            (DOWN_BIAS, d_ff_own),
        ):
            g_vec[at : at + 1, :LANES] += jnp.sum(v, 0, keepdims=True)

    @pl.when(k == 0)
    def _():
        gather(slice(SHIFT * IMG, BLOCK))

    @pl.when((k > 0) & (k < steps - 1))
    def _():
        gather(slice(0, BLOCK))

    @pl.when(k == steps - 1)
    def _():
        gather(slice(0, SHIFT * IMG))

    @pl.when(k > 0)
    def _():
        g_proj[...] += nn(turn(d_proj), attended[...].reshape(BLOCK, LANES))
        g_vec[PROJ_BIAS : PROJ_BIAS + 1, :LANES] += jnp.sum(d_proj, 0, keepdims=True)

    @pl.when(k == steps - 1)
    def _():
        for at, ref, rows in (
            (0, g_up, FEED_ROWS),
            (FEED_ROWS, g_down, FEED_ROWS),
            (2 * FEED_ROWS, g_proj, PROJ_ROWS),
        ):
            value = ref[...].T
            for s in range(PARTS):
                grads[s, at : at + rows, :184] = value[rows * s : rows * s + rows]


def attend_back_kernel(place, first_call, last_call, scal, start, mixed, probs, d_att, *refs):
    refs = list(refs)
    if last_call:
        vec, qkv, vec_conv, vec_feed = refs[:4]
        d_mixed, tail, g_qkv, g_table, g_mixed, lines = refs[-6:]
    else:
        d_mixed, g_qkv, g_table, g_mixed = refs[-4:]
    if not first_call:
        before = refs[4 if last_call else 0 :][:3]
    m = pl.program_id(0)
    k = place(m)

    @pl.when(m == 0)
    def _():
        for n, ref in enumerate((g_qkv, g_table, g_mixed)):
            ref[...] = jnp.zeros_like(ref) if first_call else before[n][...]

    counted = (k > 0).astype(F32)

    def step(pair, carry):
        query = [q * HD**-0.5 for q in window_pair(mixed, pair, 0)]
        keys = window_pair(mixed, pair, LANES)
        values = window_pair(mixed, pair, 2 * LANES)
        d_rows = window_pair(d_att, pair, 0)
        prob = probs[0, pair]
        d_prob = head_products(values, d_rows).reshape(HEADS, 64, 128)
        prob3 = prob.reshape(HEADS, 64, 128)
        d_score = prob3 * (d_prob - jnp.sum(prob3 * d_prob, 1, keepdims=True))
        d_score = d_score.reshape(HEADS * 64, 128)
        g_table[...] += counted * d_score
        prob_tiles = straight_tiles(prob)
        score_tiles = straight_tiles(d_score)
        turned = turned_tiles(d_score)
        for w in range(2):
            part = slice(64 * w, 64 * w + 64)
            d_query = mix(turned[w], keys[0][part], keys[1][part])
            put_window(d_mixed, pair, w, 0, [d * HD**-0.5 for d in d_query])
            put_window(
                d_mixed, pair, w, LANES, mix(score_tiles[w], query[0][part], query[1][part])
            )
            put_window(
                d_mixed, pair, w, 2 * LANES, mix(prob_tiles[w], d_rows[0][part], d_rows[1][part])
            )
        return carry

    lax.fori_loop(0, PAIRS, step, 0)

    @pl.when(k > 0)
    def _():
        unit, _ = normalize(start[...])
        d_all = d_mixed[...].reshape(BLOCK, 3 * LANES)
        g_qkv[...] += nn(turn(unit.reshape(BLOCK, LANES)), d_all)
        g_mixed[0:1] += jnp.sum(d_all, 0, keepdims=True)

    if not last_call:
        return

    @pl.when(m == pl.num_programs(0) - 1)
    def _():
        sums = g_mixed[...]
        cross = g_qkv[...].T
        weight = qkv[:, :184]
        lines[...] = vec_conv[...] + vec_feed[...]
        lines[PRE_GAIN : PRE_GAIN + 1, :184] = jnp.sum(cross * weight, 0, keepdims=True)
        lines[PRE_SHIFT : PRE_SHIFT + 1, :LANES] = nn(sums, qkv[...])[0:1]
        lines[QV_BIAS : QV_BIAS + 1] = sums[0:1]
        full = cross * vec[PRE_GAIN : PRE_GAIN + 1, :184] + sums.T[:, 0:1] * vec[
            PRE_SHIFT : PRE_SHIFT + 1, :184
        ]
        folded = g_table[...]
        lane, u = iota((128, LANES), 0) & 63, iota((128, LANES), 1)
        pick = (u == 112 - 15 * (lane >> 3) - (lane & 7)).astype(F32)
        spread = dot(folded, pick, 1, 0, HIGHEST).reshape(HEADS, WIN, WIN, LANES)
        rel = []
        for h in range(HEADS):
            line = jnp.zeros((WIN, LANES), F32)
            for y in range(WIN):
                line = line + pltpu.roll(spread[h, y], 15 * y, 1, stride=1, stride_axis=0)
            rel.append(jnp.sum(line, 0, keepdims=True))
        share = CHANS // PARTS
        value = lines[...]
        for s in range(PARTS):
            for m3 in range(3):
                at = s * 3 + m3
                begin = (at // 4) * LANES + (at % 4) * 48
                tail[s, 48 * m3 : 48 * m3 + 48, :184] = full[begin : begin + 48]

            def back(amount):
                return pltpu.roll(value, (3 * LANES - amount) % (3 * LANES), 1)[:, :LANES]

            row = iota((VEC_ROWS, LANES), 0)
            tail[s, QKV_ROWS : QKV_ROWS + VEC_ROWS] = jnp.where(
                row < QV_BIAS,
                back(share * s),
                jnp.where(row == QV_BIAS, back((s // 2) * 2 * LANES + (s % 2) * 96), back(96 * s)),
            )
            for h in range(HEADS):
                at = QKV_ROWS + VEC_ROWS + h
                tail[s, at : at + 1] = rel[h]


def image_back_kernel(scal, d_mixed, start, d_attn, cot, qkv, vec, *refs):
    out, padded = refs[-2:]
    rows = out.shape[0]
    m = pl.program_id(0)
    size = scal[0]
    first = wrapped(scal[1] + SHIFT) + rows * m
    unit3, scale = normalize(start[...])
    d_normed = nn(d_mixed[...].reshape(rows * IMG, 3 * LANES), qkv[...])
    grad = (d_normed * vec[PRE_GAIN : PRE_GAIN + 1, :LANES]).reshape(unit3.shape)
    value = d_attn[...] + normalize_back(grad, unit3, scale)
    padded[...] = jnp.zeros_like(padded)
    padded[:, :, :CHANS] = cot[...]
    out[...] = (plain_mask(size, first, rows) * (padded[...] + pltpu.roll(value, SHIFT, 1)))[
        :, :, :CHANS
    ]


def whole(shape):
    return pl.BlockSpec(tuple(shape), lambda m, s: (0,) * len(shape))


def rows_at(place, rows=WIN):
    def make(shape):
        rest = tuple(shape[1:])
        return pl.BlockSpec((rows,) + rest, lambda m, s: (place(m),) + (0,) * len(rest))

    return make


def untouched(shape):
    return pl.BlockSpec(memory_space=pl.ANY)


def call(kernel, steps, scal, ins, outs, scratch=(), after=(), keep=None, flops=0):
    ins = list(ins) + [(a, untouched) for a in after]
    size = sum(4 * a.size for a, make in ins if make is not untouched)
    size += sum(4 * functools.reduce(lambda p, q: p * q, s) for s, _ in outs)
    return pl.pallas_call(
        kernel,
        grid_spec=pltpu.PrefetchScalarGridSpec(
            num_scalar_prefetch=1,
            grid=(steps,),
            in_specs=[make(a.shape) for a, make in ins],
            out_specs=[make(s) for s, make in outs],
            scratch_shapes=list(scratch),
        ),
        out_shape=[jax.ShapeDtypeStruct(tuple(s), F32) for s, _ in outs],
        input_output_aliases={i + 1: o for i, o in (keep or {}).items()},
        compiler_params=pltpu.CompilerParams(
            dimension_semantics=("arbitrary",), vmem_limit_bytes=VMEM_BYTES
        ),
        cost_estimate=pl.CostEstimate(flops=flops, bytes_accessed=size, transcendentals=0),
    )(scal, *[a for a, _ in ins])


def pad_rows(value, rows):
    return jnp.pad(value, ((0, rows - value.shape[0]), (0, 0)))


def open_halves(value):
    n = value.shape[0] // HALF
    value = value.reshape(n, HALF, -1)
    return jnp.pad(value, ((0, 0), (0, 1), (0, 0))).reshape(n * (HALF + 1), -1)


def close_halves(value):
    n = value.shape[0] // (HALF + 1)
    return value.reshape(n, HALF + 1, -1)[:, :HALF].reshape(n * HALF, -1)


def body(
    images,
    item_sizes,
    cotangent,
    pre_gain,
    pre_shift,
    qkv_weight,
    qv_bias,
    rel_table,
    proj_weight,
    proj_bias,
    mid_gain,
    mid_shift,
    up_weight,
    up_bias,
    down_weight,
    down_bias,
    conv_kernel,
    conv_bias,
):
    height, breadth = images.shape[1:3]
    me = lax.axis_index("tp")
    strip = height + 2 * SHIFT
    steps = strip // WIN
    image, cot = images[0], cotangent[0]
    share = CHANS // PARTS

    short = jnp.stack([pre_gain, pre_shift, proj_bias, mid_gain, mid_shift, down_bias, conv_bias])
    vectors = jnp.concatenate(
        [
            jnp.pad(short, ((0, 0), (0, CHANS - share))),
            jnp.pad(open_halves(qv_bias[:, None]).reshape(1, -1), ((0, 0), (0, CHANS - 96))),
            jnp.pad(up_bias[None], ((0, 0), (0, CHANS - 90))),
            jnp.zeros((VEC_ROWS - 9, CHANS), F32),
        ],
        0,
    )
    mine1 = jnp.concatenate([open_halves(qkv_weight.T), open_halves(proj_weight), vectors], 0)
    mine2 = jnp.concatenate([pad_rows(up_weight.T, FEED_ROWS), pad_rows(down_weight, FEED_ROWS)], 0)
    mine3 = conv_kernel.transpose(0, 1, 3, 2).reshape(9, share, CHANS)
    all1 = gather_tp(mine1)
    x_above = from_behind(image[-SHIFT:], "tp", 1)
    x_below = from_behind(image[:SHIFT], "tp", -1)
    all2 = gather_tp(mine2)
    all3 = gather_tp(mine3)
    c_above = from_behind(cot[-SHIFT - 1 :], "tp", 1)
    c_below = from_behind(cot[: SHIFT + 1], "tp", -1)
    scal = jnp.stack([item_sizes[0], (me * height + IMG - SHIFT) % IMG, me]).astype(jnp.int32)

    def frame(lanes):
        return (strip, breadth, lanes)

    qkv, proj, vec, table = call(
        prepare_kernel,
        1,
        scal,
        [(p, whole) for p in all1] + [(rel_table.T, whole)],
        [((3 * LANES, LANES), whole), ((LANES, LANES), whole), ((VEC_ROWS, 3 * LANES), whole), ((HEADS * 64, 128), whole)],
        [pltpu.VMEM((VEC_ROWS, 3 * LANES), F32)],
        flops=10**8,
    )
    shapes = [frame(3 * LANES), (steps, PAIRS, HEADS * 64, 128), frame(LANES), frame(LANES), frame(LANES)]

    def attend(place, x, low, high, old):
        spec = rows_at(place)
        return call(
            functools.partial(attend_kernel, place),
            2,
            scal,
            [(x, rows_at(low, SHIFT)), (x, rows_at(high, SHIFT)), (qkv, whole), (vec, whole), (table, whole), (proj, whole)]
            + [(o, untouched) for o in old],
            [(s, rows_at(place, 1) if n == 1 else spec) for n, s in enumerate(shapes)],
            [pltpu.VMEM((WIN, breadth, LANES), F32)],
            keep={6 + n: n for n in range(len(old))},
            flops=4 * 10**9,
        )

    old = attend(lambda m: m + 1, image, lambda m: 2 * m + 1, lambda m: 2 * m + 2, [])
    edges = jnp.concatenate([x_above, image[:SHIFT], image[-SHIFT:], x_below], 0)
    mixed, probs, attended, after_attn, start = attend(
        lambda m: m * (steps - 1), edges, lambda m: 2 * m, lambda m: 2 * m + 1, old
    )
    rows = rows_at(lambda m: m)
    pre, after_mlp, up, down = call(
        feed_kernel,
        steps,
        scal,
        [(after_attn, rows), (vec, whole)] + [(p, whole) for p in all2],
        [(frame(HID), rows), (frame(LANES), rows), ((HID, LANES), whole), ((HID, LANES), whole)],
        flops=5 * 10**9,
    )
    d_mid, g_conv, vec_conv, wide = call(
        conv_back_kernel,
        steps,
        scal,
        [(after_mlp, whole), (cot, whole), (c_above, whole), (c_below, whole)] + [(p, whole) for p in all3],
        [(frame(LANES), rows), ((PARTS, 9 * CONV_ROWS, LANES), whole), ((VEC_ROWS, 3 * LANES), whole), ((3, LANES, 3 * LANES), whole)],
        [
            pltpu.VMEM((height + 2, breadth, 3 * LANES), F32),
            pltpu.VMEM((strip + 2, breadth, 3 * LANES), F32),
            pltpu.VMEM((3, 3 * LANES, LANES), F32),
            pltpu.VMEM((PARTS, 9, share, CHANS), F32),
            pltpu.VMEM((1, breadth, LANES), F32),
            pltpu.VMEM((3, 184, 3 * LANES), F32),
        ],
        flops=2 * 10**10,
    )
    d_attn, d_att, g_feed, vec_feed = call(
        feed_back_kernel,
        steps,
        scal,
        [(d_mid, rows), (after_attn, rows), (pre, rows), (attended, rows), (up, whole), (down, whole), (proj, whole), (vec, whole)],
        [(frame(LANES), rows), (frame(LANES), rows), ((PARTS, REST_ROWS, LANES), whole), ((VEC_ROWS, 3 * LANES), whole)],
        [pltpu.VMEM((184, HID), F32), pltpu.VMEM((184, HID), F32), pltpu.VMEM((184, LANES), F32)],
        flops=10**10,
    )

    chain = tp_stage(jnp.concatenate([g_conv, g_feed], 1), 0)
    g_shapes = [(184, 3 * LANES), (HEADS * 64, 128), (8, 3 * LANES)]

    def attend_back(at, count, old, d_mixed, after):
        place = lambda m: m + at
        first_call, last_call = at == 0, at + count == steps
        spec = rows_at(place)
        ins = [(start, spec), (mixed, spec), (probs, rows_at(place, 1)), (d_att, spec)]
        outs = [(frame(3 * LANES), spec)]
        if last_call:
            ins += [(vec, whole), (qkv, whole), (vec_conv, whole), (vec_feed, whole)]
            outs += [((PARTS, QKV_ROWS + VEC_ROWS + 8, LANES), whole)]
        scratch = []
        if last_call:
            scratch = [pltpu.VMEM(s, F32) for s in g_shapes] + [pltpu.VMEM((VEC_ROWS, 3 * LANES), F32)]
        else:
            outs += [(s, whole) for s in g_shapes]
        ins += [(o, whole) for o in old]
        keep = None
        if d_mixed is not None:
            keep = {len(ins): 0}
            ins += [(d_mixed, untouched)]
        return call(
            functools.partial(attend_back_kernel, place, first_call, last_call),
            count,
            scal,
            ins,
            outs,
            scratch,
            after=after,
            keep=keep,
            flops=5 * 10**9 * count,
        )

    d_mixed, *sums = attend_back(0, 1, [], None, [])
    chain = tp_stage(chain, 1)[0]
    d_mixed, *sums = attend_back(1, 1, sums, d_mixed, [])
    d_mixed, *sums = attend_back(2, 1, sums, d_mixed, [chain])
    bits = dp_bits()
    held = chain
    halved = []
    for n, bit in enumerate(bits):
        held = dp_halve(held, bit)
        halved.append(held)
    d_mixed, tail = attend_back(3, 1, sums, d_mixed, halved[:1])

    last = tp_stage(tail, 0)
    (block_out,) = call(
        conv_kernel_body,
        height // WIN,
        scal,
        [(after_mlp, whole), (image, whole), (wide, whole), (vec, whole)],
        [(image.shape, rows)],
        [pltpu.VMEM((height + 2, breadth, 3 * LANES), F32), pltpu.VMEM((WIN, breadth, LANES), F32)],
        after=[tail],
        flops=10**10,
    )
    last = tp_stage(last, 1)[0]
    half_rows = rows_at(lambda m: m + 1, SHIFT)
    (grad_images,) = call(
        image_back_kernel,
        height // SHIFT,
        scal,
        [(d_mixed, half_rows), (start, half_rows), (d_attn, half_rows), (cot, rows_at(lambda m: m, SHIFT)), (qkv, whole), (vec, whole)],
        [(image.shape, rows_at(lambda m: m, SHIFT))],
        [pltpu.VMEM((SHIFT, breadth, LANES), F32)],
        after=[block_out],
        flops=4 * 10**9,
    )
    for bit in reversed(bits):
        held = dp_join(held, bit)
        last = dp_add(last, bit)

    conv = held[: 9 * CONV_ROWS].reshape(3, 3, CONV_ROWS, LANES)[:, :, :share, :CHANS]
    feed = held[9 * CONV_ROWS :, :CHANS]
    vectors = last[QKV_ROWS : QKV_ROWS + VEC_ROWS]
    rel = last[QKV_ROWS + VEC_ROWS : QKV_ROWS + VEC_ROWS + HEADS, :RPOS]

    def short_vector(at):
        return vectors[at, :share]

    return (
        block_out[None],
        grad_images[None],
        short_vector(PRE_GAIN),
        short_vector(PRE_SHIFT),
        close_halves(last[:QKV_ROWS, :CHANS]).T,
        close_halves(vectors[QV_BIAS, :96][:, None])[:, 0],
        rel[:, ::-1].T,
        close_halves(feed[2 * FEED_ROWS : 2 * FEED_ROWS + PROJ_ROWS]),
        short_vector(PROJ_BIAS),
        short_vector(MID_GAIN),
        short_vector(MID_SHIFT),
        feed[:90].T,
        vectors[UP_BIAS, :90],
        feed[FEED_ROWS : FEED_ROWS + 90],
        short_vector(DOWN_BIAS),
        conv.transpose(0, 1, 3, 2),
        short_vector(CONV_BIAS),
    )


def solution(mesh):
    placed = (
        P("dp", "tp", None, None),
        P("dp"),
        P("dp", "tp", None, None),
        P("tp"),
        P("tp"),
        P(None, "tp"),
        P("tp"),
        P(),
        P("tp", None),
        P("tp"),
        P("tp"),
        P("tp"),
        P(None, "tp"),
        P("tp"),
        P("tp", None),
        P("tp"),
        P(None, None, None, "tp"),
        P("tp"),
    )
    return jax.shard_map(
        body,
        mesh=mesh,
        in_specs=placed,
        out_specs=(
            P("dp", "tp", None, None),
            P("dp", "tp", None, None),
            P("tp"),
            P("tp"),
            P(None, "tp"),
            P("tp"),
            P(),
            P("tp", None),
            P("tp"),
            P("tp"),
            P("tp"),
            P(None, "tp"),
            P("tp"),
            P("tp", None),
            P("tp"),
            P(None, None, None, "tp"),
            P("tp"),
        ),
        check_vma=False,
    )
```

```python
import functools

import jax
import jax.numpy as jnp
from jax import lax
from jax.experimental import pallas as pl
from jax.experimental.pallas import tpu as pltpu
from jax.sharding import PartitionSpec as P

WIN = 8
IMG = 96
SHIFT = 4
EPSILON = 1e-05
NEG_FILL = -1e30
CHANS = 180
HEADS = 6
HD = 30
HALF = 15
SLOT = 32
LANES = 256
INNER = 192
HID = 384
RPOS = 225
HIGH = lax.Precision.HIGH
HIGHEST = lax.Precision.HIGHEST
F32 = jnp.float32
BF16 = jnp.bfloat16
BLOCK = WIN * IMG
PAIRS = IMG // WIN // 2
PARTS = 4
MIB = 2**20
STEPS = 4

QKV_ROWS, PROJ_ROWS, VEC_ROWS = 144, 48, 16
FEED_ROWS = 96
CONV_ROWS = 48
REL_ROWS = 8
FEED_AT = 2 * QKV_ROWS
VEC_AT = FEED_AT + 3 * FEED_ROWS
REL_AT = VEC_AT + 2 * VEC_ROWS
TAIL_ROWS = REL_AT + 2 * REL_ROWS
PRE_GAIN, PRE_SHIFT, PROJ_BIAS, MID_GAIN, MID_SHIFT, DOWN_BIAS, CONV_BIAS, QV_BIAS, UP_BIAS = range(9)


def flip(axis, bit):
    return [(i, i ^ bit) for i in range(lax.axis_size(axis))]


def from_behind(block, axis, distance):
    n = lax.axis_size(axis)
    return lax.ppermute(block, axis, [((i - distance) % n, i) for i in range(n)])


def gather_tp(block):
    got = {0: block}
    for bit in (2, 1):
        got.update({k | bit: lax.ppermute(b, "tp", flip("tp", bit)) for k, b in list(got.items())})
    return [got[k] for k in range(PARTS)]


def tie(value, *others):
    return lax.optimization_barrier((value, others))[0]


def dp_bits():
    n = lax.axis_size("dp")
    return [1 << b for b in range(n.bit_length() - 1)]


def dp_halve(held, bit, *others):
    half = held.shape[0] // 2
    odd = (lax.axis_index("dp") & bit) != 0
    send = jnp.where(odd, held[:half], held[half:])
    got = lax.ppermute(send, "dp", flip("dp", bit))
    if others:
        got = tie(got, *others)
    return jnp.where(odd, held[half:], held[:half]) + got


def dp_join(held, bit):
    odd = (lax.axis_index("dp") & bit) != 0
    got = lax.ppermute(held, "dp", flip("dp", bit))
    return jnp.concatenate([jnp.where(odd, got, held), jnp.where(odd, held, got)], 0)


def dp_add(held, bit):
    return held + lax.ppermute(held, "dp", flip("dp", bit))


def dot(left, right, left_dim, right_dim, precision=None):
    return lax.dot_general(
        left,
        right,
        (((left_dim,), (right_dim,)), ((), ())),
        precision=precision,
        preferred_element_type=F32,
    )


def nn(left, right):
    return dot(left, right, 1, 0, HIGH)


def nt(left, right):
    return dot(left, right, 1, 1, HIGH)


def turn(value):
    return value.T[:184]


def iota(shape, dim):
    return lax.broadcasted_iota(jnp.int32, shape, dim)


def wrapped(position):
    return jnp.where(position >= IMG, position - IMG, position)


def frame_mask(size, first, rows=WIN):
    shape = (rows, IMG, LANES)
    row = wrapped(first + iota(shape, 0))
    col = wrapped(iota(shape, 1) + SHIFT)
    return ((row < size) & (col < size) & (iota(shape, 2) < CHANS)).astype(F32)


def plain_mask(size, first, rows):
    shape = (rows, IMG, LANES)
    row = wrapped(first + iota(shape, 0))
    return ((row < size) & (iota(shape, 1) < size) & (iota(shape, 2) < CHANS)).astype(F32)


def is_channel(shape):
    return iota(shape, len(shape) - 1) < CHANS


def mean(value):
    return jnp.sum(value, axis=-1, keepdims=True) * (1.0 / CHANS)


def normalize(value):
    centre = jnp.where(is_channel(value.shape), value - mean(value), 0.0)
    scale = lax.rsqrt(mean(centre * centre) + EPSILON)
    return centre * scale, scale


def normalize_back(grad, unit, scale):
    value = scale * (grad - mean(grad) - unit * mean(grad * unit))
    return jnp.where(is_channel(value.shape), value, 0.0)


def upper(value):
    return value.astype(BF16).astype(F32)


def parted(value):
    high = upper(value)
    return jnp.where(iota(value.shape, 1) < 64, high, value - high)


def doubled(first, second):
    left = iota(first.shape, 1) < 64
    turned0 = pltpu.roll(first, 64, 1)
    turned1 = pltpu.roll(second, 64, 1)
    return (
        jnp.where(left, first, turned0),
        jnp.where(left, turned0, first),
        jnp.where(left, second, turned1),
    )


def head_products(rows, cols):
    lanes = iota((128, 128), 1)
    even = (lanes & 63) < SLOT
    outs = []
    for moving, fixed in zip(doubled(*rows), doubled(*cols)):
        high = fixed.astype(BF16)
        low = (fixed - high.astype(F32)).astype(BF16)
        held = jnp.concatenate([high, low], 1)
        pieces = parted(moving)
        ones = jnp.where(even, pieces, 0.0).astype(BF16)
        twos = jnp.where(even, 0.0, pieces).astype(BF16)
        both = []
        for w in range(2):
            part = slice(64 * w, 64 * w + 64)
            stream = jnp.concatenate([ones[part], twos[part]], 0)
            both.append(dot(jnp.concatenate([stream, stream], 1), held, 1, 1))
        outs.append(jnp.where(lanes < 64, both[0], both[1]))
    return jnp.concatenate(outs, 0)


def mix(tiles, first, second):
    lanes = iota((64, 128), 1)

    def product(part, block):
        high = block.astype(BF16)
        low = (block - high.astype(F32)).astype(BF16)
        held = jnp.concatenate([high, high, low, low], 0)
        stream = jnp.concatenate(part, 0)
        return dot(jnp.concatenate([stream, stream], 1), held, 1, 0)

    a = product(tiles[:4], first)
    b = product(tiles[4:], second)
    one = jnp.where(
        lanes < 64,
        jnp.where(lanes < 32, a[0:64], a[64:128]),
        jnp.where(lanes < 96, a[128:192], a[192:256]),
    )
    two = jnp.where(lanes < 32, b[0:64], b[64:128])
    return one, two


def straight_tiles(table):
    left = iota(table.shape, 1) < 64
    turned = pltpu.roll(table, 64, 1)
    outs = []
    for w in range(2):
        one = jnp.where(left, table, turned) if w == 0 else jnp.where(left, turned, table)
        both = parted(one).astype(BF16)
        outs.append([both[64 * h : 64 * h + 64] for h in range(HEADS)])
    return outs


def turned_tiles(table):
    high = upper(table)
    low = table - high
    outs = [[], []]
    for h in range(HEADS):
        part = slice(64 * h, 64 * h + 64)
        both = jnp.concatenate([high[part], low[part]], 0).astype(BF16).T
        for w in range(2):
            outs[w].append(both[64 * w : 64 * w + 64])
    return outs


def window_pair(ref, pair, start):
    cols = pl.ds(pl.multiple_of(pair * 2 * WIN, 2 * WIN), 2 * WIN)
    tiles = []
    for tile in range(2):
        block = ref[:, cols, start + 128 * tile : start + 128 * tile + 128]
        tiles.append(
            jnp.concatenate(
                [block[:, :WIN].reshape(64, 128), block[:, WIN:].reshape(64, 128)], 0
            )
        )
    return tiles


def put_window(ref, pair, w, start, tiles):
    cols = pl.ds(pl.multiple_of(pair * 2 * WIN + w * WIN, WIN), WIN)
    for tile in range(2):
        ref[:, cols, start + 128 * tile : start + 128 * tile + 128] = tiles[tile].reshape(
            WIN, WIN, 128
        )


def pair_fill(size, first, pair):
    shape = (64, 128)
    j, lane = iota(shape, 0), iota(shape, 1)
    i, window = lane & 63, 2 * pair + (lane >> 6)
    rows = wrapped(first + (j >> 3))
    cols = wrapped(window * WIN + (j & 7) + SHIFT)
    apart_rows = (first == IMG - WIN + SHIFT) & ((j >> 5) != (i >> 5))
    apart_cols = (window == IMG // WIN - 1) & (((j & 7) >> 2) != ((i & 7) >> 2))
    keep = (rows < size) & (cols < size)
    return jnp.where(apart_rows | apart_cols | jnp.logical_not(keep), NEG_FILL, 0.0)


def block_first(scal, k):
    return wrapped(scal[1] + WIN * k)


def block_of(ref, k):
    return ref.at[pl.ds(WIN * k, WIN)]


def put_part(keep, send, part, me, rows, value):
    place = part ^ me

    @pl.when((place & 1) == 0)
    def _():
        keep[place >> 1, rows] = value

    @pl.when((place & 1) == 1)
    def _():
        send[place >> 1, rows] = value


def gelu_parts(hidden):
    return 0.5 * (1.0 + lax.erf(hidden * 0.5**0.5))


def pack_kernel(qkv, proj, up, down, flat, first, second, line):
    first[...] = jnp.zeros_like(first)
    second[...] = jnp.zeros_like(second)
    for n in range(9):
        first[16 * n : 16 * n + HALF, :CHANS] = qkv[HALF * n : HALF * n + HALF]
    for n in range(3):
        at = QKV_ROWS + 16 * n
        first[at : at + HALF, :CHANS] = proj[HALF * n : HALF * n + HALF]
    share, hid = CHANS // PARTS, up.shape[1]
    second[:hid, :CHANS] = up[...].T
    second[FEED_ROWS : FEED_ROWS + hid, :CHANS] = down[...].T
    line[...] = jnp.zeros_like(line)
    line[0:1, : flat.shape[1]] = flat[...]
    value = line[...]
    lanes = iota((WIN, LANES), 1)
    at = QKV_ROWS + PROJ_ROWS

    def taken(begin):
        return pltpu.roll(value, (512 - begin) % 512, 1)[:, :LANES]

    for n in range(7):
        first[at + n : at + n + 1] = jnp.where(lanes < share, taken(share * n), 0.0)[0:1]
    total = jnp.zeros((WIN, LANES), F32)
    for n in range(6):
        piece = pltpu.roll(value, (512 - 7 * share + n) % 512, 1)[:, :LANES]
        total = total + jnp.where((lanes >= 16 * n) & (lanes < 16 * n + HALF), piece, 0.0)
    first[at + QV_BIAS : at + QV_BIAS + 1] = total[0:1]
    first[at + UP_BIAS : at + UP_BIAS + 1] = jnp.where(lanes < hid, taken(7 * share + hid), 0.0)[0:1]


def prepare_kernel(scal, p0, p1, p2, p3, rel, qkv, proj, vec, table, spread):
    me = scal[2]
    for ref in (qkv, vec, spread):
        ref[...] = jnp.zeros_like(ref)
    proj[INNER:] = jnp.zeros_like(proj[INNER:])
    lanes = iota((VEC_ROWS, 3 * LANES), 1)
    row = iota((VEC_ROWS, 3 * LANES), 0)
    for k, piece in enumerate((p0, p1, p2, p3)):
        owner = me ^ k
        for m in range(3):
            at = owner * 3 + m
            start = pl.multiple_of((at // 4) * LANES + (at % 4) * 48, 16)
            qkv[pl.ds(start, 48)] = piece[48 * m : 48 * m + 48]
        proj[pl.ds(pl.multiple_of(owner * PROJ_ROWS, 16), PROJ_ROWS)] = piece[
            QKV_ROWS : QKV_ROWS + PROJ_ROWS
        ]
        spread[:VEC_ROWS, :LANES] = piece[QKV_ROWS + PROJ_ROWS :]
        value = spread[:VEC_ROWS]
        vec[...] += jnp.where(
            row < QV_BIAS,
            pltpu.roll(value, owner * (CHANS // PARTS), 1),
            jnp.where(
                row == QV_BIAS,
                pltpu.roll(value, (owner // 2) * 2 * LANES + (owner % 2) * 96, 1),
                pltpu.roll(value, owner * 96, 1),
            ),
        )
    spread[...] = jnp.zeros_like(spread)
    spread[:HEADS, :RPOS] = rel[...]
    pieces = []
    for h in range(HEADS):
        line = jnp.broadcast_to(spread[h : h + 1, :LANES], (WIN, LANES))
        for y in range(WIN):
            pieces.append(
                pltpu.roll(line, (15 * y - 112) % LANES, 1, stride=1, stride_axis=0)
            )
    lines = jnp.concatenate(pieces, 0)
    u, lane = iota((LANES, 128), 0), iota((LANES, 128), 1) & 63
    pick = (u == (lane >> 3) * 15 + (lane & 7)).astype(F32)
    table[...] = dot(lines, pick, 1, 0, HIGHEST)


def attend_kernel(
    scal, above, image, below, qkv, vec, table, proj, mixed, probs, attended, after, start
):
    height = image.shape[0]
    start[...] = jnp.zeros_like(start)
    start[:SHIFT, :, :CHANS] = above[...]
    start[SHIFT : SHIFT + height, :, :CHANS] = image[...]
    start[SHIFT + height :, :, :CHANS] = below[...]

    def block(k, carry):
        size, first = scal[0], block_first(scal, k)
        rows = pl.ds(WIN * k, WIN)
        mask = frame_mask(size, first)
        begin = mask * pltpu.roll(start[rows], IMG - SHIFT, 1)
        start[rows] = begin
        unit, _ = normalize(begin)
        normed = unit * vec[PRE_GAIN, :LANES] + vec[PRE_SHIFT, :LANES]
        here = block_of(mixed, k)
        here[...] = (
            nt(normed.reshape(BLOCK, LANES), qkv[...]) + vec[QV_BIAS : QV_BIAS + 1]
        ).reshape(WIN, IMG, 3 * LANES)
        out_here = block_of(attended, k)
        for pair in range(PAIRS):
            query = window_pair(here, pair, 0)
            keys = window_pair(here, pair, LANES)
            values = window_pair(here, pair, 2 * LANES)
            scores = head_products(keys, [q * HD**-0.5 for q in query]) + table[...]
            scores = scores.reshape(HEADS, 64, 128) + pair_fill(size, first, pair)[None]
            scores = jnp.exp(scores - jnp.max(scores, 1, keepdims=True))
            prob = (scores * (1.0 / jnp.sum(scores, 1, keepdims=True))).reshape(HEADS * 64, 128)
            probs[k, pair] = prob
            for w, tiles in enumerate(turned_tiles(prob)):
                part = slice(64 * w, 64 * w + 64)
                put_window(out_here, pair, w, 0, mix(tiles, values[0][part], values[1][part]))
        out = nn(out_here[...].reshape(BLOCK, LANES), proj[...]) + vec[PROJ_BIAS : PROJ_BIAS + 1, :LANES]
        after[rows] = begin + mask * out.reshape(WIN, IMG, LANES)
        return carry

    lax.fori_loop(0, STEPS, block, 0)


def feed_kernel(scal, value, vec, p0, p1, p2, p3, pre, after, up, down):
    for k, piece in enumerate((p0, p1, p2, p3)):
        rows = pl.ds(pl.multiple_of((scal[2] ^ k) * FEED_ROWS, 32), FEED_ROWS)
        up[rows] = piece[:FEED_ROWS]
        down[rows] = piece[FEED_ROWS:]

    def block(k, carry):
        rows = pl.ds(WIN * k, WIN)
        mask = frame_mask(scal[0], block_first(scal, k))
        here = value[rows]
        unit, _ = normalize(here)
        normed = unit * vec[MID_GAIN, :LANES] + vec[MID_SHIFT, :LANES]
        hidden = nt(normed.reshape(BLOCK, LANES), up[...]) + vec[UP_BIAS : UP_BIAS + 1, :HID]
        pre[rows] = hidden.reshape(WIN, IMG, HID)
        act = hidden * gelu_parts(hidden)
        out = nn(act, down[...]) + vec[DOWN_BIAS : DOWN_BIAS + 1, :LANES]
        after[rows] = here + mask * out.reshape(here.shape)
        return carry

    lax.fori_loop(0, STEPS, block, 0)


def put_shifted(ref, row, value):
    cols = iota(value.shape, 1)
    ref[pl.ds(row, 1), :, LANES : 2 * LANES] = value
    ref[pl.ds(row, 1), :, :LANES] = jnp.where(cols == 0, 0.0, pltpu.roll(value, 1, 1))
    ref[pl.ds(row, 1), :, 2 * LANES :] = jnp.where(
        cols == IMG - 1, 0.0, pltpu.roll(value, IMG - 1, 1)
    )


def conv_back_kernel(
    scal,
    after,
    cot,
    cot_above,
    cot_below,
    p0,
    p1,
    p2,
    p3,
    d_mid,
    keep,
    send,
    vec,
    wide,
    d_spread,
    tall,
    gathered,
    padded,
    grad,
):
    height = cot.shape[0]
    share = CHANS // PARTS
    size, base, me = scal[0], scal[1], scal[2]
    for ref in (wide, tall, padded, grad, vec):
        ref[...] = jnp.zeros_like(ref)
    for n, piece in enumerate((p0, p1, p2, p3)):
        gathered[me ^ n] = piece[...]
    for s in range(PARTS):
        rows = slice(share * s, share * s + share)
        for i in range(3):
            for j in range(3):
                part = gathered[s, 3 * i + j]
                wide[i, rows, LANES * j : LANES * j + CHANS] = part
                at = LANES * (2 - j) + share * s
                tall[i, at : at + share, :CHANS] = part

    def put(row, value, image_row):
        padded[0, :, :CHANS] = value
        shape = (1, IMG, LANES)
        mask = (image_row < size) & (iota(shape, 1) < size)
        put_shifted(d_spread, row, jnp.where(mask, padded[...], 0.0))

    for row in range(SHIFT + 1):
        put(row, cot_above[row], wrapped(base + IMG - 1 + row))
        below = height + SHIFT + 1 + row
        put(below, cot_below[row], wrapped(wrapped(base + IMG - 1 + below)))

    def two(row, carry):
        at = row + SHIFT + 1
        put(at, cot[row], wrapped(wrapped(base + IMG - 1 + at)))
        return carry

    lax.fori_loop(0, height, two, 0)
    shape = (WIN, IMG, LANES)

    def block(k, carry):
        rows = wrapped(wrapped(base + WIN * k) + iota(shape, 0))
        total = jnp.zeros(shape, F32)
        for i in range(3):
            here = d_spread[pl.ds(WIN * k + 2 - i, WIN)].reshape(BLOCK, 3 * LANES)
            part = nn(here, tall[i]).reshape(shape)
            if i == 0:
                part = jnp.where(rows == IMG - 1, 0.0, part)
            if i == 2:
                part = jnp.where(rows == 0, 0.0, part)
            total = total + part
        d_mid[pl.ds(WIN * k, WIN)] = pltpu.roll(total, IMG - SHIFT, 1)
        return carry

    lax.fori_loop(0, STEPS, block, 0)

    def gradient(k, carry):
        here = pltpu.roll(after[pl.ds(WIN * k + SHIFT, WIN)], SHIFT, 1)
        turned = turn(here.reshape(BLOCK, LANES))
        rows = wrapped(wrapped(base + WIN * k + SHIFT) + iota((WIN, IMG, 1), 0))
        for i in range(3):
            around = d_spread[pl.ds(WIN * k + SHIFT + 2 - i, WIN)]
            if i == 0:
                around = jnp.where(rows == IMG - 1, 0.0, around)
            if i == 2:
                around = jnp.where(rows == 0, 0.0, around)
            grad[i, :184] += nn(turned, around.reshape(BLOCK, 3 * LANES))
        centre = d_spread[pl.ds(WIN * k + SHIFT + 1, WIN), :, LANES : 2 * LANES]
        vec[CONV_BIAS : CONV_BIAS + 1, :LANES] += jnp.sum(
            centre.reshape(BLOCK, LANES), 0, keepdims=True
        )
        return carry

    lax.fori_loop(0, height // WIN, gradient, 0)
    for i in range(3):
        for j in range(3):
            at = CONV_ROWS * (3 * i + j)
            value = grad[i, :, LANES * (2 - j) : LANES * (3 - j)].T
            for s in range(PARTS):
                put_part(
                    keep, send, s, me, slice(at, at + share), value[share * s : share * s + share]
                )


def conv_kernel_body(scal, after, images, wide, vec, *refs):
    out, spread, padded = refs[-3:]
    height = images.shape[0]
    base = scal[1]
    padded[...] = jnp.zeros_like(padded)

    def one(row, carry):
        above = (base + SHIFT - 1 + row == IMG - 1) & (row == 0)
        below = (wrapped(wrapped(base + SHIFT - 1 + row)) == 0) & (row == height + 1)
        value = pltpu.roll(after[pl.ds(row + SHIFT - 1, 1)], SHIFT, 1)
        put_shifted(spread, row, jnp.where(above | below, 0.0, value))
        return carry

    lax.fori_loop(0, height + 2, one, 0)

    def block(k, carry):
        own = pl.ds(WIN * k, WIN)
        padded[:, :, :CHANS] = images[own]
        total = jnp.zeros((BLOCK, LANES), F32)
        for i in range(3):
            here = spread[pl.ds(WIN * k + i, WIN)].reshape(BLOCK, 3 * LANES)
            total = total + nt(here, wide[i])
        mask = plain_mask(scal[0], wrapped(base + SHIFT) + WIN * k, WIN)
        conv = (total + vec[CONV_BIAS : CONV_BIAS + 1, :LANES]).reshape(mask.shape)
        out[own] = (mask * (padded[...] + conv))[:, :, :CHANS]
        return carry

    lax.fori_loop(0, height // WIN, block, 0)


def feed_back_kernel(
    scal, d_mid, value, pre, attended, up, down, proj, vec, *refs
):
    d_attn, d_att, grads, g_proj, g_vec, g_up, g_down = refs[-7:]
    for ref in (g_up, g_down, g_proj, g_vec):
        ref[...] = jnp.zeros_like(ref)
    size = scal[0]

    def block(k, rows, part, counted):
        here = pl.ds(WIN * k, WIN)
        mask = frame_mask(size, block_first(scal, k))
        mid = d_mid[here]
        d_ff = (mask * mid).reshape(BLOCK, LANES)
        hidden = pre[here].reshape(BLOCK, HID)
        phi = gelu_parts(hidden)
        act = hidden * phi
        slope = phi + hidden * (jnp.exp(-0.5 * hidden * hidden) * 0.3989422804014327)
        d_pre = nt(d_ff, down[...]) * slope
        d_normed = nn(d_pre, up[...])
        unit3, scale = normalize(value[here])
        unit = unit3.reshape(BLOCK, LANES)
        gain = vec[MID_GAIN : MID_GAIN + 1, :LANES]
        normed = unit * gain + vec[MID_SHIFT : MID_SHIFT + 1, :LANES]
        grad = (d_normed * gain).reshape(mid.shape)
        d_out = mid + normalize_back(grad, unit3, scale)
        d_attn[here] = d_out
        d_proj = (mask * d_out).reshape(BLOCK, LANES)
        d_att[here] = nt(d_proj, proj[...]).reshape(mid.shape)
        d_ff_own, d_pre_own, d_normed_own = d_ff[part], d_pre[part], d_normed[part]
        g_down[:184] += nn(turn(d_ff_own), act[part])
        g_up[:184] += nn(turn(normed[part]), d_pre_own)
        g_vec[UP_BIAS : UP_BIAS + 1, :HID] += jnp.sum(d_pre_own, 0, keepdims=True)
        for at, v in (
            (MID_GAIN, d_normed_own * unit[part]),
            (MID_SHIFT, d_normed_own),
            (DOWN_BIAS, d_ff_own),
        ):
            g_vec[at : at + 1, :LANES] += jnp.sum(v, 0, keepdims=True)
        if counted:
            g_proj[:184] += nn(turn(d_proj), attended[here].reshape(BLOCK, LANES))
            g_vec[PROJ_BIAS : PROJ_BIAS + 1, :LANES] += jnp.sum(d_proj, 0, keepdims=True)

    block(0, None, slice(SHIFT * IMG, BLOCK), False)

    def inner(k, carry):
        block(k, None, slice(0, BLOCK), True)
        return carry

    lax.fori_loop(1, STEPS - 1, inner, 0)
    block(STEPS - 1, None, slice(0, SHIFT * IMG), True)
    for s in range(PARTS):
        rows = slice(FEED_ROWS * s, FEED_ROWS * s + FEED_ROWS)
        grads[s, :, :] = jnp.zeros_like(grads[s])
    turned_up = g_up[...].T
    turned_down = g_down[...].T
    for s in range(PARTS):
        rows = slice(FEED_ROWS * s, FEED_ROWS * s + FEED_ROWS)
        below = pltpu.roll(turned_down[rows], 64, 1)
        lanes = iota((FEED_ROWS, 128), 1)
        grads[s, :, :128] = turned_up[rows, :128]
        grads[s, :, 128:256] = jnp.where(lanes < 64, turned_up[rows, 128:], below[:, :128])
        grads[s, :, 256:] = below[:, 128:]


def attend_back_kernel(begin, end, scal, start, mixed, probs, d_att, *refs):
    refs = list(refs)
    first_call, last_call = begin == 0, end == STEPS
    if last_call:
        vec, qkv, vec_conv, vec_feed, feed, g_proj = refs[:6]
        d_mixed, keep, send, g_qkv, g_table, g_mixed, lines, proj_turned = refs[-8:]
    else:
        d_mixed, g_qkv, g_table, g_mixed = refs[-4:]
    before = refs[6 if last_call else 0 :][:3]
    for n, ref in enumerate((g_qkv, g_table, g_mixed)):
        ref[...] = jnp.zeros_like(ref) if first_call else before[n][...]

    def block(k, counted):
        here = block_of(mixed, k)
        att_here = block_of(d_att, k)
        out_here = block_of(d_mixed, k - begin)
        for pair in range(PAIRS):
            query = [q * HD**-0.5 for q in window_pair(here, pair, 0)]
            keys = window_pair(here, pair, LANES)
            values = window_pair(here, pair, 2 * LANES)
            d_rows = window_pair(att_here, pair, 0)
            prob = probs[k, pair]
            d_prob = head_products(values, d_rows).reshape(HEADS, 64, 128)
            prob3 = prob.reshape(HEADS, 64, 128)
            d_score = prob3 * (d_prob - jnp.sum(prob3 * d_prob, 1, keepdims=True))
            d_score = d_score.reshape(HEADS * 64, 128)
            if counted:
                g_table[...] += d_score
            prob_tiles = straight_tiles(prob)
            score_tiles = straight_tiles(d_score)
            turned = turned_tiles(d_score)
            for w in range(2):
                part = slice(64 * w, 64 * w + 64)
                d_query = mix(turned[w], keys[0][part], keys[1][part])
                put_window(out_here, pair, w, 0, [d * HD**-0.5 for d in d_query])
                put_window(
                    out_here, pair, w, LANES, mix(score_tiles[w], query[0][part], query[1][part])
                )
                put_window(
                    out_here,
                    pair,
                    w,
                    2 * LANES,
                    mix(prob_tiles[w], d_rows[0][part], d_rows[1][part]),
                )
        if counted:
            unit, _ = normalize(start[pl.ds(WIN * k, WIN)])
            d_all = out_here[...].reshape(BLOCK, 3 * LANES)
            g_qkv[:184] += nn(turn(unit.reshape(BLOCK, LANES)), d_all)
            g_mixed[0:1] += jnp.sum(d_all, 0, keepdims=True)

    if first_call:
        block(0, False)

    def inner(k, carry):
        block(k, True)
        return carry

    lax.fori_loop(max(begin, 1), end, inner, 0)
    if not last_call:
        return

    me = scal[2]
    sums = g_mixed[...]
    cross = g_qkv[...].T
    lines[...] = vec_conv[...] + vec_feed[...]
    lines[PRE_GAIN : PRE_GAIN + 1, :LANES] = jnp.sum(cross * qkv[...], 0, keepdims=True)
    lines[PRE_SHIFT : PRE_SHIFT + 1, :LANES] = nn(sums, qkv[...])[0:1]
    lines[QV_BIAS : QV_BIAS + 1] = sums[0:1]
    full = cross * vec[PRE_GAIN : PRE_GAIN + 1, :LANES] + sums.T[:, 0:1] * vec[
        PRE_SHIFT : PRE_SHIFT + 1, :LANES
    ]
    folded = g_table[...]
    lane, u = iota((128, LANES), 0) & 63, iota((128, LANES), 1)
    pick = (u == 112 - 15 * (lane >> 3) - (lane & 7)).astype(F32)
    spread = dot(folded, pick, 1, 0, HIGHEST).reshape(HEADS, WIN, WIN, LANES)
    rel = []
    for h in range(HEADS):
        line = jnp.zeros((WIN, LANES), F32)
        for y in range(WIN):
            line = line + pltpu.roll(spread[h, y], 15 * y, 1, stride=1, stride_axis=0)
        rel.append(jnp.sum(line, 0, keepdims=True))
    rel = jnp.concatenate(rel + [jnp.zeros((REL_ROWS - HEADS, LANES), F32)], 0)
    share = CHANS // PARTS
    value = lines[...]
    proj_turned[...] = g_proj[...].T
    lanes = iota((PROJ_ROWS, 128), 1)
    row = iota((VEC_ROWS, LANES), 0)
    for s in range(PARTS):
        put = functools.partial(put_part, keep, send, s, me)
        ours = proj_turned[PROJ_ROWS * s : PROJ_ROWS * s + PROJ_ROWS]
        for m in range(3):
            at = s * 3 + m
            at = (at // 4) * LANES + (at % 4) * 48
            put(slice(48 * m, 48 * m + 48), full[at : at + 48, :128])
            piece = pltpu.roll(ours, (64 - 60 * m) % LANES, 1)[:, :128]
            put(
                slice(QKV_ROWS + 48 * m, QKV_ROWS + 48 * m + 48),
                jnp.where(lanes < 64, full[at : at + 48, 128:], piece),
            )
        for m in range(3):
            at = FEED_AT + FEED_ROWS * m
            put(slice(at, at + FEED_ROWS), feed[s, :, 128 * m : 128 * m + 128])

        def back(amount):
            return pltpu.roll(value, (3 * LANES - amount) % (3 * LANES), 1)[:, :LANES]

        vectors = jnp.where(
            row < QV_BIAS,
            back(share * s),
            jnp.where(row == QV_BIAS, back((s // 2) * 2 * LANES + (s % 2) * 96), back(96 * s)),
        )
        for m in range(2):
            tile = slice(128 * m, 128 * m + 128)
            at = VEC_AT + VEC_ROWS * m
            put(slice(at, at + VEC_ROWS), vectors[:, tile])
            at = REL_AT + REL_ROWS * m
            put(slice(at, at + REL_ROWS), rel[:, tile])


def image_back_kernel(parts, scal, *refs):
    d_mixed = refs[:parts]
    start, d_attn, cot, qkv, vec = refs[parts : parts + 5]
    out, padded = refs[-2:]
    size = scal[0]
    padded[...] = jnp.zeros_like(padded)
    per = STEPS * WIN // parts
    for k in range(STEPS - 1):
        pieces = []
        for row in (WIN * k + SHIFT, WIN * k + WIN):
            pieces.append(d_mixed[row // per][row % per : row % per + SHIFT])
        here = slice(WIN * k + SHIFT, WIN * k + SHIFT + WIN)
        own = slice(WIN * k, WIN * k + WIN)
        unit3, scale = normalize(start[here])
        d_all = jnp.concatenate(pieces, 0).reshape(BLOCK, 3 * LANES)
        d_normed = nn(d_all, qkv[...])
        grad = (d_normed * vec[PRE_GAIN : PRE_GAIN + 1, :LANES]).reshape(unit3.shape)
        value = d_attn[here] + normalize_back(grad, unit3, scale)
        padded[:, :, :CHANS] = cot[own]
        mask = plain_mask(size, wrapped(scal[1] + SHIFT) + WIN * k, WIN)
        out[own] = (mask * (padded[...] + pltpu.roll(value, SHIFT, 1)))[:, :, :CHANS]


def call(kernel, scal, ins, outs, scratch=(), after=(), limit=16, flops=0):
    vmem = pl.BlockSpec(memory_space=pltpu.VMEM)
    specs = [vmem] * len(ins) + [pl.BlockSpec(memory_space=pl.ANY)] * len(after)
    first = [] if scal is None else [scal]
    if first:
        specs = [pl.BlockSpec(memory_space=pltpu.SMEM)] + specs
    size = sum(4 * a.size for a in ins)
    size += sum(4 * functools.reduce(lambda p, q: p * q, s) for s in outs)
    return pl.pallas_call(
        kernel,
        in_specs=specs,
        out_specs=[vmem] * len(outs),
        scratch_shapes=[pltpu.VMEM(s, F32) for s in scratch],
        out_shape=[jax.ShapeDtypeStruct(tuple(s), F32) for s in outs],
        compiler_params=pltpu.CompilerParams(vmem_limit_bytes=limit * MIB),
        cost_estimate=pl.CostEstimate(flops=flops, bytes_accessed=size, transcendentals=0),
    )(*first, *ins, *after)


def close_halves(value):
    n = value.shape[0] // (HALF + 1)
    return value.reshape(n, HALF + 1, -1)[:, :HALF].reshape(n * HALF, -1)


def body(
    images,
    item_sizes,
    cotangent,
    pre_gain,
    pre_shift,
    qkv_weight,
    qv_bias,
    rel_table,
    proj_weight,
    proj_bias,
    mid_gain,
    mid_shift,
    up_weight,
    up_bias,
    down_weight,
    down_bias,
    conv_kernel,
    conv_bias,
):
    height, breadth = images.shape[1:3]
    me = lax.axis_index("tp")
    strip = height + 2 * SHIFT
    image, cot = images[0], cotangent[0]
    share = CHANS // PARTS

    def frame(lanes):
        return (strip, breadth, lanes)

    flat = jnp.concatenate(
        [pre_gain, pre_shift, proj_bias, mid_gain, mid_shift, down_bias, conv_bias, qv_bias, up_bias]
    )[None]
    mine1, mine2 = call(
        pack_kernel,
        None,
        [qkv_weight.T, proj_weight, up_weight, down_weight.T, flat],
        [(QKV_ROWS + PROJ_ROWS + VEC_ROWS, LANES), (2 * FEED_ROWS, LANES)],
        [(WIN, 512)],
        limit=8,
    )
    mine3 = conv_kernel.transpose(0, 1, 3, 2).reshape(9, share, CHANS)
    scal = jnp.stack([item_sizes[0], (me * height + IMG - SHIFT) % IMG, me]).astype(jnp.int32)
    all1 = gather_tp(mine1)
    x_above = from_behind(image[-SHIFT:], "tp", 1)
    x_below = from_behind(image[:SHIFT], "tp", -1)
    all2 = gather_tp(mine2)
    all3 = gather_tp(mine3)
    c_above = from_behind(cot[-SHIFT - 1 :], "tp", 1)
    c_below = from_behind(cot[: SHIFT + 1], "tp", -1)

    qkv, proj, vec, table = call(
        prepare_kernel,
        scal,
        [*all1, rel_table.T],
        [(3 * LANES, LANES), (LANES, LANES), (VEC_ROWS, 3 * LANES), (HEADS * 64, 128)],
        [(VEC_ROWS, 3 * LANES)],
        limit=8,
        flops=10**8,
    )
    mixed, probs, attended, after_attn, start = call(
        attend_kernel,
        scal,
        [x_above, image, x_below, qkv, vec, table, proj],
        [frame(3 * LANES), (STEPS, PAIRS, HEADS * 64, 128), frame(LANES), frame(LANES), frame(LANES)],
        flops=10**10,
        limit=16,
    )
    pre, after_mlp, up, down = call(
        feed_kernel,
        scal,
        [after_attn, vec, *all2],
        [frame(HID), frame(LANES), (HID, LANES), (HID, LANES)],
        flops=5 * 10**9,
    )
    d_mid, conv_keep, conv_send, vec_conv, wide = call(
        conv_back_kernel,
        scal,
        [after_mlp, cot, c_above, c_below, *all3],
        [frame(LANES), (2, 9 * CONV_ROWS, LANES), (2, 9 * CONV_ROWS, LANES), (VEC_ROWS, 3 * LANES), (3, LANES, 3 * LANES)],
        [
            (strip + 2, breadth, 3 * LANES),
            (3, 3 * LANES, LANES),
            (PARTS, 9, share, CHANS),
            (1, breadth, LANES),
            (3, LANES, 3 * LANES),
        ],
        flops=2 * 10**10,
        limit=32,
    )
    got_a = lax.ppermute(conv_send, "tp", flip("tp", 1))
    d_attn, d_att, g_feed, g_proj, vec_feed = call(
        feed_back_kernel,
        scal,
        [d_mid, after_attn, pre, attended, up, down, proj, vec],
        [frame(LANES), frame(LANES), (PARTS, FEED_ROWS, HID), (LANES, LANES), (VEC_ROWS, 3 * LANES)],
        [(LANES, HID), (LANES, HID)],
        after=[conv_send],
        flops=10**10,
    )
    got_a = tie(got_a, d_att)
    send_b = conv_keep[1] + got_a[1]
    got_b = lax.ppermute(send_b, "tp", flip("tp", 2))

    g_shapes = [(LANES, 3 * LANES), (HEADS * 64, 128), (8, 3 * LANES)]

    def attend_back(begin, end, old, after):
        ins = [start, mixed, probs, d_att]
        outs = [((end - begin) * WIN, breadth, 3 * LANES)]
        scratch = []
        if end == STEPS:
            ins += [vec, qkv, vec_conv, vec_feed, g_feed, g_proj]
            outs += [(2, TAIL_ROWS, 128)] * 2
            scratch = g_shapes + [(VEC_ROWS, 3 * LANES), (LANES, LANES)]
        else:
            outs += g_shapes
        return call(
            functools.partial(attend_back_kernel, begin, end),
            scal,
            ins + list(old),
            outs,
            scratch,
            after=after,
            flops=5 * 10**9 * (end - begin),
        )

    d_mixed0, *sums = attend_back(0, 2, [], [send_b])
    got_b = tie(got_b, d_mixed0)
    held = conv_keep[0] + got_a[0] + got_b
    bits = dp_bits()
    d_mixed1, tail_keep, tail_send = attend_back(2, STEPS, sums, [held])
    held = dp_halve(held, bits[0], d_mixed1)

    last_a = lax.ppermute(tail_send, "tp", flip("tp", 1))
    (grad_images,) = call(
        functools.partial(image_back_kernel, 2),
        scal,
        [d_mixed0, d_mixed1, start, d_attn, cot, qkv, vec],
        [image.shape],
        [(WIN, breadth, LANES)],
        after=[tail_send],
        flops=4 * 10**9,
    )
    last_a = tie(last_a, grad_images)
    last_send = tail_keep[1] + last_a[1]
    last_b = lax.ppermute(last_send, "tp", flip("tp", 2))
    (block_out,) = call(
        conv_kernel_body,
        scal,
        [after_mlp, image, wide, vec],
        [image.shape],
        [(height + 2, breadth, 3 * LANES), (WIN, breadth, LANES)],
        after=[last_send],
        flops=10**10,
        limit=24,
    )
    last_b = tie(last_b, block_out)
    last = tail_keep[0] + last_a[0] + last_b
    for bit in bits[1:]:
        held = dp_add(held, bit)
    last = dp_halve(last, bits[0])
    for bit in bits[1:]:
        last = dp_add(last, bit)
    held = dp_join(held, bits[0])
    last = dp_join(last, bits[0])

    conv = held.reshape(3, 3, CONV_ROWS, LANES)[:, :, :share, :CHANS]
    qkv_rows = jnp.concatenate([last[:QKV_ROWS], last[QKV_ROWS : 2 * QKV_ROWS]], 1)
    feed = jnp.concatenate(
        [last[FEED_AT + FEED_ROWS * m : FEED_AT + FEED_ROWS * (m + 1)] for m in range(3)], 1
    )
    vectors = jnp.concatenate(
        [last[VEC_AT + VEC_ROWS * m : VEC_AT + VEC_ROWS * (m + 1)] for m in range(2)], 1
    )
    rel = jnp.concatenate(
        [last[REL_AT + REL_ROWS * m : REL_AT + REL_ROWS * (m + 1)] for m in range(2)], 1
    )
    proj_rows = jnp.concatenate(
        [qkv_rows[48 * m : 48 * m + 48, INNER : INNER + 60] for m in range(3)], 1
    )

    def short_vector(at):
        return vectors[at, :share]

    return (
        block_out[None],
        grad_images[None],
        short_vector(PRE_GAIN),
        short_vector(PRE_SHIFT),
        close_halves(qkv_rows[:, :CHANS]).T,
        close_halves(vectors[QV_BIAS, :96][:, None])[:, 0],
        rel[:HEADS, :RPOS][:, ::-1].T,
        close_halves(proj_rows),
        short_vector(PROJ_BIAS),
        short_vector(MID_GAIN),
        short_vector(MID_SHIFT),
        feed[:90, :CHANS].T,
        vectors[UP_BIAS, :90],
        feed[:90, INNER : INNER + CHANS],
        short_vector(DOWN_BIAS),
        conv.transpose(0, 1, 3, 2),
        short_vector(CONV_BIAS),
    )


def solution(mesh):
    placed = (
        P("dp", "tp", None, None),
        P("dp"),
        P("dp", "tp", None, None),
        P("tp"),
        P("tp"),
        P(None, "tp"),
        P("tp"),
        P(),
        P("tp", None),
        P("tp"),
        P("tp"),
        P("tp"),
        P(None, "tp"),
        P("tp"),
        P("tp", None),
        P("tp"),
        P(None, None, None, "tp"),
        P("tp"),
    )
    return jax.shard_map(
        body,
        mesh=mesh,
        in_specs=placed,
        out_specs=(
            P("dp", "tp", None, None),
            P("dp", "tp", None, None),
            P("tp"),
            P("tp"),
            P(None, "tp"),
            P("tp"),
            P(),
            P("tp", None),
            P("tp"),
            P("tp"),
            P("tp"),
            P(None, "tp"),
            P("tp"),
            P("tp", None),
            P("tp"),
            P(None, None, None, "tp"),
            P("tp"),
        ),
        check_vma=False,
    )
```

```python
import functools

import jax
import jax.numpy as jnp
from jax import lax
from jax.experimental import pallas as pl
from jax.experimental.pallas import tpu as pltpu
from jax.sharding import PartitionSpec as P

WIN = 8
IMG = 96
SHIFT = 4
EPSILON = 1e-05
NEG_FILL = -1e30
CHANS = 180
HEADS = 6
HD = 30
HALF = 15
SLOT = 32
LANES = 256
INNER = 192
HID = 384
RPOS = 225
HIGH = lax.Precision.HIGH
HIGHEST = lax.Precision.HIGHEST
F32 = jnp.float32
BF16 = jnp.bfloat16
BLOCK = WIN * IMG
PAIRS = IMG // WIN // 2
PARTS = 4
MIB = 2**20
STEPS = 4

QKV_ROWS, PROJ_ROWS, VEC_ROWS = 144, 48, 16
FEED_ROWS = 96
CONV_ROWS = 48
REL_ROWS = 8
FEED_AT = 2 * QKV_ROWS
VEC_AT = FEED_AT + 3 * FEED_ROWS
REL_AT = VEC_AT + 2 * VEC_ROWS
TAIL_ROWS = REL_AT + 2 * REL_ROWS
PRE_GAIN, PRE_SHIFT, PROJ_BIAS, MID_GAIN, MID_SHIFT, DOWN_BIAS, CONV_BIAS, QV_BIAS, UP_BIAS = range(9)


def flip(axis, bit):
    return [(i, i ^ bit) for i in range(lax.axis_size(axis))]


def from_behind(block, axis, distance):
    n = lax.axis_size(axis)
    return lax.ppermute(block, axis, [((i - distance) % n, i) for i in range(n)])


def gather_tp(block):
    got = {0: block}
    for bit in (2, 1):
        got.update({k | bit: lax.ppermute(b, "tp", flip("tp", bit)) for k, b in list(got.items())})
    return [got[k] for k in range(PARTS)]


def tie(value, *others):
    return lax.optimization_barrier((value, others))[0]


def dp_bits():
    n = lax.axis_size("dp")
    return [1 << b for b in range(n.bit_length() - 1)]


def dp_halve(held, bit, *others):
    half = held.shape[0] // 2
    odd = (lax.axis_index("dp") & bit) != 0
    send = jnp.where(odd, held[:half], held[half:])
    got = lax.ppermute(send, "dp", flip("dp", bit))
    if others:
        got = tie(got, *others)
    return jnp.where(odd, held[half:], held[:half]) + got


def dp_join(held, bit):
    odd = (lax.axis_index("dp") & bit) != 0
    got = lax.ppermute(held, "dp", flip("dp", bit))
    return jnp.concatenate([jnp.where(odd, got, held), jnp.where(odd, held, got)], 0)


def dp_add(held, bit):
    return held + lax.ppermute(held, "dp", flip("dp", bit))


def dot(left, right, left_dim, right_dim, precision=None):
    return lax.dot_general(
        left,
        right,
        (((left_dim,), (right_dim,)), ((), ())),
        precision=precision,
        preferred_element_type=F32,
    )


def nn(left, right):
    return dot(left, right, 1, 0, HIGH)


def nt(left, right):
    return dot(left, right, 1, 1, HIGH)


def turn(value):
    return value.T[:184]


def iota(shape, dim):
    return lax.broadcasted_iota(jnp.int32, shape, dim)


def wrapped(position):
    return jnp.where(position >= IMG, position - IMG, position)


def frame_mask(size, first, rows=WIN):
    shape = (rows, IMG, LANES)
    row = wrapped(first + iota(shape, 0))
    col = wrapped(iota(shape, 1) + SHIFT)
    return ((row < size) & (col < size) & (iota(shape, 2) < CHANS)).astype(F32)


def plain_mask(size, first, rows):
    shape = (rows, IMG, LANES)
    row = wrapped(first + iota(shape, 0))
    return ((row < size) & (iota(shape, 1) < size) & (iota(shape, 2) < CHANS)).astype(F32)


def is_channel(shape):
    return iota(shape, len(shape) - 1) < CHANS


def mean(value):
    return jnp.sum(value, axis=-1, keepdims=True) * (1.0 / CHANS)


def normalize(value):
    centre = jnp.where(is_channel(value.shape), value - mean(value), 0.0)
    scale = lax.rsqrt(mean(centre * centre) + EPSILON)
    return centre * scale, scale


def normalize_back(grad, unit, scale):
    value = scale * (grad - mean(grad) - unit * mean(grad * unit))
    return jnp.where(is_channel(value.shape), value, 0.0)


def upper(value):
    return value.astype(BF16).astype(F32)


def parted(value):
    high = upper(value)
    return jnp.where(iota(value.shape, 1) < 64, high, value - high)


def doubled(first, second):
    left = iota(first.shape, 1) < 64
    turned0 = pltpu.roll(first, 64, 1)
    turned1 = pltpu.roll(second, 64, 1)
    return (
        jnp.where(left, first, turned0),
        jnp.where(left, turned0, first),
        jnp.where(left, second, turned1),
    )


def head_products(rows, cols):
    lanes = iota((128, 128), 1)
    even = (lanes & 63) < SLOT
    outs = []
    for moving, fixed in zip(doubled(*rows), doubled(*cols)):
        high = fixed.astype(BF16)
        low = (fixed - high.astype(F32)).astype(BF16)
        held = jnp.concatenate([high, low], 1)
        pieces = parted(moving)
        ones = jnp.where(even, pieces, 0.0).astype(BF16)
        twos = jnp.where(even, 0.0, pieces).astype(BF16)
        both = []
        for w in range(2):
            part = slice(64 * w, 64 * w + 64)
            stream = jnp.concatenate([ones[part], twos[part]], 0)
            both.append(dot(jnp.concatenate([stream, stream], 1), held, 1, 1))
        outs.append(jnp.where(lanes < 64, both[0], both[1]))
    return jnp.concatenate(outs, 0)


def mix(tiles, first, second):
    lanes = iota((64, 128), 1)

    def product(part, block):
        high = block.astype(BF16)
        low = (block - high.astype(F32)).astype(BF16)
        held = jnp.concatenate([high, high, low, low], 0)
        stream = jnp.concatenate(part, 0)
        return dot(jnp.concatenate([stream, stream], 1), held, 1, 0)

    a = product(tiles[:4], first)
    b = product(tiles[4:], second)
    one = jnp.where(
        lanes < 64,
        jnp.where(lanes < 32, a[0:64], a[64:128]),
        jnp.where(lanes < 96, a[128:192], a[192:256]),
    )
    two = jnp.where(lanes < 32, b[0:64], b[64:128])
    return one, two


def straight_tiles(table):
    left = iota(table.shape, 1) < 64
    turned = pltpu.roll(table, 64, 1)
    outs = []
    for w in range(2):
        one = jnp.where(left, table, turned) if w == 0 else jnp.where(left, turned, table)
        both = parted(one).astype(BF16)
        outs.append([both[64 * h : 64 * h + 64] for h in range(HEADS)])
    return outs


def turned_tiles(table):
    high = upper(table)
    low = table - high
    outs = [[], []]
    for h in range(HEADS):
        part = slice(64 * h, 64 * h + 64)
        both = jnp.concatenate([high[part], low[part]], 0).astype(BF16).T
        for w in range(2):
            outs[w].append(both[64 * w : 64 * w + 64])
    return outs


def window_pair(ref, pair, start):
    cols = pl.ds(pl.multiple_of(pair * 2 * WIN, 2 * WIN), 2 * WIN)
    tiles = []
    for tile in range(2):
        block = ref[:, cols, start + 128 * tile : start + 128 * tile + 128]
        tiles.append(
            jnp.concatenate(
                [block[:, :WIN].reshape(64, 128), block[:, WIN:].reshape(64, 128)], 0
            )
        )
    return tiles


def put_window(ref, pair, w, start, tiles):
    cols = pl.ds(pl.multiple_of(pair * 2 * WIN + w * WIN, WIN), WIN)
    for tile in range(2):
        ref[:, cols, start + 128 * tile : start + 128 * tile + 128] = tiles[tile].reshape(
            WIN, WIN, 128
        )


def pair_fill(size, first, pair):
    shape = (64, 128)
    j, lane = iota(shape, 0), iota(shape, 1)
    i, window = lane & 63, 2 * pair + (lane >> 6)
    rows = wrapped(first + (j >> 3))
    cols = wrapped(window * WIN + (j & 7) + SHIFT)
    apart_rows = (first == IMG - WIN + SHIFT) & ((j >> 5) != (i >> 5))
    apart_cols = (window == IMG // WIN - 1) & (((j & 7) >> 2) != ((i & 7) >> 2))
    keep = (rows < size) & (cols < size)
    return jnp.where(apart_rows | apart_cols | jnp.logical_not(keep), NEG_FILL, 0.0)


def block_first(scal, k):
    return wrapped(scal[1] + WIN * k)


def block_of(ref, k):
    return ref.at[pl.ds(WIN * k, WIN)]


def put_part(keep, send, part, me, rows, value):
    place = part ^ me

    @pl.when((place & 1) == 0)
    def _():
        keep[place >> 1, rows] = value

    @pl.when((place & 1) == 1)
    def _():
        send[place >> 1, rows] = value


def gelu_parts(hidden):
    return 0.5 * (1.0 + lax.erf(hidden * 0.5**0.5))


def pack_kernel(qkv, proj, up, down, flat, first, second, line):
    first[...] = jnp.zeros_like(first)
    second[...] = jnp.zeros_like(second)
    for n in range(9):
        first[16 * n : 16 * n + HALF, :CHANS] = qkv[HALF * n : HALF * n + HALF]
    for n in range(3):
        at = QKV_ROWS + 16 * n
        first[at : at + HALF, :CHANS] = proj[HALF * n : HALF * n + HALF]
    share, hid = CHANS // PARTS, up.shape[1]
    second[:hid, :CHANS] = up[...].T
    second[FEED_ROWS : FEED_ROWS + hid, :CHANS] = down[...].T
    line[...] = jnp.zeros_like(line)
    line[0:1, : flat.shape[1]] = flat[...]
    value = line[...]
    lanes = iota((WIN, LANES), 1)
    at = QKV_ROWS + PROJ_ROWS

    def taken(begin):
        return pltpu.roll(value, (512 - begin) % 512, 1)[:, :LANES]

    for n in range(7):
        first[at + n : at + n + 1] = jnp.where(lanes < share, taken(share * n), 0.0)[0:1]
    total = jnp.zeros((WIN, LANES), F32)
    for n in range(6):
        piece = pltpu.roll(value, (512 - 7 * share + n) % 512, 1)[:, :LANES]
        total = total + jnp.where((lanes >= 16 * n) & (lanes < 16 * n + HALF), piece, 0.0)
    first[at + QV_BIAS : at + QV_BIAS + 1] = total[0:1]
    first[at + UP_BIAS : at + UP_BIAS + 1] = jnp.where(lanes < hid, taken(7 * share + hid), 0.0)[0:1]


def prepare_kernel(scal, p0, p1, p2, p3, rel, qkv, proj, vec, table, spread):
    me = scal[2]
    for ref in (qkv, vec, spread):
        ref[...] = jnp.zeros_like(ref)
    proj[INNER:] = jnp.zeros_like(proj[INNER:])
    lanes = iota((VEC_ROWS, 3 * LANES), 1)
    row = iota((VEC_ROWS, 3 * LANES), 0)
    for k, piece in enumerate((p0, p1, p2, p3)):
        owner = me ^ k
        for m in range(3):
            at = owner * 3 + m
            start = pl.multiple_of((at // 4) * LANES + (at % 4) * 48, 16)
            qkv[pl.ds(start, 48)] = piece[48 * m : 48 * m + 48]
        proj[pl.ds(pl.multiple_of(owner * PROJ_ROWS, 16), PROJ_ROWS)] = piece[
            QKV_ROWS : QKV_ROWS + PROJ_ROWS
        ]
        spread[:VEC_ROWS, :LANES] = piece[QKV_ROWS + PROJ_ROWS :]
        value = spread[:VEC_ROWS]
        vec[...] += jnp.where(
            row < QV_BIAS,
            pltpu.roll(value, owner * (CHANS // PARTS), 1),
            jnp.where(
                row == QV_BIAS,
                pltpu.roll(value, (owner // 2) * 2 * LANES + (owner % 2) * 96, 1),
                pltpu.roll(value, owner * 96, 1),
            ),
        )
    spread[...] = jnp.zeros_like(spread)
    spread[:HEADS, :RPOS] = rel[...]
    pieces = []
    for h in range(HEADS):
        line = jnp.broadcast_to(spread[h : h + 1, :LANES], (WIN, LANES))
        for y in range(WIN):
            pieces.append(
                pltpu.roll(line, (15 * y - 112) % LANES, 1, stride=1, stride_axis=0)
            )
    lines = jnp.concatenate(pieces, 0)
    u, lane = iota((LANES, 128), 0), iota((LANES, 128), 1) & 63
    pick = (u == (lane >> 3) * 15 + (lane & 7)).astype(F32)
    table[...] = dot(lines, pick, 1, 0, HIGHEST)


def attend_kernel(edges, scal, *refs):
    m = pl.program_id(0)
    if edges:
        above, image, below, qkv, vec, table, proj = refs[:7]
        k = m * (STEPS - 1)
    else:
        image, qkv, vec, table, proj = refs[:5]
        k = m + 1
    mixed, probs, attended, after, start, wide = refs[-6:]
    height = image.shape[0]

    @pl.when(m == 0)
    def _():
        wide[...] = jnp.zeros_like(wide)
        if edges:
            wide[:SHIFT, :, :CHANS] = above[...]
            wide[SHIFT:, :, :CHANS] = image[:SHIFT]

    if edges:

        @pl.when(m == 1)
        def _():
            wide[:SHIFT, :, :CHANS] = image[height - SHIFT :]
            wide[SHIFT:, :, :CHANS] = below[...]

    else:
        wide[:, :, :CHANS] = image[pl.ds(WIN * k - SHIFT, WIN)]
    size, first = scal[0], block_first(scal, k)
    rows = pl.ds(WIN * k, WIN)
    mask = frame_mask(size, first)
    begin = mask * pltpu.roll(wide[...], IMG - SHIFT, 1)
    start[rows] = begin
    unit, _ = normalize(begin)
    normed = unit * vec[PRE_GAIN, :LANES] + vec[PRE_SHIFT, :LANES]
    mixed[...] = (
        nt(normed.reshape(BLOCK, LANES), qkv[...]) + vec[QV_BIAS : QV_BIAS + 1]
    ).reshape(WIN, IMG, 3 * LANES)
    out_here = block_of(attended, k)
    for pair in range(PAIRS):
        query = window_pair(mixed, pair, 0)
        keys = window_pair(mixed, pair, LANES)
        values = window_pair(mixed, pair, 2 * LANES)
        scores = head_products(keys, [q * HD**-0.5 for q in query]) + table[...]
        scores = scores.reshape(HEADS, 64, 128) + pair_fill(size, first, pair)[None]
        scores = jnp.exp(scores - jnp.max(scores, 1, keepdims=True))
        prob = (scores * (1.0 / jnp.sum(scores, 1, keepdims=True))).reshape(HEADS * 64, 128)
        probs[0, pair] = prob
        for w, tiles in enumerate(turned_tiles(prob)):
            part = slice(64 * w, 64 * w + 64)
            put_window(out_here, pair, w, 0, mix(tiles, values[0][part], values[1][part]))
    out = nn(out_here[...].reshape(BLOCK, LANES), proj[...]) + vec[PROJ_BIAS : PROJ_BIAS + 1, :LANES]
    after[rows] = begin + mask * out.reshape(WIN, IMG, LANES)


def feed_kernel(scal, value, vec, p0, p1, p2, p3, pre, after, up, down):
    for k, piece in enumerate((p0, p1, p2, p3)):
        rows = pl.ds(pl.multiple_of((scal[2] ^ k) * FEED_ROWS, 32), FEED_ROWS)
        up[rows] = piece[:FEED_ROWS]
        down[rows] = piece[FEED_ROWS:]

    def block(k, carry):
        rows = pl.ds(WIN * k, WIN)
        mask = frame_mask(scal[0], block_first(scal, k))
        here = value[rows]
        unit, _ = normalize(here)
        normed = unit * vec[MID_GAIN, :LANES] + vec[MID_SHIFT, :LANES]
        hidden = nt(normed.reshape(BLOCK, LANES), up[...]) + vec[UP_BIAS : UP_BIAS + 1, :HID]
        pre[rows] = hidden.reshape(WIN, IMG, HID)
        act = hidden * gelu_parts(hidden)
        out = nn(act, down[...]) + vec[DOWN_BIAS : DOWN_BIAS + 1, :LANES]
        after[rows] = here + mask * out.reshape(here.shape)
        return carry

    lax.fori_loop(0, STEPS, block, 0)


def put_shifted(ref, value):
    cols = iota(value.shape, 1)
    ref[:, :, LANES : 2 * LANES] = value
    ref[:, :, :LANES] = jnp.where(cols == 0, 0.0, pltpu.roll(value, 1, 1))
    ref[:, :, 2 * LANES :] = jnp.where(cols == IMG - 1, 0.0, pltpu.roll(value, IMG - 1, 1))


def conv_back_kernel(
    scal,
    after,
    cot,
    cot_above,
    cot_below,
    p0,
    p1,
    p2,
    p3,
    d_mid,
    keep,
    send,
    vec,
    wide,
    padded,
    d_spread,
    tall,
    gathered,
    grad,
):
    height = cot.shape[0]
    share = CHANS // PARTS
    size, base, me = scal[0], scal[1], scal[2]
    for ref in (wide, tall, padded, grad, vec):
        ref[...] = jnp.zeros_like(ref)
    for n, piece in enumerate((p0, p1, p2, p3)):
        gathered[me ^ n] = piece[...]
    for s in range(PARTS):
        rows = slice(share * s, share * s + share)
        for i in range(3):
            for j in range(3):
                part = gathered[s, 3 * i + j]
                wide[i, rows, LANES * j : LANES * j + CHANS] = part
                at = LANES * (2 - j) + share * s
                tall[i, at : at + share, :CHANS] = part
    edge = SHIFT + 1
    padded[:edge, :, :CHANS] = cot_above[...]
    padded[edge : edge + height, :, :CHANS] = cot[...]
    padded[edge + height :, :, :CHANS] = cot_below[...]
    shape = (WIN, IMG, LANES)

    def block(k, own):
        tall_shape = (WIN + 2, IMG, LANES)
        row = wrapped(wrapped(wrapped(base + IMG - 1 + WIN * k) + iota(tall_shape, 0)))
        inside = (row < size) & (iota(tall_shape, 1) < size)
        put_shifted(d_spread, jnp.where(inside, padded[pl.ds(WIN * k, WIN + 2)], 0.0))
        rows = wrapped(wrapped(base + WIN * k) + iota(shape, 0))
        rows_all = wrapped(wrapped(base + WIN * k) + iota((WIN, IMG, 3 * LANES), 0))
        total = jnp.zeros(shape, F32)
        here = pltpu.roll(after[pl.ds(WIN * k, WIN)], SHIFT, 1)[own]
        turned = turn(here.reshape(-1, LANES))
        for i in range(3):
            around = d_spread[2 - i : 2 - i + WIN]
            part = nn(around.reshape(BLOCK, 3 * LANES), tall[i]).reshape(shape)
            if i == 0:
                part = jnp.where(rows == IMG - 1, 0.0, part)
                around = jnp.where(rows_all == IMG - 1, 0.0, around)
            if i == 2:
                part = jnp.where(rows == 0, 0.0, part)
                around = jnp.where(rows_all == 0, 0.0, around)
            total = total + part
            grad[i, :184] += nn(turned, around[own].reshape(-1, 3 * LANES))
        d_mid[pl.ds(WIN * k, WIN)] = pltpu.roll(total, IMG - SHIFT, 1)
        centre = d_spread[1 : 1 + WIN, :, LANES : 2 * LANES][own]
        vec[CONV_BIAS : CONV_BIAS + 1, :LANES] += jnp.sum(
            centre.reshape(-1, LANES), 0, keepdims=True
        )

    block(0, slice(SHIFT, WIN))

    def inner(k, carry):
        block(k, slice(0, WIN))
        return carry

    lax.fori_loop(1, STEPS - 1, inner, 0)
    block(STEPS - 1, slice(0, SHIFT))
    for i in range(3):
        for j in range(3):
            at = CONV_ROWS * (3 * i + j)
            value = grad[i, :, LANES * (2 - j) : LANES * (3 - j)].T
            for s in range(PARTS):
                put_part(
                    keep, send, s, me, slice(at, at + share), value[share * s : share * s + share]
                )


def conv_kernel_body(scal, after, images, wide, vec, *refs):
    out, spread, padded = refs[-3:]
    height = images.shape[0]
    padded[...] = jnp.zeros_like(padded)
    tall_shape = (WIN + 2, IMG, LANES)

    def block(k, carry):
        own = pl.ds(WIN * k, WIN)
        first = wrapped(scal[1] + SHIFT) + WIN * k
        row = first - 1 + iota(tall_shape, 0)
        value = pltpu.roll(after[pl.ds(WIN * k + SHIFT - 1, WIN + 2)], SHIFT, 1)
        put_shifted(spread, jnp.where((row < 0) | (row >= IMG), 0.0, value))
        padded[:, :, :CHANS] = images[own]
        total = jnp.zeros((BLOCK, LANES), F32)
        for i in range(3):
            total = total + nt(spread[i : i + WIN].reshape(BLOCK, 3 * LANES), wide[i])
        mask = plain_mask(scal[0], first, WIN)
        conv = (total + vec[CONV_BIAS : CONV_BIAS + 1, :LANES]).reshape(mask.shape)
        out[own] = (mask * (padded[...] + conv))[:, :, :CHANS]
        return carry

    lax.fori_loop(0, height // WIN, block, 0)


def feed_back_kernel(
    scal, d_mid, value, pre, attended, up, down, proj, vec, *refs
):
    d_attn, d_att, grads, g_proj, g_vec, g_up, g_down = refs[-7:]
    for ref in (g_up, g_down, g_proj, g_vec):
        ref[...] = jnp.zeros_like(ref)
    size = scal[0]

    def block(k, rows, part, counted):
        here = pl.ds(WIN * k, WIN)
        mask = frame_mask(size, block_first(scal, k))
        mid = d_mid[here]
        d_ff = (mask * mid).reshape(BLOCK, LANES)
        hidden = pre[here].reshape(BLOCK, HID)
        phi = gelu_parts(hidden)
        act = hidden * phi
        slope = phi + hidden * (jnp.exp(-0.5 * hidden * hidden) * 0.3989422804014327)
        d_pre = nt(d_ff, down[...]) * slope
        d_normed = nn(d_pre, up[...])
        unit3, scale = normalize(value[here])
        unit = unit3.reshape(BLOCK, LANES)
        gain = vec[MID_GAIN : MID_GAIN + 1, :LANES]
        normed = unit * gain + vec[MID_SHIFT : MID_SHIFT + 1, :LANES]
        grad = (d_normed * gain).reshape(mid.shape)
        d_out = mid + normalize_back(grad, unit3, scale)
        d_attn[here] = d_out
        d_proj = (mask * d_out).reshape(BLOCK, LANES)
        d_att[here] = nt(d_proj, proj[...]).reshape(mid.shape)
        d_ff_own, d_pre_own, d_normed_own = d_ff[part], d_pre[part], d_normed[part]
        g_down[:184] += nn(turn(d_ff_own), act[part])
        g_up[:184] += nn(turn(normed[part]), d_pre_own)
        g_vec[UP_BIAS : UP_BIAS + 1, :HID] += jnp.sum(d_pre_own, 0, keepdims=True)
        for at, v in (
            (MID_GAIN, d_normed_own * unit[part]),
            (MID_SHIFT, d_normed_own),
            (DOWN_BIAS, d_ff_own),
        ):
            g_vec[at : at + 1, :LANES] += jnp.sum(v, 0, keepdims=True)
        if counted:
            g_proj[:184] += nn(turn(d_proj), attended[here].reshape(BLOCK, LANES))
            g_vec[PROJ_BIAS : PROJ_BIAS + 1, :LANES] += jnp.sum(d_proj, 0, keepdims=True)

    block(0, None, slice(SHIFT * IMG, BLOCK), False)

    def inner(k, carry):
        block(k, None, slice(0, BLOCK), True)
        return carry

    lax.fori_loop(1, STEPS - 1, inner, 0)
    block(STEPS - 1, None, slice(0, SHIFT * IMG), True)
    for s in range(PARTS):
        rows = slice(FEED_ROWS * s, FEED_ROWS * s + FEED_ROWS)
        grads[s, :, :] = jnp.zeros_like(grads[s])
    turned_up = g_up[...].T
    turned_down = g_down[...].T
    for s in range(PARTS):
        rows = slice(FEED_ROWS * s, FEED_ROWS * s + FEED_ROWS)
        below = pltpu.roll(turned_down[rows], 64, 1)
        lanes = iota((FEED_ROWS, 128), 1)
        grads[s, :, :128] = turned_up[rows, :128]
        grads[s, :, 128:256] = jnp.where(lanes < 64, turned_up[rows, 128:], below[:, :128])
        grads[s, :, 256:] = below[:, 128:]


def attend_back_kernel(begin, end, scal, start, mixed, probs, d_att, *refs):
    refs = list(refs)
    first_call, last_call = begin == 0, end == STEPS
    if last_call:
        vec, qkv, vec_conv, vec_feed, feed, g_proj = refs[:6]
        d_mixed, keep, send, g_qkv, g_table, g_mixed, lines, proj_turned = refs[-8:]
    else:
        d_mixed, g_qkv, g_table, g_mixed = refs[-4:]
    before = refs[6 if last_call else 0 :][:3]
    m = pl.program_id(0)
    k = m + begin

    @pl.when(m == 0)
    def _():
        for n, ref in enumerate((g_qkv, g_table, g_mixed)):
            ref[...] = jnp.zeros_like(ref) if first_call else before[n][...]

    counted = (k > 0).astype(F32)
    att_here = block_of(d_att, k)
    out_here = block_of(d_mixed, m)
    for pair in range(PAIRS):
        query = [q * HD**-0.5 for q in window_pair(mixed, pair, 0)]
        keys = window_pair(mixed, pair, LANES)
        values = window_pair(mixed, pair, 2 * LANES)
        d_rows = window_pair(att_here, pair, 0)
        prob = probs[0, pair]
        d_prob = head_products(values, d_rows).reshape(HEADS, 64, 128)
        prob3 = prob.reshape(HEADS, 64, 128)
        d_score = prob3 * (d_prob - jnp.sum(prob3 * d_prob, 1, keepdims=True))
        d_score = d_score.reshape(HEADS * 64, 128)
        g_table[...] += counted * d_score if first_call else d_score
        prob_tiles = straight_tiles(prob)
        score_tiles = straight_tiles(d_score)
        turned = turned_tiles(d_score)
        for w in range(2):
            part = slice(64 * w, 64 * w + 64)
            d_query = mix(turned[w], keys[0][part], keys[1][part])
            put_window(out_here, pair, w, 0, [d * HD**-0.5 for d in d_query])
            put_window(
                out_here, pair, w, LANES, mix(score_tiles[w], query[0][part], query[1][part])
            )
            put_window(
                out_here, pair, w, 2 * LANES, mix(prob_tiles[w], d_rows[0][part], d_rows[1][part])
            )

    def gather():
        unit, _ = normalize(start[pl.ds(WIN * k, WIN)])
        d_all = out_here[...].reshape(BLOCK, 3 * LANES)
        g_qkv[:184] += nn(turn(unit.reshape(BLOCK, LANES)), d_all)
        g_mixed[0:1] += jnp.sum(d_all, 0, keepdims=True)

    if first_call:
        pl.when(k > 0)(gather)
    else:
        gather()
    if last_call:

        @pl.when(m == pl.num_programs(0) - 1)
        def _():
            finish(
                scal[2], vec, qkv, vec_conv, vec_feed, feed, g_proj, keep, send, g_qkv, g_table,
                g_mixed, lines, proj_turned,
            )


def finish(
    me, vec, qkv, vec_conv, vec_feed, feed, g_proj, keep, send, g_qkv, g_table, g_mixed, lines,
    proj_turned,
):
    sums = g_mixed[...]
    cross = g_qkv[...].T
    lines[...] = vec_conv[...] + vec_feed[...]
    lines[PRE_GAIN : PRE_GAIN + 1, :LANES] = jnp.sum(cross * qkv[...], 0, keepdims=True)
    lines[PRE_SHIFT : PRE_SHIFT + 1, :LANES] = nn(sums, qkv[...])[0:1]
    lines[QV_BIAS : QV_BIAS + 1] = sums[0:1]
    full = cross * vec[PRE_GAIN : PRE_GAIN + 1, :LANES] + sums.T[:, 0:1] * vec[
        PRE_SHIFT : PRE_SHIFT + 1, :LANES
    ]
    folded = g_table[...]
    lane, u = iota((128, LANES), 0) & 63, iota((128, LANES), 1)
    pick = (u == 112 - 15 * (lane >> 3) - (lane & 7)).astype(F32)
    spread = dot(folded, pick, 1, 0, HIGHEST).reshape(HEADS, WIN, WIN, LANES)
    rel = []
    for h in range(HEADS):
        line = jnp.zeros((WIN, LANES), F32)
        for y in range(WIN):
            line = line + pltpu.roll(spread[h, y], 15 * y, 1, stride=1, stride_axis=0)
        rel.append(jnp.sum(line, 0, keepdims=True))
    rel = jnp.concatenate(rel + [jnp.zeros((REL_ROWS - HEADS, LANES), F32)], 0)
    share = CHANS // PARTS
    value = lines[...]
    proj_turned[...] = g_proj[...].T
    lanes = iota((PROJ_ROWS, 128), 1)
    row = iota((VEC_ROWS, LANES), 0)
    for s in range(PARTS):
        put = functools.partial(put_part, keep, send, s, me)
        ours = proj_turned[PROJ_ROWS * s : PROJ_ROWS * s + PROJ_ROWS]
        for m in range(3):
            at = s * 3 + m
            at = (at // 4) * LANES + (at % 4) * 48
            put(slice(48 * m, 48 * m + 48), full[at : at + 48, :128])
            piece = pltpu.roll(ours, (64 - 60 * m) % LANES, 1)[:, :128]
            put(
                slice(QKV_ROWS + 48 * m, QKV_ROWS + 48 * m + 48),
                jnp.where(lanes < 64, full[at : at + 48, 128:], piece),
            )
        for m in range(3):
            at = FEED_AT + FEED_ROWS * m
            put(slice(at, at + FEED_ROWS), feed[s, :, 128 * m : 128 * m + 128])

        def back(amount):
            return pltpu.roll(value, (3 * LANES - amount) % (3 * LANES), 1)[:, :LANES]

        vectors = jnp.where(
            row < QV_BIAS,
            back(share * s),
            jnp.where(row == QV_BIAS, back((s // 2) * 2 * LANES + (s % 2) * 96), back(96 * s)),
        )
        for m in range(2):
            tile = slice(128 * m, 128 * m + 128)
            at = VEC_AT + VEC_ROWS * m
            put(slice(at, at + VEC_ROWS), vectors[:, tile])
            at = REL_AT + REL_ROWS * m
            put(slice(at, at + REL_ROWS), rel[:, tile])


def image_back_kernel(parts, scal, *refs):
    d_mixed = refs[:parts]
    start, d_attn, cot, qkv, vec = refs[parts : parts + 5]
    out, padded = refs[-2:]
    size = scal[0]
    padded[...] = jnp.zeros_like(padded)
    per = STEPS * WIN // parts
    for k in range(STEPS - 1):
        pieces = []
        for row in (WIN * k + SHIFT, WIN * k + WIN):
            pieces.append(d_mixed[row // per][row % per : row % per + SHIFT])
        here = slice(WIN * k + SHIFT, WIN * k + SHIFT + WIN)
        own = slice(WIN * k, WIN * k + WIN)
        unit3, scale = normalize(start[here])
        d_all = jnp.concatenate(pieces, 0).reshape(BLOCK, 3 * LANES)
        d_normed = nn(d_all, qkv[...])
        grad = (d_normed * vec[PRE_GAIN : PRE_GAIN + 1, :LANES]).reshape(unit3.shape)
        value = d_attn[here] + normalize_back(grad, unit3, scale)
        padded[:, :, :CHANS] = cot[own]
        mask = plain_mask(size, wrapped(scal[1] + SHIFT) + WIN * k, WIN)
        out[own] = (mask * (padded[...] + pltpu.roll(value, SHIFT, 1)))[:, :, :CHANS]


def unpack_kernel(last, qkv, proj, up, down, rel, vectors):
    share = CHANS // PARTS
    for n in range(9):
        rows = slice(16 * n, 16 * n + HALF)
        qkv[HALF * n : HALF * n + HALF, :128] = last[rows]
        second = slice(QKV_ROWS + 16 * n, QKV_ROWS + 16 * n + HALF)
        qkv[HALF * n : HALF * n + HALF, 128:] = last[second][:, : CHANS - 128]
    pieces = [last[QKV_ROWS + 48 * m : QKV_ROWS + 48 * m + 48] for m in range(3)]
    pieces = [jnp.concatenate([p, jnp.zeros_like(p)], 1) for p in pieces]
    whole = [pltpu.roll(p, (60 * m - 64) % LANES, 1) for m, p in enumerate(pieces)]
    lanes = iota((PROJ_ROWS, LANES), 1)
    value = jnp.where(lanes < 60, whole[0], jnp.where(lanes < 120, whole[1], whole[2]))
    for n in range(3):
        proj[HALF * n : HALF * n + HALF] = value[16 * n : 16 * n + HALF, :CHANS]
    tiles = [last[FEED_AT + FEED_ROWS * m : FEED_AT + FEED_ROWS * (m + 1)] for m in range(3)]
    hid = up.shape[1]
    up[...] = jnp.concatenate(tiles[:2], 1).T[:CHANS, :hid]
    below = pltpu.roll(jnp.concatenate([tiles[1], tiles[2]], 1), LANES - 64, 1)
    down[...] = below.T[:CHANS, :hid]
    lines = jnp.concatenate([last[REL_AT : REL_AT + REL_ROWS], last[REL_AT + REL_ROWS :]], 1)
    a, b = iota((LANES, LANES), 0), iota((LANES, LANES), 1)
    rel[...] = dot(lines, (a + b == RPOS - 1).astype(F32), 1, 0, HIGHEST)[:HEADS, :RPOS]
    vectors[...] = last[VEC_AT : VEC_AT + VEC_ROWS]


def blocked(rows, place):
    def make(shape):
        rest = tuple(shape[1:])
        return pl.BlockSpec((rows,) + rest, lambda m: (place(m),) + (0,) * len(rest))

    return make


def resident(shape):
    return pl.BlockSpec(memory_space=pltpu.VMEM)


def untouched(shape):
    return pl.BlockSpec(memory_space=pl.ANY)


def call(kernel, scal, ins, outs, scratch=(), after=(), limit=10, flops=0, steps=None, keep=None):
    ins = [i if isinstance(i, tuple) else (i, resident) for i in ins]
    outs = [o if callable(o[-1]) else (o, resident) for o in outs]
    ins = [(a if f is resident else pltpu.with_memory_space_constraint(a, pltpu.HBM), f) for a, f in ins]
    ins += [(a, untouched) for a in after]
    first = [] if scal is None else [scal]
    specs = [pl.BlockSpec(memory_space=pltpu.SMEM)] * len(first) + [f(a.shape) for a, f in ins]
    size = sum(4 * a.size for a, f in ins if f is not untouched)
    size += sum(4 * functools.reduce(lambda p, q: p * q, s) for s, _ in outs)
    return pl.pallas_call(
        kernel,
        grid=() if steps is None else (steps,),
        in_specs=specs,
        out_specs=[f(s) for s, f in outs],
        scratch_shapes=[pltpu.VMEM(s, F32) for s in scratch],
        out_shape=[
            jax.ShapeDtypeStruct(tuple(s), F32) if f is resident else pltpu.HBM(tuple(s), F32)
            for s, f in outs
        ],
        input_output_aliases={i + len(first): o for i, o in (keep or {}).items()},
        compiler_params=pltpu.CompilerParams(vmem_limit_bytes=limit * MIB),
        cost_estimate=pl.CostEstimate(flops=flops, bytes_accessed=size, transcendentals=0),
    )(*first, *[a for a, _ in ins])


def close_halves(value):
    n = value.shape[0] // (HALF + 1)
    return value.reshape(n, HALF + 1, -1)[:, :HALF].reshape(n * HALF, -1)


def body(
    images,
    item_sizes,
    cotangent,
    pre_gain,
    pre_shift,
    qkv_weight,
    qv_bias,
    rel_table,
    proj_weight,
    proj_bias,
    mid_gain,
    mid_shift,
    up_weight,
    up_bias,
    down_weight,
    down_bias,
    conv_kernel,
    conv_bias,
):
    height, breadth = images.shape[1:3]
    me = lax.axis_index("tp")
    strip = height + 2 * SHIFT
    image, cot = images[0], cotangent[0]
    share = CHANS // PARTS

    def frame(lanes):
        return (strip, breadth, lanes)

    flat = jnp.concatenate(
        [pre_gain, pre_shift, proj_bias, mid_gain, mid_shift, down_bias, conv_bias, qv_bias, up_bias]
    )[None]
    at_once = lambda shape: pl.BlockSpec(tuple(shape), lambda m: (0,) * len(shape))
    mine1, mine2 = call(
        pack_kernel,
        None,
        [(a, at_once) for a in (qkv_weight.T, proj_weight, up_weight, down_weight.T, flat)],
        [(QKV_ROWS + PROJ_ROWS + VEC_ROWS, LANES), (2 * FEED_ROWS, LANES)],
        [(WIN, 512)],
        limit=8,
        steps=1,
    )
    mine3 = conv_kernel.transpose(0, 1, 3, 2).reshape(9, share, CHANS)
    scal = jnp.stack([item_sizes[0], (me * height + IMG - SHIFT) % IMG, me]).astype(jnp.int32)
    all1 = gather_tp(mine1)
    x_above = from_behind(image[-SHIFT:], "tp", 1)
    x_below = from_behind(image[:SHIFT], "tp", -1)
    all2 = gather_tp(mine2)
    all3 = gather_tp(mine3)
    c_above = from_behind(cot[-SHIFT - 1 :], "tp", 1)
    c_below = from_behind(cot[: SHIFT + 1], "tp", -1)

    qkv, proj, vec, table = call(
        prepare_kernel,
        scal,
        [*all1, rel_table.T],
        [(3 * LANES, LANES), (LANES, LANES), (VEC_ROWS, 3 * LANES), (HEADS * 64, 128)],
        [(VEC_ROWS, 3 * LANES)],
        limit=8,
        flops=10**8,
    )

    def attend(edges, arrays, old):
        place = (lambda m: m * (STEPS - 1)) if edges else (lambda m: m + 1)
        ins = [*arrays, qkv, vec, table, proj]
        keep = {len(ins) + n: n for n in range(len(old))}
        ins += [(o, untouched) for o in old[:2]] + list(old[2:])
        return call(
            functools.partial(attend_kernel, edges),
            scal,
            ins,
            [
                (frame(3 * LANES), blocked(WIN, place)),
                ((STEPS, PAIRS, HEADS * 64, 128), blocked(1, place)),
                frame(LANES),
                frame(LANES),
                frame(LANES),
            ],
            [(WIN, breadth, LANES)],
            flops=5 * 10**9,
            limit=16,
            steps=2,
            keep=keep,
        )

    old = attend(False, [image], [])
    mixed, probs, attended, after_attn, start = attend(True, [x_above, image, x_below], old)
    pre, after_mlp, up, down = call(
        feed_kernel,
        scal,
        [after_attn, vec, *all2],
        [frame(HID), frame(LANES), (HID, LANES), (HID, LANES)],
        flops=5 * 10**9,
    )
    d_mid, conv_keep, conv_send, vec_conv, wide = call(
        conv_back_kernel,
        scal,
        [after_mlp, cot, c_above, c_below, *all3],
        [frame(LANES), (2, 9 * CONV_ROWS, LANES), (2, 9 * CONV_ROWS, LANES), (VEC_ROWS, 3 * LANES), (3, LANES, 3 * LANES)],
        [
            (strip + 2, breadth, LANES),
            (WIN + 2, breadth, 3 * LANES),
            (3, 3 * LANES, LANES),
            (PARTS, 9, share, CHANS),
            (3, LANES, 3 * LANES),
        ],
        flops=2 * 10**10,
        limit=20,
    )
    got_a = lax.ppermute(conv_send, "tp", flip("tp", 1))
    d_attn, d_att, g_feed, g_proj, vec_feed = call(
        feed_back_kernel,
        scal,
        [d_mid, after_attn, pre, attended, up, down, proj, vec],
        [frame(LANES), frame(LANES), (PARTS, FEED_ROWS, HID), (LANES, LANES), (VEC_ROWS, 3 * LANES)],
        [(LANES, HID), (LANES, HID)],
        after=[conv_send],
        flops=10**10,
        limit=14,
    )
    got_a = tie(got_a, d_att)
    send_b = conv_keep[1] + got_a[1]
    got_b = lax.ppermute(send_b, "tp", flip("tp", 2))

    g_shapes = [(LANES, 3 * LANES), (HEADS * 64, 128), (8, 3 * LANES)]

    def attend_back(begin, end, old, after):
        place = lambda m: m + begin
        ins = [start, (mixed, blocked(WIN, place)), (probs, blocked(1, place)), d_att]
        outs = [((end - begin) * WIN, breadth, 3 * LANES)]
        scratch = []
        if end == STEPS:
            ins += [vec, qkv, vec_conv, vec_feed, g_feed, g_proj]
            outs += [(2, TAIL_ROWS, 128)] * 2
            scratch = g_shapes + [(VEC_ROWS, 3 * LANES), (LANES, LANES)]
        else:
            outs += g_shapes
        return call(
            functools.partial(attend_back_kernel, begin, end),
            scal,
            ins + list(old),
            outs,
            scratch,
            after=after,
            flops=5 * 10**9 * (end - begin),
            limit=16,
            steps=end - begin,
        )

    d_mixed0, *sums = attend_back(0, 2, [], [send_b])
    got_b = tie(got_b, d_mixed0)
    held = conv_keep[0] + got_a[0] + got_b
    bits = dp_bits()
    d_mixed1, tail_keep, tail_send = attend_back(2, STEPS, sums, [held])
    held = dp_halve(held, bits[0], d_mixed1)

    last_a = lax.ppermute(tail_send, "tp", flip("tp", 1))
    (grad_images,) = call(
        functools.partial(image_back_kernel, 2),
        scal,
        [d_mixed0, d_mixed1, start, d_attn, cot, qkv, vec],
        [image.shape],
        [(WIN, breadth, LANES)],
        after=[tail_send],
        flops=4 * 10**9,
    )
    last_a = tie(last_a, grad_images)
    last_send = tail_keep[1] + last_a[1]
    last_b = lax.ppermute(last_send, "tp", flip("tp", 2))
    (block_out,) = call(
        conv_kernel_body,
        scal,
        [after_mlp, image, wide, vec],
        [image.shape],
        [(WIN + 2, breadth, 3 * LANES), (WIN, breadth, LANES)],
        after=[last_send],
        flops=10**10,
    )
    last_b = tie(last_b, block_out)
    last = tail_keep[0] + last_a[0] + last_b
    for bit in bits[1:]:
        held = dp_add(held, bit)
    last = dp_halve(last, bits[0])
    for bit in bits[1:]:
        last = dp_add(last, bit)
    held = dp_join(held, bits[0])
    last = dp_join(last, bits[0])

    conv = held.reshape(3, 3, CONV_ROWS, LANES)[:, :, :share, :CHANS]
    hid = up_weight.shape[1]
    g_qkv, g_proj, g_up, g_down, g_rel, vectors = call(
        unpack_kernel,
        None,
        [last],
        [(qkv_weight.shape[1], CHANS), (share, CHANS), (CHANS, hid), (CHANS, hid), (HEADS, RPOS), (VEC_ROWS, 128)],
        limit=8,
    )

    def short_vector(at):
        return vectors[at, :share]

    return (
        block_out[None],
        grad_images[None],
        short_vector(PRE_GAIN),
        short_vector(PRE_SHIFT),
        g_qkv.T,
        close_halves(vectors[QV_BIAS, :96][:, None])[:, 0],
        g_rel.T,
        g_proj,
        short_vector(PROJ_BIAS),
        short_vector(MID_GAIN),
        short_vector(MID_SHIFT),
        g_up,
        vectors[UP_BIAS, :hid],
        g_down.T,
        short_vector(DOWN_BIAS),
        conv.transpose(0, 1, 3, 2),
        short_vector(CONV_BIAS),
    )


def solution(mesh):
    placed = (
        P("dp", "tp", None, None),
        P("dp"),
        P("dp", "tp", None, None),
        P("tp"),
        P("tp"),
        P(None, "tp"),
        P("tp"),
        P(),
        P("tp", None),
        P("tp"),
        P("tp"),
        P("tp"),
        P(None, "tp"),
        P("tp"),
        P("tp", None),
        P("tp"),
        P(None, None, None, "tp"),
        P("tp"),
    )
    return jax.shard_map(
        body,
        mesh=mesh,
        in_specs=placed,
        out_specs=(
            P("dp", "tp", None, None),
            P("dp", "tp", None, None),
            P("tp"),
            P("tp"),
            P(None, "tp"),
            P("tp"),
            P(),
            P("tp", None),
            P("tp"),
            P("tp"),
            P("tp"),
            P(None, "tp"),
            P("tp"),
            P("tp", None),
            P("tp"),
            P(None, None, None, "tp"),
            P("tp"),
        ),
        check_vma=False,
    )
```

```python
import functools

import jax
import jax.numpy as jnp
from jax import lax
from jax.experimental import pallas as pl
from jax.experimental.pallas import tpu as pltpu
from jax.sharding import PartitionSpec as P

WIN = 8
IMG = 96
SHIFT = 4
EPSILON = 1e-05
NEG_FILL = -1e30
CHANS = 180
HEADS = 6
HD = 30
HALF = 15
SLOT = 32
LANES = 256
INNER = 192
HID = 384
RPOS = 225
HIGH = lax.Precision.HIGH
HIGHEST = lax.Precision.HIGHEST
F32 = jnp.float32
BF16 = jnp.bfloat16
BLOCK = WIN * IMG
PAIRS = IMG // WIN // 2
PARTS = 4
MIB = 2**20
STEPS = 4

QKV_ROWS, PROJ_ROWS, VEC_ROWS = 144, 48, 16
FEED_ROWS = 96
CONV_ROWS = 48
REL_ROWS = 8
FEED_AT = 2 * QKV_ROWS
VEC_AT = FEED_AT + 3 * FEED_ROWS
REL_AT = VEC_AT + 2 * VEC_ROWS
TAIL_ROWS = REL_AT + 2 * REL_ROWS
PRE_GAIN, PRE_SHIFT, PROJ_BIAS, MID_GAIN, MID_SHIFT, DOWN_BIAS, CONV_BIAS, QV_BIAS, UP_BIAS = range(9)


def flip(axis, bit):
    return [(i, i ^ bit) for i in range(lax.axis_size(axis))]


def from_behind(block, axis, distance):
    n = lax.axis_size(axis)
    return lax.ppermute(block, axis, [((i - distance) % n, i) for i in range(n)])


def gather_tp(block, *others):
    got = {0: block}
    for bit in (2, 1):
        if others and bit == 1:
            got[2] = tie(got[2], *others)
        got.update({k | bit: lax.ppermute(b, "tp", flip("tp", bit)) for k, b in list(got.items())})
    return [got[k] for k in range(PARTS)]


def tie(value, *others):
    return lax.optimization_barrier((value, others))[0]


def dp_bits():
    n = lax.axis_size("dp")
    return [1 << b for b in range(n.bit_length() - 1)]


def dp_halve(held, bit, *others):
    half = held.shape[0] // 2
    odd = (lax.axis_index("dp") & bit) != 0
    send = jnp.where(odd, held[:half], held[half:])
    got = lax.ppermute(send, "dp", flip("dp", bit))
    if others:
        got = tie(got, *others)
    return jnp.where(odd, held[half:], held[:half]) + got


def dp_join(held, bit, *others):
    odd = (lax.axis_index("dp") & bit) != 0
    got = lax.ppermute(held, "dp", flip("dp", bit))
    if others:
        got = tie(got, *others)
    return jnp.concatenate([jnp.where(odd, got, held), jnp.where(odd, held, got)], 0)


def dp_add(held, bit, *others):
    got = lax.ppermute(held, "dp", flip("dp", bit))
    if others:
        got = tie(got, *others)
    return held + got


def dot(left, right, left_dim, right_dim, precision=None):
    return lax.dot_general(
        left,
        right,
        (((left_dim,), (right_dim,)), ((), ())),
        precision=precision,
        preferred_element_type=F32,
    )


def nn(left, right):
    return dot(left, right, 1, 0, HIGH)


def nt(left, right):
    return dot(left, right, 1, 1, HIGH)


def turn(value):
    return value.T[:184]


def iota(shape, dim):
    return lax.broadcasted_iota(jnp.int32, shape, dim)


def wrapped(position):
    return jnp.where(position >= IMG, position - IMG, position)


def frame_mask(size, first, rows=WIN):
    shape = (rows, IMG, LANES)
    row = wrapped(first + iota(shape, 0))
    col = wrapped(iota(shape, 1) + SHIFT)
    return ((row < size) & (col < size) & (iota(shape, 2) < CHANS)).astype(F32)


def plain_mask(size, first, rows):
    shape = (rows, IMG, LANES)
    row = wrapped(first + iota(shape, 0))
    return ((row < size) & (iota(shape, 1) < size) & (iota(shape, 2) < CHANS)).astype(F32)


def is_channel(shape):
    return iota(shape, len(shape) - 1) < CHANS


def mean(value):
    return jnp.sum(value, axis=-1, keepdims=True) * (1.0 / CHANS)


def normalize(value):
    centre = jnp.where(is_channel(value.shape), value - mean(value), 0.0)
    scale = lax.rsqrt(mean(centre * centre) + EPSILON)
    return centre * scale, scale


def normalize_back(grad, unit, scale):
    value = scale * (grad - mean(grad) - unit * mean(grad * unit))
    return jnp.where(is_channel(value.shape), value, 0.0)


def upper(value):
    return value.astype(BF16).astype(F32)


def parted(value):
    high = upper(value)
    return jnp.where(iota(value.shape, 1) < 64, high, value - high)


def doubled(first, second):
    left = iota(first.shape, 1) < 64
    turned0 = pltpu.roll(first, 64, 1)
    turned1 = pltpu.roll(second, 64, 1)
    return (
        jnp.where(left, first, turned0),
        jnp.where(left, turned0, first),
        jnp.where(left, second, turned1),
    )


def head_products(rows, cols):
    lanes = iota((128, 128), 1)
    even = (lanes & 63) < SLOT
    outs = []
    for moving, fixed in zip(doubled(*rows), doubled(*cols)):
        high = fixed.astype(BF16)
        low = (fixed - high.astype(F32)).astype(BF16)
        held = jnp.concatenate([high, low], 1)
        pieces = parted(moving)
        ones = jnp.where(even, pieces, 0.0).astype(BF16)
        twos = jnp.where(even, 0.0, pieces).astype(BF16)
        both = []
        for w in range(2):
            part = slice(64 * w, 64 * w + 64)
            stream = jnp.concatenate([ones[part], twos[part]], 0)
            both.append(dot(jnp.concatenate([stream, stream], 1), held, 1, 1))
        outs.append(jnp.where(lanes < 64, both[0], both[1]))
    return jnp.concatenate(outs, 0)


def mix(tiles, first, second):
    lanes = iota((64, 128), 1)

    def product(part, block):
        high = block.astype(BF16)
        low = (block - high.astype(F32)).astype(BF16)
        held = jnp.concatenate([high, high, low, low], 0)
        stream = jnp.concatenate(part, 0)
        return dot(jnp.concatenate([stream, stream], 1), held, 1, 0)

    a = product(tiles[:4], first)
    b = product(tiles[4:], second)
    one = jnp.where(
        lanes < 64,
        jnp.where(lanes < 32, a[0:64], a[64:128]),
        jnp.where(lanes < 96, a[128:192], a[192:256]),
    )
    two = jnp.where(lanes < 32, b[0:64], b[64:128])
    return one, two


def straight_tiles(table):
    left = iota(table.shape, 1) < 64
    turned = pltpu.roll(table, 64, 1)
    outs = []
    for w in range(2):
        one = jnp.where(left, table, turned) if w == 0 else jnp.where(left, turned, table)
        both = parted(one).astype(BF16)
        outs.append([both[64 * h : 64 * h + 64] for h in range(HEADS)])
    return outs


def turned_tiles(table):
    high = upper(table)
    low = table - high
    outs = [[], []]
    for h in range(HEADS):
        part = slice(64 * h, 64 * h + 64)
        both = jnp.concatenate([high[part], low[part]], 0).astype(BF16).T
        for w in range(2):
            outs[w].append(both[64 * w : 64 * w + 64])
    return outs


def window_pair(ref, pair, start):
    cols = pl.ds(pl.multiple_of(pair * 2 * WIN, 2 * WIN), 2 * WIN)
    tiles = []
    for tile in range(2):
        block = ref[:, cols, start + 128 * tile : start + 128 * tile + 128]
        tiles.append(
            jnp.concatenate(
                [block[:, :WIN].reshape(64, 128), block[:, WIN:].reshape(64, 128)], 0
            )
        )
    return tiles


def put_window(ref, pair, w, start, tiles):
    cols = pl.ds(pl.multiple_of(pair * 2 * WIN + w * WIN, WIN), WIN)
    for tile in range(2):
        ref[:, cols, start + 128 * tile : start + 128 * tile + 128] = tiles[tile].reshape(
            WIN, WIN, 128
        )


def pair_fill(size, first, pair):
    shape = (64, 128)
    j, lane = iota(shape, 0), iota(shape, 1)
    i, window = lane & 63, 2 * pair + (lane >> 6)
    rows = wrapped(first + (j >> 3))
    cols = wrapped(window * WIN + (j & 7) + SHIFT)
    apart_rows = (first == IMG - WIN + SHIFT) & ((j >> 5) != (i >> 5))
    apart_cols = (window == IMG // WIN - 1) & (((j & 7) >> 2) != ((i & 7) >> 2))
    keep = (rows < size) & (cols < size)
    return jnp.where(apart_rows | apart_cols | jnp.logical_not(keep), NEG_FILL, 0.0)


def block_first(scal, k):
    return wrapped(scal[1] + WIN * k)


def block_of(ref, k):
    return ref.at[pl.ds(WIN * k, WIN)]


def put_part(keep, send, part, me, store):
    place = part ^ me
    pl.when((place & 1) == 0)(lambda: store(keep.at[place >> 1]))
    pl.when((place & 1) == 1)(lambda: store(send.at[place >> 1]))


def gelu_parts(hidden):
    return 0.5 * (1.0 + lax.erf(hidden * 0.5**0.5))


def pack_kernel(qkv, proj, up, down, *refs):
    vectors, (first, second) = refs[:9], refs[9:]
    first[...] = jnp.zeros_like(first)
    second[...] = jnp.zeros_like(second)
    for n in range(9):
        first[16 * n : 16 * n + HALF, :CHANS] = qkv[HALF * n : HALF * n + HALF]
    for n in range(3):
        at = QKV_ROWS + 16 * n
        first[at : at + HALF, :CHANS] = proj[HALF * n : HALF * n + HALF]
    share, hid = CHANS // PARTS, up.shape[1]
    second[:hid, :CHANS] = up[...].T
    second[FEED_ROWS : FEED_ROWS + hid, :CHANS] = down[...].T
    at = QKV_ROWS + PROJ_ROWS
    for n, ref in enumerate(vectors):
        if n != QV_BIAS:
            first[at + n : at + n + 1, : ref.shape[1]] = ref[...]
    for n in range(6):
        first[at + QV_BIAS : at + QV_BIAS + 1, 16 * n : 16 * n + HALF] = vectors[QV_BIAS][
            :, HALF * n : HALF * n + HALF
        ]


def rims_kernel(cot, *refs):
    first, last = refs[-2:]
    height, n = cot.shape[1], first.shape[0]
    for row in range(n):
        first[row] = cot[:, row, :].T
        last[row] = cot[:, height - n + row, :].T


def prepare_kernel(scal, p0, p1, p2, p3, rel, qkv, proj, vec, table, spread):
    me = scal[2]
    for ref in (qkv, vec, spread):
        ref[...] = jnp.zeros_like(ref)
    proj[INNER:] = jnp.zeros_like(proj[INNER:])
    lanes = iota((VEC_ROWS, 3 * LANES), 1)
    row = iota((VEC_ROWS, 3 * LANES), 0)
    for k, piece in enumerate((p0, p1, p2, p3)):
        owner = me ^ k
        for m in range(3):
            at = owner * 3 + m
            start = pl.multiple_of((at // 4) * LANES + (at % 4) * 48, 16)
            qkv[pl.ds(start, 48)] = piece[48 * m : 48 * m + 48]
        proj[pl.ds(pl.multiple_of(owner * PROJ_ROWS, 16), PROJ_ROWS)] = piece[
            QKV_ROWS : QKV_ROWS + PROJ_ROWS
        ]
        spread[:VEC_ROWS, :LANES] = piece[QKV_ROWS + PROJ_ROWS :]
        value = spread[:VEC_ROWS]
        vec[...] += jnp.where(
            row < QV_BIAS,
            pltpu.roll(value, owner * (CHANS // PARTS), 1),
            jnp.where(
                row == QV_BIAS,
                pltpu.roll(value, (owner // 2) * 2 * LANES + (owner % 2) * 96, 1),
                pltpu.roll(value, owner * 96, 1),
            ),
        )
    spread[...] = jnp.zeros_like(spread)
    spread[:HEADS, :RPOS] = rel[...]
    pieces = []
    for h in range(HEADS):
        line = jnp.broadcast_to(spread[h : h + 1, :LANES], (WIN, LANES))
        for y in range(WIN):
            pieces.append(
                pltpu.roll(line, (15 * y - 112) % LANES, 1, stride=1, stride_axis=0)
            )
    lines = jnp.concatenate(pieces, 0)
    u, lane = iota((LANES, 128), 0), iota((LANES, 128), 1) & 63
    pick = (u == (lane >> 3) * 15 + (lane & 7)).astype(F32)
    table[...] = dot(lines, pick, 1, 0, HIGHEST)


def attend_kernel(edges, scal, *refs):
    m = pl.program_id(0)
    if edges:
        above, image, below, qkv, vec, table, proj = refs[:7]
        k = m * (STEPS - 1)
    else:
        image, qkv, vec, table, proj = refs[:5]
        k = m + 1
    mixed, probs, attended, after, start, wide = refs[-6:]
    height = image.shape[0]

    @pl.when(m == 0)
    def _():
        wide[...] = jnp.zeros_like(wide)
        if edges:
            wide[:SHIFT, :, :CHANS] = above[...]
            wide[SHIFT:, :, :CHANS] = image[:SHIFT]

    if edges:

        @pl.when(m == 1)
        def _():
            wide[:SHIFT, :, :CHANS] = image[height - SHIFT :]
            wide[SHIFT:, :, :CHANS] = below[...]

    else:
        wide[:, :, :CHANS] = image[pl.ds(WIN * k - SHIFT, WIN)]
    size, first = scal[0], block_first(scal, k)
    rows = pl.ds(WIN * k, WIN)
    mask = frame_mask(size, first)
    begin = mask * pltpu.roll(wide[...], IMG - SHIFT, 1)
    start[rows] = begin
    unit, _ = normalize(begin)
    normed = unit * vec[PRE_GAIN, :LANES] + vec[PRE_SHIFT, :LANES]
    mixed[...] = (
        nt(normed.reshape(BLOCK, LANES), qkv[...]) + vec[QV_BIAS : QV_BIAS + 1]
    ).reshape(WIN, IMG, 3 * LANES)
    out_here = block_of(attended, k)
    for pair in range(PAIRS):
        query = window_pair(mixed, pair, 0)
        keys = window_pair(mixed, pair, LANES)
        values = window_pair(mixed, pair, 2 * LANES)
        scores = head_products(keys, [q * HD**-0.5 for q in query]) + table[...]
        scores = scores.reshape(HEADS, 64, 128) + pair_fill(size, first, pair)[None]
        scores = jnp.exp(scores - jnp.max(scores, 1, keepdims=True))
        prob = (scores * (1.0 / jnp.sum(scores, 1, keepdims=True))).reshape(HEADS * 64, 128)
        probs[0, pair] = prob
        for w, tiles in enumerate(turned_tiles(prob)):
            part = slice(64 * w, 64 * w + 64)
            put_window(out_here, pair, w, 0, mix(tiles, values[0][part], values[1][part]))
    out = nn(out_here[...].reshape(BLOCK, LANES), proj[...]) + vec[PROJ_BIAS : PROJ_BIAS + 1, :LANES]
    after[rows] = begin + mask * out.reshape(WIN, IMG, LANES)


def feed_kernel(scal, value, vec, p0, p1, p2, p3, pre, after, up, down):
    for k, piece in enumerate((p0, p1, p2, p3)):
        rows = pl.ds(pl.multiple_of((scal[2] ^ k) * FEED_ROWS, 32), FEED_ROWS)
        up[rows] = piece[:FEED_ROWS]
        down[rows] = piece[FEED_ROWS:]

    def block(k, carry):
        rows = pl.ds(WIN * k, WIN)
        mask = frame_mask(scal[0], block_first(scal, k))
        here = value[rows]
        unit, _ = normalize(here)
        normed = unit * vec[MID_GAIN, :LANES] + vec[MID_SHIFT, :LANES]
        hidden = nt(normed.reshape(BLOCK, LANES), up[...]) + vec[UP_BIAS : UP_BIAS + 1, :HID]
        pre[rows] = hidden.reshape(WIN, IMG, HID)
        act = hidden * gelu_parts(hidden)
        out = nn(act, down[...]) + vec[DOWN_BIAS : DOWN_BIAS + 1, :LANES]
        after[rows] = here + mask * out.reshape(here.shape)
        return carry

    lax.fori_loop(0, STEPS, block, 0)


def put_shifted(ref, value):
    cols = iota(value.shape, 1)
    ref[:, :, LANES : 2 * LANES] = value
    ref[:, :, :LANES] = jnp.where(cols == 0, 0.0, pltpu.roll(value, 1, 1))
    ref[:, :, 2 * LANES :] = jnp.where(cols == IMG - 1, 0.0, pltpu.roll(value, IMG - 1, 1))


def conv_back_kernel(
    scal,
    after,
    cot,
    cot_above,
    cot_below,
    p0,
    p1,
    p2,
    p3,
    d_mid,
    keep,
    send,
    vec,
    wide,
    padded,
    d_spread,
    tall,
    gathered,
    grad,
    taps,
):
    height = cot.shape[1]
    share = CHANS // PARTS
    size, base, me = scal[0], scal[1], scal[2]
    for ref in (wide, tall, padded, grad, vec):
        ref[...] = jnp.zeros_like(ref)
    for n, piece in enumerate((p0, p1, p2, p3)):
        gathered[me ^ n] = piece[...]
    for s in range(PARTS):
        rows = slice(share * s, share * s + share)
        for i in range(3):
            for j in range(3):
                part = gathered[s, 3 * i + j]
                wide[i, rows, LANES * j : LANES * j + CHANS] = part
                at = LANES * (2 - j) + share * s
                tall[i, at : at + share, :CHANS] = part
    edge = SHIFT + 1
    padded[:edge, :, :CHANS] = cot_above[...]
    for row in range(height):
        padded[edge + row, :, :CHANS] = cot[:, row, :].T
    padded[edge + height :, :, :CHANS] = cot_below[...]
    shape = (WIN, IMG, LANES)

    def block(k, own):
        tall_shape = (WIN + 2, IMG, LANES)
        row = wrapped(wrapped(wrapped(base + IMG - 1 + WIN * k) + iota(tall_shape, 0)))
        inside = (row < size) & (iota(tall_shape, 1) < size)
        put_shifted(d_spread, jnp.where(inside, padded[pl.ds(WIN * k, WIN + 2)], 0.0))
        rows = wrapped(wrapped(base + WIN * k) + iota(shape, 0))
        rows_all = wrapped(wrapped(base + WIN * k) + iota((WIN, IMG, 3 * LANES), 0))
        total = jnp.zeros(shape, F32)
        here = pltpu.roll(after[pl.ds(WIN * k, WIN)], SHIFT, 1)[own]
        turned = turn(here.reshape(-1, LANES))
        for i in range(3):
            around = d_spread[2 - i : 2 - i + WIN]
            part = nn(around.reshape(BLOCK, 3 * LANES), tall[i]).reshape(shape)
            if i == 0:
                part = jnp.where(rows == IMG - 1, 0.0, part)
                around = jnp.where(rows_all == IMG - 1, 0.0, around)
            if i == 2:
                part = jnp.where(rows == 0, 0.0, part)
                around = jnp.where(rows_all == 0, 0.0, around)
            total = total + part
            grad[i, :184] += nn(turned, around[own].reshape(-1, 3 * LANES))
        d_mid[pl.ds(WIN * k, WIN)] = pltpu.roll(total, IMG - SHIFT, 1)
        centre = d_spread[1 : 1 + WIN, :, LANES : 2 * LANES][own]
        vec[CONV_BIAS : CONV_BIAS + 1, :LANES] += jnp.sum(
            centre.reshape(-1, LANES), 0, keepdims=True
        )

    block(0, slice(SHIFT, WIN))

    def inner(k, carry):
        block(k, slice(0, WIN))
        return carry

    lax.fori_loop(1, STEPS - 1, inner, 0)
    block(STEPS - 1, slice(0, SHIFT))
    for i in range(3):
        for j in range(3):
            taps[3 * i + j] = grad[i, :, LANES * (2 - j) : LANES * (3 - j)].T[:CHANS]
    for s in range(PARTS):

        def store(ref, s=s):
            for n in range(9):
                ref[CONV_ROWS * n : CONV_ROWS * n + share] = taps[n, share * s : share * s + share]

        put_part(keep, send, s, me, store)


def conv_kernel_body(k, scal, after, start, wide, vec, *refs):
    out, spread, ready, done = refs[-4:]
    tall_shape = (WIN + 2, IMG, LANES)
    first = wrapped(scal[1] + SHIFT) + WIN * k
    row = first - 1 + iota(tall_shape, 0)
    value = pltpu.roll(after[pl.ds(WIN * k + SHIFT - 1, WIN + 2)], SHIFT, 1)
    put_shifted(spread, jnp.where((row < 0) | (row >= IMG), 0.0, value))
    total = jnp.zeros((BLOCK, LANES), F32)
    for i in range(3):
        total = total + nt(spread[i : i + WIN].reshape(BLOCK, 3 * LANES), wide[i])
    mask = plain_mask(scal[0], first, WIN)
    conv = (total + vec[CONV_BIAS : CONV_BIAS + 1, :LANES]).reshape(mask.shape)
    here = pltpu.roll(start[pl.ds(WIN * k + SHIFT, WIN)], SHIFT, 1)
    ready[...] = (here + mask * conv)[:, :, :CHANS]
    copy = pltpu.make_async_copy(ready, out.at[pl.ds(WIN * k, WIN)], done.at[0])
    copy.start()
    copy.wait()


def feed_back_kernel(
    scal, d_mid, value, pre, attended, up, down, proj, vec, *refs
):
    d_attn, d_att, grads, g_proj, g_vec, g_up, g_down = refs[-7:]
    for ref in (g_up, g_down, g_proj, g_vec):
        ref[...] = jnp.zeros_like(ref)
    size = scal[0]

    def block(k, rows, part, counted):
        here = pl.ds(WIN * k, WIN)
        mask = frame_mask(size, block_first(scal, k))
        mid = d_mid[here]
        d_ff = (mask * mid).reshape(BLOCK, LANES)
        hidden = pre[here].reshape(BLOCK, HID)
        phi = gelu_parts(hidden)
        act = hidden * phi
        slope = phi + hidden * (jnp.exp(-0.5 * hidden * hidden) * 0.3989422804014327)
        d_pre = nt(d_ff, down[...]) * slope
        d_normed = nn(d_pre, up[...])
        unit3, scale = normalize(value[here])
        unit = unit3.reshape(BLOCK, LANES)
        gain = vec[MID_GAIN : MID_GAIN + 1, :LANES]
        normed = unit * gain + vec[MID_SHIFT : MID_SHIFT + 1, :LANES]
        grad = (d_normed * gain).reshape(mid.shape)
        d_out = mid + normalize_back(grad, unit3, scale)
        d_attn[here] = d_out
        d_proj = (mask * d_out).reshape(BLOCK, LANES)
        d_att[here] = nt(d_proj, proj[...]).reshape(mid.shape)
        d_ff_own, d_pre_own, d_normed_own = d_ff[part], d_pre[part], d_normed[part]
        g_down[:184] += nn(turn(d_ff_own), act[part])
        g_up[:184] += nn(turn(normed[part]), d_pre_own)
        g_vec[UP_BIAS : UP_BIAS + 1, :HID] += jnp.sum(d_pre_own, 0, keepdims=True)
        for at, v in (
            (MID_GAIN, d_normed_own * unit[part]),
            (MID_SHIFT, d_normed_own),
            (DOWN_BIAS, d_ff_own),
        ):
            g_vec[at : at + 1, :LANES] += jnp.sum(v, 0, keepdims=True)
        if counted:
            g_proj[:184] += nn(turn(d_proj), attended[here].reshape(BLOCK, LANES))
            g_vec[PROJ_BIAS : PROJ_BIAS + 1, :LANES] += jnp.sum(d_proj, 0, keepdims=True)

    block(0, None, slice(SHIFT * IMG, BLOCK), False)

    def inner(k, carry):
        block(k, None, slice(0, BLOCK), True)
        return carry

    lax.fori_loop(1, STEPS - 1, inner, 0)
    block(STEPS - 1, None, slice(0, SHIFT * IMG), True)
    for s in range(PARTS):
        rows = slice(FEED_ROWS * s, FEED_ROWS * s + FEED_ROWS)
        grads[s, :, :] = jnp.zeros_like(grads[s])
    turned_up = g_up[...].T
    turned_down = g_down[...].T
    for s in range(PARTS):
        rows = slice(FEED_ROWS * s, FEED_ROWS * s + FEED_ROWS)
        below = pltpu.roll(turned_down[rows], 64, 1)
        lanes = iota((FEED_ROWS, 128), 1)
        grads[s, :, :128] = turned_up[rows, :128]
        grads[s, :, 128:256] = jnp.where(lanes < 64, turned_up[rows, 128:], below[:, :128])
        grads[s, :, 256:] = below[:, 128:]


def attend_back_kernel(begin, end, scal, start, mixed, probs, d_att, *refs):
    refs = list(refs)
    first_call, last_call = begin == 0, end == STEPS
    if last_call:
        vec, qkv, vec_conv, vec_feed, feed, g_proj = refs[:6]
        d_mixed, keep, send, g_qkv, g_table, g_mixed, lines, proj_turned, turned_qkv = refs[-9:]
    else:
        d_mixed, g_qkv, g_table, g_mixed = refs[-4:]
    before = refs[6 if last_call else 0 :][:3]
    m = pl.program_id(0)
    k = m + begin

    @pl.when(m == 0)
    def _():
        for n, ref in enumerate((g_qkv, g_table, g_mixed)):
            ref[...] = jnp.zeros_like(ref) if first_call else before[n][...]

    counted = (k > 0).astype(F32)
    att_here = block_of(d_att, k)
    out_here = block_of(d_mixed, m)
    for pair in range(PAIRS):
        query = [q * HD**-0.5 for q in window_pair(mixed, pair, 0)]
        keys = window_pair(mixed, pair, LANES)
        values = window_pair(mixed, pair, 2 * LANES)
        d_rows = window_pair(att_here, pair, 0)
        prob = probs[0, pair]
        d_prob = head_products(values, d_rows).reshape(HEADS, 64, 128)
        prob3 = prob.reshape(HEADS, 64, 128)
        d_score = prob3 * (d_prob - jnp.sum(prob3 * d_prob, 1, keepdims=True))
        d_score = d_score.reshape(HEADS * 64, 128)
        g_table[...] += counted * d_score if first_call else d_score
        prob_tiles = straight_tiles(prob)
        score_tiles = straight_tiles(d_score)
        turned = turned_tiles(d_score)
        for w in range(2):
            part = slice(64 * w, 64 * w + 64)
            d_query = mix(turned[w], keys[0][part], keys[1][part])
            put_window(out_here, pair, w, 0, [d * HD**-0.5 for d in d_query])
            put_window(
                out_here, pair, w, LANES, mix(score_tiles[w], query[0][part], query[1][part])
            )
            put_window(
                out_here, pair, w, 2 * LANES, mix(prob_tiles[w], d_rows[0][part], d_rows[1][part])
            )

    def gather():
        unit, _ = normalize(start[pl.ds(WIN * k, WIN)])
        d_all = out_here[...].reshape(BLOCK, 3 * LANES)
        g_qkv[:184] += nn(turn(unit.reshape(BLOCK, LANES)), d_all)
        g_mixed[0:1] += jnp.sum(d_all, 0, keepdims=True)

    if first_call:
        pl.when(k > 0)(gather)
    else:
        gather()
    if last_call:

        @pl.when(m == pl.num_programs(0) - 1)
        def _():
            finish(
                scal[2], vec, qkv, vec_conv, vec_feed, feed, g_proj, keep, send, g_qkv, g_table,
                g_mixed, lines, proj_turned, turned_qkv,
            )


def finish(
    me, vec, qkv, vec_conv, vec_feed, feed, g_proj, keep, send, g_qkv, g_table, g_mixed, lines,
    proj_turned, turned_qkv,
):
    sums = g_mixed[...]
    cross = g_qkv[...].T
    lines[...] = vec_conv[...] + vec_feed[...]
    lines[PRE_GAIN : PRE_GAIN + 1, :LANES] = jnp.sum(cross * qkv[...], 0, keepdims=True)
    lines[PRE_SHIFT : PRE_SHIFT + 1, :LANES] = nn(sums, qkv[...])[0:1]
    lines[QV_BIAS : QV_BIAS + 1] = sums[0:1]
    turned_qkv[...] = cross * vec[PRE_GAIN : PRE_GAIN + 1, :LANES] + sums.T[:, 0:1] * vec[
        PRE_SHIFT : PRE_SHIFT + 1, :LANES
    ]
    folded = g_table[...]
    lane, u = iota((128, LANES), 0) & 63, iota((128, LANES), 1)
    pick = (u == 112 - 15 * (lane >> 3) - (lane & 7)).astype(F32)
    spread = dot(folded, pick, 1, 0, HIGHEST).reshape(HEADS, WIN, WIN, LANES)
    rel = []
    for h in range(HEADS):
        line = jnp.zeros((WIN, LANES), F32)
        for y in range(WIN):
            line = line + pltpu.roll(spread[h, y], 15 * y, 1, stride=1, stride_axis=0)
        rel.append(jnp.sum(line, 0, keepdims=True))
    rel = jnp.concatenate(rel + [jnp.zeros((REL_ROWS - HEADS, LANES), F32)], 0)
    share = CHANS // PARTS
    proj_turned[...] = g_proj[...].T
    lanes = iota((PROJ_ROWS, 128), 1)
    row = iota((VEC_ROWS, LANES), 0)
    for s in range(PARTS):

        def store(ref, s=s):
            ours = proj_turned[PROJ_ROWS * s : PROJ_ROWS * s + PROJ_ROWS]
            for m in range(3):
                at = s * 3 + m
                at = (at // 4) * LANES + (at % 4) * 48
                ref[48 * m : 48 * m + 48] = turned_qkv[at : at + 48, :128]
                piece = pltpu.roll(ours, (64 - 60 * m) % LANES, 1)[:, :128]
                ref[QKV_ROWS + 48 * m : QKV_ROWS + 48 * m + 48] = jnp.where(
                    lanes < 64, turned_qkv[at : at + 48, 128:], piece
                )
            for m in range(3):
                at = FEED_AT + FEED_ROWS * m
                ref[at : at + FEED_ROWS] = feed[s, :, 128 * m : 128 * m + 128]
            value = lines[...]

            def back(amount):
                return pltpu.roll(value, (3 * LANES - amount) % (3 * LANES), 1)[:, :LANES]

            vectors = jnp.where(
                row < QV_BIAS,
                back(share * s),
                jnp.where(
                    row == QV_BIAS, back((s // 2) * 2 * LANES + (s % 2) * 96), back(96 * s)
                ),
            )
            for m in range(2):
                tile = slice(128 * m, 128 * m + 128)
                at = VEC_AT + VEC_ROWS * m
                ref[at : at + VEC_ROWS] = vectors[:, tile]
                at = REL_AT + REL_ROWS * m
                ref[at : at + REL_ROWS] = rel[:, tile]

        put_part(keep, send, s, me, store)


def image_back_kernel(parts, scal, *refs):
    d_mixed = refs[:parts]
    start, d_attn, cot, qkv, vec = refs[parts : parts + 5]
    out, ready, done = refs[-3:]
    size = scal[0]
    copies = []
    per = STEPS * WIN // parts
    for k in range(STEPS - 1):
        pieces = []
        for row in (WIN * k + SHIFT, WIN * k + WIN):
            pieces.append(d_mixed[row // per][row % per : row % per + SHIFT])
        here = slice(WIN * k + SHIFT, WIN * k + SHIFT + WIN)
        own = slice(WIN * k, WIN * k + WIN)
        unit3, scale = normalize(start[here])
        d_all = jnp.concatenate(pieces, 0).reshape(BLOCK, 3 * LANES)
        d_normed = nn(d_all, qkv[...])
        grad = (d_normed * vec[PRE_GAIN : PRE_GAIN + 1, :LANES]).reshape(unit3.shape)
        value = d_attn[here] + normalize_back(grad, unit3, scale)
        near = cot[WIN * k + SHIFT + 1 : WIN * k + SHIFT + 1 + WIN]
        mask = plain_mask(size, wrapped(scal[1] + SHIFT) + WIN * k, WIN)
        ready[own] = (mask * (near + pltpu.roll(value, SHIFT, 1)))[:, :, :CHANS]
        copies.append(pltpu.make_async_copy(ready.at[own], out.at[own], done.at[k]))
        copies[-1].start()
    for copy in copies:
        copy.wait()


def unpack_kernel(last, qkv, proj, up, down, rel, *vectors):
    share = CHANS // PARTS
    for n in range(9):
        rows = slice(16 * n, 16 * n + HALF)
        qkv[HALF * n : HALF * n + HALF, :128] = last[rows]
        second = slice(QKV_ROWS + 16 * n, QKV_ROWS + 16 * n + HALF)
        qkv[HALF * n : HALF * n + HALF, 128:] = last[second][:, : CHANS - 128]
    pieces = [last[QKV_ROWS + 48 * m : QKV_ROWS + 48 * m + 48] for m in range(3)]
    pieces = [jnp.concatenate([p, jnp.zeros_like(p)], 1) for p in pieces]
    whole = [pltpu.roll(p, (60 * m - 64) % LANES, 1) for m, p in enumerate(pieces)]
    lanes = iota((PROJ_ROWS, LANES), 1)
    value = jnp.where(lanes < 60, whole[0], jnp.where(lanes < 120, whole[1], whole[2]))
    for n in range(3):
        proj[HALF * n : HALF * n + HALF] = value[16 * n : 16 * n + HALF, :CHANS]
    tiles = [last[FEED_AT + FEED_ROWS * m : FEED_AT + FEED_ROWS * (m + 1)] for m in range(3)]
    hid = up.shape[1]
    up[...] = jnp.concatenate(tiles[:2], 1).T[:CHANS, :hid]
    below = pltpu.roll(jnp.concatenate([tiles[1], tiles[2]], 1), LANES - 64, 1)
    down[...] = below.T[:CHANS, :hid]
    lines = jnp.concatenate([last[REL_AT : REL_AT + REL_ROWS], last[REL_AT + REL_ROWS :]], 1)
    a, b = iota((LANES, LANES), 0), iota((LANES, LANES), 1)
    rel[...] = dot(lines, (a + b == RPOS - 1).astype(F32), 1, 0, HIGHEST)[:HEADS, :RPOS]
    for n, ref in enumerate(vectors):
        if n != QV_BIAS:
            ref[...] = last[VEC_AT + n : VEC_AT + n + 1, : ref.shape[1]]
    for n in range(6):
        vectors[QV_BIAS][:, HALF * n : HALF * n + HALF] = last[
            VEC_AT + QV_BIAS : VEC_AT + QV_BIAS + 1, 16 * n : 16 * n + HALF
        ]


def blocked(rows, place):
    def make(shape):
        rest = tuple(shape[1:])
        return pl.BlockSpec((rows,) + rest, lambda m: (place(m),) + (0,) * len(rest))

    return make


def resident(shape):
    return pl.BlockSpec(memory_space=pltpu.VMEM)


def untouched(shape):
    return pl.BlockSpec(memory_space=pl.ANY)


def call(kernel, scal, ins, outs, scratch=(), after=(), limit=10, flops=0, steps=None, keep=None):
    ins = [i if isinstance(i, tuple) else (i, resident) for i in ins]
    outs = [o if callable(o[-1]) else (o, resident) for o in outs]
    ins = [(a if f is resident else pltpu.with_memory_space_constraint(a, pltpu.HBM), f) for a, f in ins]
    ins += [(a, untouched) for a in after]
    first = [] if scal is None else [scal]
    specs = [pl.BlockSpec(memory_space=pltpu.SMEM)] * len(first) + [f(a.shape) for a, f in ins]
    size = sum(4 * a.size for a, f in ins if f is not untouched)
    size += sum(4 * functools.reduce(lambda p, q: p * q, s) for s, _ in outs)
    return pl.pallas_call(
        kernel,
        grid=() if steps is None else (steps,),
        in_specs=specs,
        out_specs=[f(s) for s, f in outs],
        scratch_shapes=[pltpu.VMEM(s, F32) if isinstance(s, tuple) else s for s in scratch],
        out_shape=[
            jax.ShapeDtypeStruct(tuple(s), F32) if f is resident else pltpu.HBM(tuple(s), F32)
            for s, f in outs
        ],
        input_output_aliases={i + len(first): o for i, o in (keep or {}).items()},
        compiler_params=pltpu.CompilerParams(vmem_limit_bytes=limit * MIB),
        cost_estimate=pl.CostEstimate(flops=flops, bytes_accessed=size, transcendentals=0),
    )(*first, *[a for a, _ in ins])


def body(
    images,
    item_sizes,
    cotangent,
    pre_gain,
    pre_shift,
    qkv_weight,
    qv_bias,
    rel_table,
    proj_weight,
    proj_bias,
    mid_gain,
    mid_shift,
    up_weight,
    up_bias,
    down_weight,
    down_bias,
    conv_kernel,
    conv_bias,
):
    height, breadth = images.shape[1:3]
    me = lax.axis_index("tp")
    strip = height + 2 * SHIFT
    image = images[0]
    cot = cotangent[0].transpose(2, 0, 1)
    share = CHANS // PARTS

    def frame(lanes):
        return (strip, breadth, lanes)

    vectors = [pre_gain, pre_shift, proj_bias, mid_gain, mid_shift, down_bias, conv_bias, qv_bias, up_bias]
    at_once = lambda shape: pl.BlockSpec(tuple(shape), lambda m: (0,) * len(shape))
    mine1, mine2 = call(
        pack_kernel,
        None,
        [(a, at_once) for a in (qkv_weight.T, proj_weight, up_weight, down_weight.T, *[v[None] for v in vectors])],
        [(QKV_ROWS + PROJ_ROWS + VEC_ROWS, LANES), (2 * FEED_ROWS, LANES)],
        limit=8,
        steps=1,
    )
    mine3 = conv_kernel.transpose(0, 1, 3, 2).reshape(9, share, CHANS)
    scal = jnp.stack([item_sizes[0], (me * height + IMG - SHIFT) % IMG, me]).astype(jnp.int32)
    x_first, x_last = tie((image[:SHIFT], image[-SHIFT:]), mine1)
    x_above = from_behind(x_last, "tp", 1)
    x_below = from_behind(x_first, "tp", -1)
    all1 = gather_tp(mine1, x_first, x_last)

    qkv, proj, vec, table = call(
        prepare_kernel,
        scal,
        [*all1, rel_table.T],
        [(3 * LANES, LANES), (LANES, LANES), (VEC_ROWS, 3 * LANES), (HEADS * 64, 128)],
        [(VEC_ROWS, 3 * LANES)],
        limit=8,
        flops=10**8,
    )

    def attend(edges, arrays, old):
        place = (lambda m: m * (STEPS - 1)) if edges else (lambda m: m + 1)
        ins = [*arrays, qkv, vec, table, proj]
        keep = {len(ins) + n: n for n in range(len(old))}
        ins += [(o, untouched) for o in old[:2]] + list(old[2:])
        return call(
            functools.partial(attend_kernel, edges),
            scal,
            ins,
            [
                (frame(3 * LANES), blocked(WIN, place)),
                ((STEPS, PAIRS, HEADS * 64, 128), blocked(1, place)),
                frame(LANES),
                frame(LANES),
                frame(LANES),
            ],
            [(WIN, breadth, LANES)],
            flops=5 * 10**9,
            limit=16,
            steps=2,
            keep=keep,
        )

    old = attend(False, [image], [])
    all2 = gather_tp(mine2, old[2])
    c_first, c_last = call(
        rims_kernel, None, [cot], [(SHIFT + 1, breadth, CHANS)] * 2, after=[old[2]], limit=8
    )
    c_above = from_behind(c_last, "tp", 1)
    c_below = from_behind(c_first, "tp", -1)
    mixed, probs, attended, after_attn, start = attend(True, [x_above, image, x_below], old)
    all3 = gather_tp(tie(mine3, old[2]), after_attn)
    pre, after_mlp, up, down = call(
        feed_kernel,
        scal,
        [after_attn, vec, *all2],
        [frame(HID), frame(LANES), (HID, LANES), (HID, LANES)],
        flops=5 * 10**9,
    )
    d_mid, conv_keep, conv_send, vec_conv, wide, cot_rows = call(
        conv_back_kernel,
        scal,
        [after_mlp, cot, c_above, c_below, *all3],
        [
            frame(LANES),
            (2, 9 * CONV_ROWS, LANES),
            (2, 9 * CONV_ROWS, LANES),
            (VEC_ROWS, 3 * LANES),
            (3, LANES, 3 * LANES),
            (strip + 2, breadth, LANES),
        ],
        [
            (WIN + 2, breadth, 3 * LANES),
            (3, 3 * LANES, LANES),
            (PARTS, 9, share, CHANS),
            (3, LANES, 3 * LANES),
            (9, CHANS, LANES),
        ],
        flops=2 * 10**10,
        limit=20,
    )
    got_a = lax.ppermute(conv_send, "tp", flip("tp", 1))
    d_attn, d_att, g_feed, g_proj, vec_feed = call(
        feed_back_kernel,
        scal,
        [d_mid, after_attn, pre, attended, up, down, proj, vec],
        [frame(LANES), frame(LANES), (PARTS, FEED_ROWS, HID), (LANES, LANES), (VEC_ROWS, 3 * LANES)],
        [(LANES, HID), (LANES, HID)],
        after=[conv_send],
        flops=10**10,
        limit=14,
    )
    got_a = tie(got_a, d_att)
    send_b = conv_keep[1] + got_a[1]
    got_b = lax.ppermute(send_b, "tp", flip("tp", 2))

    g_shapes = [(LANES, 3 * LANES), (HEADS * 64, 128), (8, 3 * LANES)]

    def attend_back(begin, end, old, after):
        place = lambda m: m + begin
        ins = [start, (mixed, blocked(WIN, place)), (probs, blocked(1, place)), d_att]
        outs = [((end - begin) * WIN, breadth, 3 * LANES)]
        scratch = []
        if end == STEPS:
            ins += [vec, qkv, vec_conv, vec_feed, g_feed, g_proj]
            outs += [(2, TAIL_ROWS, 128)] * 2
            scratch = g_shapes + [(VEC_ROWS, 3 * LANES), (LANES, LANES), (3 * LANES, LANES)]
        else:
            outs += g_shapes
        return call(
            functools.partial(attend_back_kernel, begin, end),
            scal,
            ins + list(old),
            outs,
            scratch,
            after=after,
            flops=5 * 10**9 * (end - begin),
            limit=16,
            steps=end - begin,
        )

    d_mixed0, *sums = attend_back(0, 2, [], [send_b])
    got_b = tie(got_b, d_mixed0)
    held = conv_keep[0] + got_a[0] + got_b
    bits = dp_bits()
    d_mixed1, tail_keep, tail_send = attend_back(2, STEPS, sums, [held])
    held = dp_halve(held, bits[0], d_mixed1)

    blocks = height // WIN

    def convolve(k, old, after):
        ins = [after_mlp, start, wide, vec]
        return call(
            functools.partial(conv_kernel_body, k),
            scal,
            ins + [(o, untouched) for o in old],
            [((height, breadth, CHANS), untouched)],
            [(WIN + 2, breadth, 3 * LANES), (WIN, breadth, CHANS), pltpu.SemaphoreType.DMA((1,))],
            after=after,
            flops=4 * 10**9,
            keep={len(ins): 0} if old else None,
        )[0]

    last_a = lax.ppermute(tail_send, "tp", flip("tp", 1))
    block_out = convolve(0, [], [tail_send])
    last_a = tie(last_a, block_out)
    last_send = tail_keep[1] + last_a[1]
    last_b = lax.ppermute(last_send, "tp", flip("tp", 2))
    if len(bits) > 1:
        held = dp_add(held, bits[1], block_out)
    (grad_images,) = call(
        functools.partial(image_back_kernel, 2),
        scal,
        [d_mixed0, d_mixed1, start, d_attn, cot_rows, qkv, vec],
        [((height, breadth, CHANS), untouched)],
        [(height, breadth, CHANS), pltpu.SemaphoreType.DMA((STEPS - 1,))],
        after=[last_send],
        flops=4 * 10**9,
    )
    last_b = tie(last_b, grad_images)
    last = tail_keep[0] + last_a[0] + last_b
    for k in range(1, blocks):
        if k == 1:
            block_out = convolve(k, [block_out], [last])
            last = dp_halve(last, bits[0], block_out)
        elif k <= len(bits):
            block_out = convolve(k, [block_out], [last])
            last = dp_add(last, bits[k - 1], block_out)
    grad_images = tie(grad_images, last)
    for bit in bits[2:]:
        held = dp_add(held, bit, grad_images)
    for bit in bits[blocks - 1 :]:
        last = dp_add(last, bit)
    held = dp_join(held, bits[0], last)
    block_out = tie(block_out, last)
    last = dp_join(last, bits[0])

    conv = held.reshape(3, 3, CONV_ROWS, LANES)[:, :, :share, :CHANS]
    hid = up_weight.shape[1]
    g_qkv, g_proj, g_up, g_down, g_rel, *g_vec = call(
        unpack_kernel,
        None,
        [last],
        [(qkv_weight.shape[1], CHANS), (share, CHANS), (CHANS, hid), (CHANS, hid), (HEADS, RPOS)] + [(1, v.shape[0]) for v in vectors],
        limit=8,
    )

    g_vec = [g[0] for g in g_vec]
    return (
        block_out[None],
        grad_images[None],
        g_vec[PRE_GAIN],
        g_vec[PRE_SHIFT],
        g_qkv.T,
        g_vec[QV_BIAS],
        g_rel.T,
        g_proj,
        g_vec[PROJ_BIAS],
        g_vec[MID_GAIN],
        g_vec[MID_SHIFT],
        g_up,
        g_vec[UP_BIAS],
        g_down.T,
        g_vec[DOWN_BIAS],
        conv.transpose(0, 1, 3, 2),
        g_vec[CONV_BIAS],
    )


def solution(mesh):
    placed = (
        P("dp", "tp", None, None),
        P("dp"),
        P("dp", "tp", None, None),
        P("tp"),
        P("tp"),
        P(None, "tp"),
        P("tp"),
        P(),
        P("tp", None),
        P("tp"),
        P("tp"),
        P("tp"),
        P(None, "tp"),
        P("tp"),
        P("tp", None),
        P("tp"),
        P(None, None, None, "tp"),
        P("tp"),
    )
    return jax.shard_map(
        body,
        mesh=mesh,
        in_specs=placed,
        out_specs=(
            P("dp", "tp", None, None),
            P("dp", "tp", None, None),
            P("tp"),
            P("tp"),
            P(None, "tp"),
            P("tp"),
            P(),
            P("tp", None),
            P("tp"),
            P("tp"),
            P("tp"),
            P(None, "tp"),
            P("tp"),
            P("tp", None),
            P("tp"),
            P(None, None, None, "tp"),
            P("tp"),
        ),
        check_vma=False,
    )
```

```python
import functools

import jax
import jax.numpy as jnp
from jax import lax
from jax.experimental import pallas as pl
from jax.experimental.pallas import tpu as pltpu
from jax.sharding import PartitionSpec as P

WIN = 8
IMG = 96
SHIFT = 4
EPSILON = 1e-05
NEG_FILL = -1e30
CHANS = 180
HEADS = 6
HD = 30
HALF = 15
SLOT = 32
LANES = 256
INNER = 192
HID = 384
RPOS = 225
HIGH = lax.Precision.HIGH
HIGHEST = lax.Precision.HIGHEST
F32 = jnp.float32
BF16 = jnp.bfloat16
BLOCK = WIN * IMG
PAIRS = IMG // WIN // 2
PARTS = 4
MIB = 2**20
STEPS = 4

QKV_ROWS, PROJ_ROWS, VEC_ROWS = 144, 48, 16
FEED_ROWS = 96
CONV_ROWS = 48
REL_ROWS = 8
FEED_AT = 2 * QKV_ROWS
VEC_AT = FEED_AT + 3 * FEED_ROWS
REL_AT = VEC_AT + VEC_ROWS
TAIL_ROWS = REL_AT + 2 * REL_ROWS
PRE_GAIN, PRE_SHIFT, PROJ_BIAS, MID_GAIN, MID_SHIFT, DOWN_BIAS, CONV_BIAS, QV_BIAS, UP_BIAS = range(9)


def flip(axis, bit):
    return [(i, i ^ bit) for i in range(lax.axis_size(axis))]


def from_behind(block, axis, distance):
    n = lax.axis_size(axis)
    return lax.ppermute(block, axis, [((i - distance) % n, i) for i in range(n)])


def gather_tp(block, *others):
    got = {0: block}
    for bit in (2, 1):
        if others and bit == 1:
            got[2] = tie(got[2], *others)
        got.update({k | bit: lax.ppermute(b, "tp", flip("tp", bit)) for k, b in list(got.items())})
    return [got[k] for k in range(PARTS)]


def tie(value, *others):
    return lax.optimization_barrier((value, others))[0]


def dp_bits():
    n = lax.axis_size("dp")
    return [1 << b for b in range(n.bit_length() - 1)]


def dp_halve(held, bit, *others):
    half = held.shape[0] // 2
    odd = (lax.axis_index("dp") & bit) != 0
    send = jnp.where(odd, held[:half], held[half:])
    got = lax.ppermute(send, "dp", flip("dp", bit))
    if others:
        got = tie(got, *others)
    return jnp.where(odd, held[half:], held[:half]) + got


def dp_join(held, bit, *others):
    odd = (lax.axis_index("dp") & bit) != 0
    got = lax.ppermute(held, "dp", flip("dp", bit))
    if others:
        got = tie(got, *others)
    return jnp.concatenate([jnp.where(odd, got, held), jnp.where(odd, held, got)], 0)


def dp_add(held, bit, *others):
    got = lax.ppermute(held, "dp", flip("dp", bit))
    if others:
        got = tie(got, *others)
    return held + got


def dot(left, right, left_dim, right_dim, precision=None):
    return lax.dot_general(
        left,
        right,
        (((left_dim,), (right_dim,)), ((), ())),
        precision=precision,
        preferred_element_type=F32,
    )


def nn(left, right):
    return dot(left, right, 1, 0, HIGH)


def nt(left, right):
    return dot(left, right, 1, 1, HIGH)


def turn(value):
    return value.T[:184]


def iota(shape, dim):
    return lax.broadcasted_iota(jnp.int32, shape, dim)


def wrapped(position):
    return jnp.where(position >= IMG, position - IMG, position)


def frame_mask(size, first, rows=WIN):
    shape = (rows, IMG, LANES)
    row = wrapped(first + iota(shape, 0))
    col = wrapped(iota(shape, 1) + SHIFT)
    return ((row < size) & (col < size) & (iota(shape, 2) < CHANS)).astype(F32)


def plain_mask(size, first, rows):
    shape = (rows, IMG, LANES)
    row = wrapped(first + iota(shape, 0))
    return ((row < size) & (iota(shape, 1) < size) & (iota(shape, 2) < CHANS)).astype(F32)


def is_channel(shape):
    return iota(shape, len(shape) - 1) < CHANS


def mean(value):
    return jnp.sum(value, axis=-1, keepdims=True) * (1.0 / CHANS)


def normalize(value):
    centre = jnp.where(is_channel(value.shape), value - mean(value), 0.0)
    scale = lax.rsqrt(mean(centre * centre) + EPSILON)
    return centre * scale, scale


def normalize_back(grad, unit, scale):
    value = scale * (grad - mean(grad) - unit * mean(grad * unit))
    return jnp.where(is_channel(value.shape), value, 0.0)


def upper(value):
    return value.astype(BF16).astype(F32)


def parted(value):
    high = upper(value)
    return jnp.where(iota(value.shape, 1) < 64, high, value - high)


def doubled(first, second):
    left = iota(first.shape, 1) < 64
    turned0 = pltpu.roll(first, 64, 1)
    turned1 = pltpu.roll(second, 64, 1)
    return (
        jnp.where(left, first, turned0),
        jnp.where(left, turned0, first),
        jnp.where(left, second, turned1),
    )


def head_products(rows, cols):
    lanes = iota((128, 128), 1)
    even = (lanes & 63) < SLOT
    outs = []
    for moving, fixed in zip(doubled(*rows), doubled(*cols)):
        high = fixed.astype(BF16)
        low = (fixed - high.astype(F32)).astype(BF16)
        held = jnp.concatenate([high, low], 1)
        pieces = parted(moving)
        ones = jnp.where(even, pieces, 0.0).astype(BF16)
        twos = jnp.where(even, 0.0, pieces).astype(BF16)
        both = []
        for w in range(2):
            part = slice(64 * w, 64 * w + 64)
            stream = jnp.concatenate([ones[part], twos[part]], 0)
            both.append(dot(jnp.concatenate([stream, stream], 1), held, 1, 1))
        outs.append(jnp.where(lanes < 64, both[0], both[1]))
    return jnp.concatenate(outs, 0)


def mix(tiles, first, second):
    n = tiles[0].shape[0]
    lanes = iota((n, 128), 1)

    def product(part, block):
        high = block.astype(BF16)
        low = (block - high.astype(F32)).astype(BF16)
        held = jnp.concatenate([high, high, low, low], 0)
        stream = jnp.concatenate(part, 0)
        return dot(jnp.concatenate([stream, stream], 1), held, 1, 0)

    a = product(tiles[:4], first)
    b = product(tiles[4:], second)
    one = jnp.where(
        lanes < 64,
        jnp.where(lanes < 32, a[:n], a[n : 2 * n]),
        jnp.where(lanes < 96, a[2 * n : 3 * n], a[3 * n :]),
    )
    two = jnp.where(lanes < 32, b[:n], b[n:])
    return one, two


def straight_tiles(table):
    left = iota(table.shape, 1) < 64
    turned = pltpu.roll(table, 64, 1)
    outs = []
    for w in range(2):
        one = jnp.where(left, table, turned) if w == 0 else jnp.where(left, turned, table)
        both = parted(one).astype(BF16)
        outs.append([both[64 * h : 64 * h + 64] for h in range(HEADS)])
    return outs


def turned_tiles(table):
    high = upper(table)
    low = table - high
    outs = [[], []]
    for h in range(HEADS):
        part = slice(64 * h, 64 * h + 64)
        both = jnp.concatenate([high[part], low[part]], 0).astype(BF16).T
        for w in range(2):
            outs[w].append(both[64 * w : 64 * w + 64])
    return outs


def window_pair(ref, pair, start):
    cols = pl.ds(pl.multiple_of(pair * 2 * WIN, 2 * WIN), 2 * WIN)
    tiles = []
    for tile in range(2):
        block = ref[:, cols, start + 128 * tile : start + 128 * tile + 128]
        tiles.append(
            jnp.concatenate(
                [block[:, :WIN].reshape(64, 128), block[:, WIN:].reshape(64, 128)], 0
            )
        )
    return tiles


def put_window(ref, pair, w, start, tiles):
    cols = pl.ds(pl.multiple_of(pair * 2 * WIN + w * WIN, WIN), WIN)
    rows = tiles[0].shape[0] // WIN
    for tile in range(2):
        ref[WIN - rows :, cols, start + 128 * tile : start + 128 * tile + 128] = tiles[
            tile
        ].reshape(rows, WIN, 128)


def pair_fill(size, first, pair):
    shape = (64, 128)
    j, lane = iota(shape, 0), iota(shape, 1)
    i, window = lane & 63, 2 * pair + (lane >> 6)
    rows = wrapped(first + (j >> 3))
    cols = wrapped(window * WIN + (j & 7) + SHIFT)
    apart_rows = (first == IMG - WIN + SHIFT) & ((j >> 5) != (i >> 5))
    apart_cols = (window == IMG // WIN - 1) & (((j & 7) >> 2) != ((i & 7) >> 2))
    keep = (rows < size) & (cols < size)
    return jnp.where(apart_rows | apart_cols | jnp.logical_not(keep), NEG_FILL, 0.0)


def block_first(scal, k):
    return wrapped(scal[1] + WIN * k)


def block_of(ref, k):
    return ref.at[pl.ds(WIN * k, WIN)]


def put_part(keep, send, part, me, store):
    place = part ^ me
    pl.when((place & 1) == 0)(lambda: store(keep.at[place >> 1]))
    pl.when((place & 1) == 1)(lambda: store(send.at[place >> 1]))


def gelu_parts(hidden):
    return 0.5 * (1.0 + lax.erf(hidden * 0.5**0.5))


def pack_kernel(qkv, proj, up, down, *refs):
    vectors, (first, second) = refs[:9], refs[9:]
    first[...] = jnp.zeros_like(first)
    second[...] = jnp.zeros_like(second)
    for n in range(9):
        first[16 * n : 16 * n + HALF, :CHANS] = qkv[HALF * n : HALF * n + HALF]
    for n in range(3):
        at = QKV_ROWS + 16 * n
        first[at : at + HALF, :CHANS] = proj[HALF * n : HALF * n + HALF]
    share, hid = CHANS // PARTS, up.shape[1]
    second[:hid, :CHANS] = up[...].T
    second[FEED_ROWS : FEED_ROWS + hid, :CHANS] = down[...].T
    at = QKV_ROWS + PROJ_ROWS
    for n, ref in enumerate(vectors):
        if n != QV_BIAS:
            first[at + n : at + n + 1, : ref.shape[1]] = ref[...]
    for n in range(6):
        first[at + QV_BIAS : at + QV_BIAS + 1, 16 * n : 16 * n + HALF] = vectors[QV_BIAS][
            :, HALF * n : HALF * n + HALF
        ]


def rims_kernel(cot, *refs):
    first, last = refs[-2:]
    height, n = cot.shape[1], first.shape[0]
    for row in range(n):
        first[row] = cot[:, row, :].T
        last[row] = cot[:, height - n + row, :].T


def prepare_kernel(scal, p0, p1, p2, p3, rel, qkv, proj, vec, table, spread):
    me = scal[2]
    for ref in (qkv, vec, spread):
        ref[...] = jnp.zeros_like(ref)
    proj[INNER:] = jnp.zeros_like(proj[INNER:])
    lanes = iota((VEC_ROWS, 3 * LANES), 1)
    row = iota((VEC_ROWS, 3 * LANES), 0)
    for k, piece in enumerate((p0, p1, p2, p3)):
        owner = me ^ k
        for m in range(3):
            at = owner * 3 + m
            start = pl.multiple_of((at // 4) * LANES + (at % 4) * 48, 16)
            qkv[pl.ds(start, 48)] = piece[48 * m : 48 * m + 48]
        proj[pl.ds(pl.multiple_of(owner * PROJ_ROWS, 16), PROJ_ROWS)] = piece[
            QKV_ROWS : QKV_ROWS + PROJ_ROWS
        ]
        spread[:VEC_ROWS, :LANES] = piece[QKV_ROWS + PROJ_ROWS :]
        value = spread[:VEC_ROWS]
        vec[...] += jnp.where(
            row < QV_BIAS,
            pltpu.roll(value, owner * (CHANS // PARTS), 1),
            jnp.where(
                row == QV_BIAS,
                pltpu.roll(value, (owner // 2) * 2 * LANES + (owner % 2) * 96, 1),
                pltpu.roll(value, owner * 96, 1),
            ),
        )
    spread[...] = jnp.zeros_like(spread)
    spread[:HEADS, :RPOS] = rel[...]
    pieces = []
    for h in range(HEADS):
        line = jnp.broadcast_to(spread[h : h + 1, :LANES], (WIN, LANES))
        for y in range(WIN):
            pieces.append(
                pltpu.roll(line, (15 * y - 112) % LANES, 1, stride=1, stride_axis=0)
            )
    lines = jnp.concatenate(pieces, 0)
    u, lane = iota((LANES, 128), 0), iota((LANES, 128), 1) & 63
    pick = (u == (lane >> 3) * 15 + (lane & 7)).astype(F32)
    table[...] = dot(lines, pick, 1, 0, HIGHEST)


def attend_kernel(edges, scal, *refs):
    m = pl.program_id(0)
    if edges:
        above, image, below, qkv, vec, table, proj = refs[:7]
        k = m * (STEPS - 1)
    else:
        image, qkv, vec, table, proj = refs[:5]
        k = m + 1
    mixed, probs, attended, after, start, wide = refs[-6:]
    height = image.shape[0]

    @pl.when(m == 0)
    def _():
        wide[...] = jnp.zeros_like(wide)
        if edges:
            wide[:SHIFT, :, :CHANS] = above[...]
            wide[SHIFT:, :, :CHANS] = image[:SHIFT]

    if edges:

        @pl.when(m == 1)
        def _():
            wide[:SHIFT, :, :CHANS] = image[height - SHIFT :]
            wide[SHIFT:, :, :CHANS] = below[...]

    else:
        wide[:, :, :CHANS] = image[pl.ds(WIN * k - SHIFT, WIN)]
    size, first = scal[0], block_first(scal, k)
    rows = pl.ds(WIN * k, WIN)
    mask = frame_mask(size, first)
    begin = mask * pltpu.roll(wide[...], IMG - SHIFT, 1)
    start[rows] = begin
    unit, _ = normalize(begin)
    normed = unit * vec[PRE_GAIN, :LANES] + vec[PRE_SHIFT, :LANES]
    mixed[...] = (
        nt(normed.reshape(BLOCK, LANES), qkv[...]) + vec[QV_BIAS : QV_BIAS + 1]
    ).reshape(WIN, IMG, 3 * LANES)
    out_here = block_of(attended, k)
    for pair in range(PAIRS):
        query = window_pair(mixed, pair, 0)
        keys = window_pair(mixed, pair, LANES)
        values = window_pair(mixed, pair, 2 * LANES)
        scores = head_products(keys, [q * HD**-0.5 for q in query]) + table[...]
        scores = scores.reshape(HEADS, 64, 128) + pair_fill(size, first, pair)[None]
        scores = jnp.exp(scores - jnp.max(scores, 1, keepdims=True))
        prob = (scores * (1.0 / jnp.sum(scores, 1, keepdims=True))).reshape(HEADS * 64, 128)
        probs[0, pair] = prob
        for w, tiles in enumerate(turned_tiles(prob)):
            part = slice(64 * w, 64 * w + 64)
            put_window(out_here, pair, w, 0, mix(tiles, values[0][part], values[1][part]))
    out = nn(out_here[...].reshape(BLOCK, LANES), proj[...]) + vec[PROJ_BIAS : PROJ_BIAS + 1, :LANES]
    after[rows] = begin + mask * out.reshape(WIN, IMG, LANES)


def feed_kernel(scal, value, vec, p0, p1, p2, p3, pre, after, up, down):
    for k, piece in enumerate((p0, p1, p2, p3)):
        rows = pl.ds(pl.multiple_of((scal[2] ^ k) * FEED_ROWS, 32), FEED_ROWS)
        up[rows] = piece[:FEED_ROWS]
        down[rows] = piece[FEED_ROWS:]

    def block(k, carry):
        rows = pl.ds(WIN * k, WIN)
        mask = frame_mask(scal[0], block_first(scal, k))
        here = value[rows]
        unit, _ = normalize(here)
        normed = unit * vec[MID_GAIN, :LANES] + vec[MID_SHIFT, :LANES]
        hidden = nt(normed.reshape(BLOCK, LANES), up[...]) + vec[UP_BIAS : UP_BIAS + 1, :HID]
        pre[rows] = hidden.reshape(WIN, IMG, HID)
        act = hidden * gelu_parts(hidden)
        out = nn(act, down[...]) + vec[DOWN_BIAS : DOWN_BIAS + 1, :LANES]
        after[rows] = here + mask * out.reshape(here.shape)
        return carry

    lax.fori_loop(0, STEPS, block, 0)


def put_shifted(ref, value):
    cols = iota(value.shape, 1)
    ref[:, :, LANES : 2 * LANES] = value
    ref[:, :, :LANES] = jnp.where(cols == 0, 0.0, pltpu.roll(value, 1, 1))
    ref[:, :, 2 * LANES :] = jnp.where(cols == IMG - 1, 0.0, pltpu.roll(value, IMG - 1, 1))


def conv_back_kernel(
    scal,
    after,
    cot,
    cot_above,
    cot_below,
    p0,
    p1,
    p2,
    p3,
    d_mid,
    keep,
    send,
    vec,
    wide,
    padded,
    d_spread,
    tall,
    gathered,
    grad,
    taps,
):
    height = cot.shape[1]
    share = CHANS // PARTS
    size, base, me = scal[0], scal[1], scal[2]
    for ref in (wide, tall, padded, grad, vec):
        ref[...] = jnp.zeros_like(ref)
    for n, piece in enumerate((p0, p1, p2, p3)):
        gathered[me ^ n] = piece[...]
    for s in range(PARTS):
        rows = slice(share * s, share * s + share)
        for i in range(3):
            for j in range(3):
                part = gathered[s, 3 * i + j]
                wide[i, rows, LANES * j : LANES * j + CHANS] = part
                at = LANES * (2 - j) + share * s
                tall[i, at : at + share, :CHANS] = part
    edge = SHIFT + 1
    padded[:edge, :, :CHANS] = cot_above[...]
    for row in range(height):
        padded[edge + row, :, :CHANS] = cot[:, row, :].T
    padded[edge + height :, :, :CHANS] = cot_below[...]
    shape = (WIN, IMG, LANES)

    def block(k, own):
        tall_shape = (WIN + 2, IMG, LANES)
        row = wrapped(wrapped(wrapped(base + IMG - 1 + WIN * k) + iota(tall_shape, 0)))
        inside = (row < size) & (iota(tall_shape, 1) < size)
        put_shifted(d_spread, jnp.where(inside, padded[pl.ds(WIN * k, WIN + 2)], 0.0))
        rows = wrapped(wrapped(base + WIN * k) + iota(shape, 0))
        rows_all = wrapped(wrapped(base + WIN * k) + iota((WIN, IMG, 3 * LANES), 0))
        total = jnp.zeros(shape, F32)
        here = pltpu.roll(after[pl.ds(WIN * k, WIN)], SHIFT, 1)[own]
        turned = turn(here.reshape(-1, LANES))
        for i in range(3):
            around = d_spread[2 - i : 2 - i + WIN]
            part = nn(around.reshape(BLOCK, 3 * LANES), tall[i]).reshape(shape)
            if i == 0:
                part = jnp.where(rows == IMG - 1, 0.0, part)
                around = jnp.where(rows_all == IMG - 1, 0.0, around)
            if i == 2:
                part = jnp.where(rows == 0, 0.0, part)
                around = jnp.where(rows_all == 0, 0.0, around)
            total = total + part
            grad[i, :184] += nn(turned, around[own].reshape(-1, 3 * LANES))
        d_mid[pl.ds(WIN * k, WIN)] = pltpu.roll(total, IMG - SHIFT, 1)
        centre = d_spread[1 : 1 + WIN, :, LANES : 2 * LANES][own]
        vec[CONV_BIAS : CONV_BIAS + 1, :LANES] += jnp.sum(
            centre.reshape(-1, LANES), 0, keepdims=True
        )

    block(0, slice(SHIFT, WIN))

    def inner(k, carry):
        block(k, slice(0, WIN))
        return carry

    lax.fori_loop(1, STEPS - 1, inner, 0)
    block(STEPS - 1, slice(0, SHIFT))
    for i in range(3):
        for j in range(3):
            taps[3 * i + j] = grad[i, :, LANES * (2 - j) : LANES * (3 - j)].T[:CHANS]
    for s in range(PARTS):

        def store(ref, s=s):
            for n in range(9):
                ref[CONV_ROWS * n : CONV_ROWS * n + share] = taps[n, share * s : share * s + share]

        put_part(keep, send, s, me, store)


def conv_kernel_body(k, scal, after, start, wide, vec, *refs):
    out, spread, ready, done = refs[-4:]
    tall_shape = (WIN + 2, IMG, LANES)
    first = wrapped(scal[1] + SHIFT) + WIN * k
    row = first - 1 + iota(tall_shape, 0)
    value = pltpu.roll(after[pl.ds(WIN * k + SHIFT - 1, WIN + 2)], SHIFT, 1)
    put_shifted(spread, jnp.where((row < 0) | (row >= IMG), 0.0, value))
    total = jnp.zeros((BLOCK, LANES), F32)
    for i in range(3):
        total = total + nt(spread[i : i + WIN].reshape(BLOCK, 3 * LANES), wide[i])
    mask = plain_mask(scal[0], first, WIN)
    conv = (total + vec[CONV_BIAS : CONV_BIAS + 1, :LANES]).reshape(mask.shape)
    here = pltpu.roll(start[pl.ds(WIN * k + SHIFT, WIN)], SHIFT, 1)
    ready[...] = (here + mask * conv)[:, :, :CHANS]
    copy = pltpu.make_async_copy(ready, out.at[pl.ds(WIN * k, WIN)], done.at[0])
    copy.start()
    copy.wait()


def feed_back_kernel(
    scal, d_mid, value, pre, attended, up, down, proj, vec, *refs
):
    d_attn, d_att, grads, g_proj, g_vec, g_up, g_down = refs[-7:]
    for ref in (g_up, g_down, g_proj, g_vec):
        ref[...] = jnp.zeros_like(ref)
    size = scal[0]

    def block(k, rows, part, counted):
        here = pl.ds(WIN * k, WIN)
        mask = frame_mask(size, block_first(scal, k))
        mid = d_mid[here]
        d_ff = (mask * mid).reshape(BLOCK, LANES)
        hidden = pre[here].reshape(BLOCK, HID)
        phi = gelu_parts(hidden)
        act = hidden * phi
        slope = phi + hidden * (jnp.exp(-0.5 * hidden * hidden) * 0.3989422804014327)
        d_pre = nt(d_ff, down[...]) * slope
        d_normed = nn(d_pre, up[...])
        unit3, scale = normalize(value[here])
        unit = unit3.reshape(BLOCK, LANES)
        gain = vec[MID_GAIN : MID_GAIN + 1, :LANES]
        normed = unit * gain + vec[MID_SHIFT : MID_SHIFT + 1, :LANES]
        grad = (d_normed * gain).reshape(mid.shape)
        d_out = mid + normalize_back(grad, unit3, scale)
        d_attn[here] = d_out
        d_proj = (mask * d_out).reshape(BLOCK, LANES)
        d_att[here] = nt(d_proj, proj[...]).reshape(mid.shape)
        d_ff_own, d_pre_own, d_normed_own = d_ff[part], d_pre[part], d_normed[part]
        g_down[:184] += nn(turn(d_ff_own), act[part])
        g_up[:184] += nn(turn(normed[part]), d_pre_own)
        g_vec[UP_BIAS : UP_BIAS + 1, :HID] += jnp.sum(d_pre_own, 0, keepdims=True)
        for at, v in (
            (MID_GAIN, d_normed_own * unit[part]),
            (MID_SHIFT, d_normed_own),
            (DOWN_BIAS, d_ff_own),
        ):
            g_vec[at : at + 1, :LANES] += jnp.sum(v, 0, keepdims=True)
        if counted:
            g_proj[:184] += nn(turn(d_proj), attended[here].reshape(BLOCK, LANES))
            g_vec[PROJ_BIAS : PROJ_BIAS + 1, :LANES] += jnp.sum(d_proj, 0, keepdims=True)

    block(0, None, slice(SHIFT * IMG, BLOCK), False)

    def inner(k, carry):
        block(k, None, slice(0, BLOCK), True)
        return carry

    lax.fori_loop(1, STEPS - 1, inner, 0)
    block(STEPS - 1, None, slice(0, SHIFT * IMG), True)
    for s in range(PARTS):
        rows = slice(FEED_ROWS * s, FEED_ROWS * s + FEED_ROWS)
        grads[s, :, :] = jnp.zeros_like(grads[s])
    turned_up = g_up[...].T
    turned_down = g_down[...].T
    for s in range(PARTS):
        rows = slice(FEED_ROWS * s, FEED_ROWS * s + FEED_ROWS)
        below = pltpu.roll(turned_down[rows], 64, 1)
        lanes = iota((FEED_ROWS, 128), 1)
        grads[s, :, :128] = turned_up[rows, :128]
        grads[s, :, 128:256] = jnp.where(lanes < 64, turned_up[rows, 128:], below[:, :128])
        grads[s, :, 256:] = below[:, 128:]


def attend_back_kernel(begin, end, scal, start, mixed, probs, d_att, *refs):
    refs = list(refs)
    first_call, last_call = begin == 0, end == STEPS
    if last_call:
        vec, qkv, vec_conv, vec_feed, feed, g_proj = refs[:6]
        d_mixed, keep, send, g_qkv, g_table, g_mixed, lines, proj_turned, turned_qkv = refs[-9:]
    else:
        d_mixed, g_qkv, g_table, g_mixed = refs[-4:]
    before = refs[6 if last_call else 0 :][:3]
    m = pl.program_id(0)
    k = m + begin

    @pl.when(m == 0)
    def _():
        for n, ref in enumerate((g_qkv, g_table, g_mixed)):
            ref[...] = jnp.zeros_like(ref) if first_call else before[n][...]

    att_here = block_of(d_att, k)
    out_here = block_of(d_mixed, m)

    def work(begin_at):
        for pair in range(PAIRS):
            query = [q * HD**-0.5 for q in window_pair(mixed, pair, 0)]
            keys = window_pair(mixed, pair, LANES)
            values = window_pair(mixed, pair, 2 * LANES)
            d_rows = window_pair(att_here, pair, 0)
            prob = probs[0, pair]
            d_prob = head_products(values, d_rows).reshape(HEADS, 64, 128)
            prob3 = prob.reshape(HEADS, 64, 128)
            d_score = prob3 * (d_prob - jnp.sum(prob3 * d_prob, 1, keepdims=True))
            d_score = d_score.reshape(HEADS * 64, 128)
            if begin_at == 0:
                g_table[...] += d_score
            prob_tiles = straight_tiles(prob)
            score_tiles = straight_tiles(d_score)
            turned = turned_tiles(d_score)
            for w in range(2):
                part = slice(64 * w, 64 * w + 64)

                def mixed_of(tiles, pieces):
                    return mix([t[begin_at:] for t in tiles], pieces[0][part], pieces[1][part])

                d_query = mixed_of(turned[w], keys)
                put_window(out_here, pair, w, 0, [d * HD**-0.5 for d in d_query])
                put_window(out_here, pair, w, LANES, mixed_of(score_tiles[w], query))
                put_window(out_here, pair, w, 2 * LANES, mixed_of(prob_tiles[w], d_rows))
        if begin_at == 0:
            unit, _ = normalize(start[pl.ds(WIN * k, WIN)])
            d_all = out_here[...].reshape(BLOCK, 3 * LANES)
            g_qkv[:184] += nn(turn(unit.reshape(BLOCK, LANES)), d_all)
            g_mixed[0:1] += jnp.sum(d_all, 0, keepdims=True)

    if first_call:
        pl.when(k == 0)(lambda: work(SHIFT * WIN))
        pl.when(k > 0)(lambda: work(0))
    else:
        work(0)
    if last_call:

        @pl.when(m == pl.num_programs(0) - 1)
        def _():
            finish(
                scal[2], vec, qkv, vec_conv, vec_feed, feed, g_proj, keep, send, g_qkv, g_table,
                g_mixed, lines, proj_turned, turned_qkv,
            )


def finish(
    me, vec, qkv, vec_conv, vec_feed, feed, g_proj, keep, send, g_qkv, g_table, g_mixed, lines,
    proj_turned, turned_qkv,
):
    sums = g_mixed[...]
    cross = g_qkv[...].T
    lines[...] = vec_conv[...] + vec_feed[...]
    lines[PRE_GAIN : PRE_GAIN + 1, :LANES] = jnp.sum(cross * qkv[...], 0, keepdims=True)
    lines[PRE_SHIFT : PRE_SHIFT + 1, :LANES] = nn(sums, qkv[...])[0:1]
    lines[QV_BIAS : QV_BIAS + 1] = sums[0:1]
    turned_qkv[...] = cross * vec[PRE_GAIN : PRE_GAIN + 1, :LANES] + sums.T[:, 0:1] * vec[
        PRE_SHIFT : PRE_SHIFT + 1, :LANES
    ]
    folded = g_table[...]
    lane, u = iota((128, LANES), 0) & 63, iota((128, LANES), 1)
    pick = (u == 112 - 15 * (lane >> 3) - (lane & 7)).astype(F32)
    spread = dot(folded, pick, 1, 0, HIGHEST).reshape(HEADS, WIN, WIN, LANES)
    rel = []
    for h in range(HEADS):
        line = jnp.zeros((WIN, LANES), F32)
        for y in range(WIN):
            line = line + pltpu.roll(spread[h, y], 15 * y, 1, stride=1, stride_axis=0)
        rel.append(jnp.sum(line, 0, keepdims=True))
    rel = jnp.concatenate(rel + [jnp.zeros((REL_ROWS - HEADS, LANES), F32)], 0)
    share = CHANS // PARTS
    proj_turned[...] = g_proj[...].T
    lanes = iota((PROJ_ROWS, 128), 1)
    row = iota((VEC_ROWS, LANES), 0)
    for s in range(PARTS):

        def store(ref, s=s):
            ours = proj_turned[PROJ_ROWS * s : PROJ_ROWS * s + PROJ_ROWS]
            for m in range(3):
                at = s * 3 + m
                at = (at // 4) * LANES + (at % 4) * 48
                ref[48 * m : 48 * m + 48] = turned_qkv[at : at + 48, :128]
                piece = pltpu.roll(ours, (64 - 60 * m) % LANES, 1)[:, :128]
                ref[QKV_ROWS + 48 * m : QKV_ROWS + 48 * m + 48] = jnp.where(
                    lanes < 64, turned_qkv[at : at + 48, 128:], piece
                )
            for m in range(3):
                at = FEED_AT + FEED_ROWS * m
                ref[at : at + FEED_ROWS] = feed[s, :, 128 * m : 128 * m + 128]
            value = lines[...]

            def back(amount):
                return pltpu.roll(value, (3 * LANES - amount) % (3 * LANES), 1)[:, :LANES]

            vectors = jnp.where(
                row < QV_BIAS,
                back(share * s),
                jnp.where(
                    row == QV_BIAS, back((s // 2) * 2 * LANES + (s % 2) * 96), back(96 * s)
                ),
            )
            ref[VEC_AT : VEC_AT + VEC_ROWS] = vectors[:, :128]
            for m in range(2):
                at = REL_AT + REL_ROWS * m
                ref[at : at + REL_ROWS] = rel[:, 128 * m : 128 * m + 128]

        put_part(keep, send, s, me, store)


def image_back_kernel(parts, scal, *refs):
    d_mixed = refs[:parts]
    start, d_attn, cot, qkv, vec = refs[parts : parts + 5]
    out, ready, done = refs[-3:]
    size = scal[0]
    copies = []
    per = STEPS * WIN // parts
    for k in range(STEPS - 1):
        pieces = []
        for row in (WIN * k + SHIFT, WIN * k + WIN):
            pieces.append(d_mixed[row // per][row % per : row % per + SHIFT])
        here = slice(WIN * k + SHIFT, WIN * k + SHIFT + WIN)
        own = slice(WIN * k, WIN * k + WIN)
        unit3, scale = normalize(start[here])
        d_all = jnp.concatenate(pieces, 0).reshape(BLOCK, 3 * LANES)
        d_normed = nn(d_all, qkv[...])
        grad = (d_normed * vec[PRE_GAIN : PRE_GAIN + 1, :LANES]).reshape(unit3.shape)
        value = d_attn[here] + normalize_back(grad, unit3, scale)
        near = cot[WIN * k + SHIFT + 1 : WIN * k + SHIFT + 1 + WIN]
        mask = plain_mask(size, wrapped(scal[1] + SHIFT) + WIN * k, WIN)
        ready[own] = (mask * (near + pltpu.roll(value, SHIFT, 1)))[:, :, :CHANS]
        copies.append(pltpu.make_async_copy(ready.at[own], out.at[own], done.at[k]))
        copies[-1].start()
    for copy in copies:
        copy.wait()


def unpack_kernel(last, qkv, proj, up, down, rel, *vectors):
    share = CHANS // PARTS
    for n in range(9):
        rows = slice(16 * n, 16 * n + HALF)
        qkv[HALF * n : HALF * n + HALF, :128] = last[rows]
        second = slice(QKV_ROWS + 16 * n, QKV_ROWS + 16 * n + HALF)
        qkv[HALF * n : HALF * n + HALF, 128:] = last[second][:, : CHANS - 128]
    pieces = [last[QKV_ROWS + 48 * m : QKV_ROWS + 48 * m + 48] for m in range(3)]
    pieces = [jnp.concatenate([p, jnp.zeros_like(p)], 1) for p in pieces]
    whole = [pltpu.roll(p, (60 * m - 64) % LANES, 1) for m, p in enumerate(pieces)]
    lanes = iota((PROJ_ROWS, LANES), 1)
    value = jnp.where(lanes < 60, whole[0], jnp.where(lanes < 120, whole[1], whole[2]))
    for n in range(3):
        proj[HALF * n : HALF * n + HALF] = value[16 * n : 16 * n + HALF, :CHANS]
    tiles = [last[FEED_AT + FEED_ROWS * m : FEED_AT + FEED_ROWS * (m + 1)] for m in range(3)]
    hid = up.shape[1]
    up[...] = jnp.concatenate(tiles[:2], 1).T[:CHANS, :hid]
    below = pltpu.roll(jnp.concatenate([tiles[1], tiles[2]], 1), LANES - 64, 1)
    down[...] = below.T[:CHANS, :hid]
    lines = jnp.concatenate([last[REL_AT : REL_AT + REL_ROWS], last[REL_AT + REL_ROWS : TAIL_ROWS]], 1)
    a, b = iota((LANES, LANES), 0), iota((LANES, LANES), 1)
    rel[...] = dot(lines, (a + b == RPOS - 1).astype(F32), 1, 0, HIGHEST)[:HEADS, :RPOS]
    for n, ref in enumerate(vectors):
        if n != QV_BIAS:
            ref[...] = last[VEC_AT + n : VEC_AT + n + 1, : ref.shape[1]]
    for n in range(6):
        vectors[QV_BIAS][:, HALF * n : HALF * n + HALF] = last[
            VEC_AT + QV_BIAS : VEC_AT + QV_BIAS + 1, 16 * n : 16 * n + HALF
        ]


def blocked(rows, place):
    def make(shape):
        rest = tuple(shape[1:])
        return pl.BlockSpec((rows,) + rest, lambda m: (place(m),) + (0,) * len(rest))

    return make


def resident(shape):
    return pl.BlockSpec(memory_space=pltpu.VMEM)


def untouched(shape):
    return pl.BlockSpec(memory_space=pl.ANY)


def call(kernel, scal, ins, outs, scratch=(), after=(), limit=10, flops=0, steps=None, keep=None):
    ins = [i if isinstance(i, tuple) else (i, resident) for i in ins]
    outs = [o if callable(o[-1]) else (o, resident) for o in outs]
    ins = [(a if f is resident else pltpu.with_memory_space_constraint(a, pltpu.HBM), f) for a, f in ins]
    ins += [(a, untouched) for a in after]
    first = [] if scal is None else [scal]
    specs = [pl.BlockSpec(memory_space=pltpu.SMEM)] * len(first) + [f(a.shape) for a, f in ins]
    size = sum(4 * a.size for a, f in ins if f is not untouched)
    size += sum(4 * functools.reduce(lambda p, q: p * q, s) for s, _ in outs)
    return pl.pallas_call(
        kernel,
        grid=() if steps is None else (steps,),
        in_specs=specs,
        out_specs=[f(s) for s, f in outs],
        scratch_shapes=[pltpu.VMEM(s, F32) if isinstance(s, tuple) else s for s in scratch],
        out_shape=[
            jax.ShapeDtypeStruct(tuple(s), F32) if f is resident else pltpu.HBM(tuple(s), F32)
            for s, f in outs
        ],
        input_output_aliases={i + len(first): o for i, o in (keep or {}).items()},
        compiler_params=pltpu.CompilerParams(vmem_limit_bytes=limit * MIB),
        cost_estimate=pl.CostEstimate(flops=flops, bytes_accessed=size, transcendentals=0),
    )(*first, *[a for a, _ in ins])


def body(
    images,
    item_sizes,
    cotangent,
    pre_gain,
    pre_shift,
    qkv_weight,
    qv_bias,
    rel_table,
    proj_weight,
    proj_bias,
    mid_gain,
    mid_shift,
    up_weight,
    up_bias,
    down_weight,
    down_bias,
    conv_kernel,
    conv_bias,
):
    height, breadth = images.shape[1:3]
    me = lax.axis_index("tp")
    strip = height + 2 * SHIFT
    image = images[0]
    cot = cotangent[0].transpose(2, 0, 1)
    share = CHANS // PARTS

    def frame(lanes):
        return (strip, breadth, lanes)

    vectors = [pre_gain, pre_shift, proj_bias, mid_gain, mid_shift, down_bias, conv_bias, qv_bias, up_bias]
    at_once = lambda shape: pl.BlockSpec(tuple(shape), lambda m: (0,) * len(shape))
    mine1, mine2 = call(
        pack_kernel,
        None,
        [(a, at_once) for a in (qkv_weight.T, proj_weight, up_weight, down_weight.T, *[v[None] for v in vectors])],
        [(QKV_ROWS + PROJ_ROWS + VEC_ROWS, LANES), (2 * FEED_ROWS, LANES)],
        limit=8,
        steps=1,
    )
    mine3 = conv_kernel.transpose(0, 1, 3, 2).reshape(9, share, CHANS)
    scal = jnp.stack([item_sizes[0], (me * height + IMG - SHIFT) % IMG, me]).astype(jnp.int32)
    x_first, x_last = tie((image[:SHIFT], image[-SHIFT:]), mine1)
    x_above = from_behind(x_last, "tp", 1)
    x_below = from_behind(x_first, "tp", -1)
    all1 = gather_tp(mine1, x_first, x_last)

    qkv, proj, vec, table = call(
        prepare_kernel,
        scal,
        [*all1, rel_table.T],
        [(3 * LANES, LANES), (LANES, LANES), (VEC_ROWS, 3 * LANES), (HEADS * 64, 128)],
        [(VEC_ROWS, 3 * LANES)],
        limit=8,
        flops=10**8,
    )

    def attend(edges, arrays, old):
        place = (lambda m: m * (STEPS - 1)) if edges else (lambda m: m + 1)
        ins = [*arrays, qkv, vec, table, proj]
        keep = {len(ins) + n: n for n in range(len(old))}
        ins += [(o, untouched) for o in old[:2]] + list(old[2:])
        return call(
            functools.partial(attend_kernel, edges),
            scal,
            ins,
            [
                (frame(3 * LANES), blocked(WIN, place)),
                ((STEPS, PAIRS, HEADS * 64, 128), blocked(1, place)),
                frame(LANES),
                frame(LANES),
                frame(LANES),
            ],
            [(WIN, breadth, LANES)],
            flops=5 * 10**9,
            limit=16,
            steps=2,
            keep=keep,
        )

    old = attend(False, [image], [])
    all2 = gather_tp(mine2, old[2])
    c_first, c_last = call(
        rims_kernel, None, [cot], [(SHIFT + 1, breadth, CHANS)] * 2, after=[old[2]], limit=8
    )
    c_above = from_behind(c_last, "tp", 1)
    c_below = from_behind(c_first, "tp", -1)
    mixed, probs, attended, after_attn, start = attend(True, [x_above, image, x_below], old)
    all3 = gather_tp(tie(mine3, old[2]), after_attn)
    pre, after_mlp, up, down = call(
        feed_kernel,
        scal,
        [after_attn, vec, *all2],
        [frame(HID), frame(LANES), (HID, LANES), (HID, LANES)],
        flops=5 * 10**9,
    )
    d_mid, conv_keep, conv_send, vec_conv, wide, cot_rows = call(
        conv_back_kernel,
        scal,
        [after_mlp, cot, c_above, c_below, *all3],
        [
            frame(LANES),
            (2, 9 * CONV_ROWS, LANES),
            (2, 9 * CONV_ROWS, LANES),
            (VEC_ROWS, 3 * LANES),
            (3, LANES, 3 * LANES),
            (strip + 2, breadth, LANES),
        ],
        [
            (WIN + 2, breadth, 3 * LANES),
            (3, 3 * LANES, LANES),
            (PARTS, 9, share, CHANS),
            (3, LANES, 3 * LANES),
            (9, CHANS, LANES),
        ],
        flops=2 * 10**10,
        limit=20,
    )
    got_a = lax.ppermute(conv_send, "tp", flip("tp", 1))
    d_attn, d_att, g_feed, g_proj, vec_feed = call(
        feed_back_kernel,
        scal,
        [d_mid, after_attn, pre, attended, up, down, proj, vec],
        [frame(LANES), frame(LANES), (PARTS, FEED_ROWS, HID), (LANES, LANES), (VEC_ROWS, 3 * LANES)],
        [(LANES, HID), (LANES, HID)],
        after=[conv_send],
        flops=10**10,
        limit=14,
    )
    got_a = tie(got_a, d_att)
    send_b = conv_keep[1] + got_a[1]
    got_b = lax.ppermute(send_b, "tp", flip("tp", 2))

    g_shapes = [(LANES, 3 * LANES), (HEADS * 64, 128), (8, 3 * LANES)]

    def attend_back(begin, end, old, after):
        place = lambda m: m + begin
        ins = [start, (mixed, blocked(WIN, place)), (probs, blocked(1, place)), d_att]
        outs = [((end - begin) * WIN, breadth, 3 * LANES)]
        scratch = []
        if end == STEPS:
            ins += [vec, qkv, vec_conv, vec_feed, g_feed, g_proj]
            outs += [(2, TAIL_ROWS, 128)] * 2
            scratch = g_shapes + [(VEC_ROWS, 3 * LANES), (LANES, LANES), (3 * LANES, LANES)]
        else:
            outs += g_shapes
        return call(
            functools.partial(attend_back_kernel, begin, end),
            scal,
            ins + list(old),
            outs,
            scratch,
            after=after,
            flops=5 * 10**9 * (end - begin),
            limit=16 if begin else 20,
            steps=end - begin,
        )

    d_mixed0, *sums = attend_back(0, 2, [], [send_b])
    got_b = tie(got_b, d_mixed0)
    held = conv_keep[0] + got_a[0] + got_b
    bits = dp_bits()
    d_mixed1, tail_keep, tail_send = attend_back(2, STEPS, sums, [held])
    held = dp_halve(held, bits[0], d_mixed1)

    blocks = height // WIN

    def convolve(k, old, after):
        ins = [after_mlp, start, wide, vec]
        return call(
            functools.partial(conv_kernel_body, k),
            scal,
            ins + [(o, untouched) for o in old],
            [((height, breadth, CHANS), untouched)],
            [(WIN + 2, breadth, 3 * LANES), (WIN, breadth, CHANS), pltpu.SemaphoreType.DMA((1,))],
            after=after,
            flops=4 * 10**9,
            keep={len(ins): 0} if old else None,
        )[0]

    last_a = lax.ppermute(tail_send, "tp", flip("tp", 1))
    block_out = convolve(0, [], [tail_send, held])
    last_a = tie(last_a, block_out)
    last_send = tail_keep[1] + last_a[1]
    last_b = lax.ppermute(last_send, "tp", flip("tp", 2))
    (grad_images,) = call(
        functools.partial(image_back_kernel, 2),
        scal,
        [d_mixed0, d_mixed1, start, d_attn, cot_rows, qkv, vec],
        [((height, breadth, CHANS), untouched)],
        [(height, breadth, CHANS), pltpu.SemaphoreType.DMA((STEPS - 1,))],
        after=[last_send],
        flops=4 * 10**9,
    )
    if len(bits) > 1:
        held = dp_add(held, bits[1], grad_images)
    last_b = tie(last_b, grad_images)
    last = tail_keep[0] + last_a[0] + last_b
    for k in range(1, blocks):
        if k == 1:
            block_out = convolve(k, [block_out], [last])
            last = dp_halve(last, bits[0], block_out)
        elif k <= len(bits):
            block_out = convolve(k, [block_out], [last])
            last = dp_add(last, bits[k - 1], block_out)
    grad_images = tie(grad_images, last)
    for bit in bits[2:]:
        held = dp_add(held, bit, grad_images)
    for bit in bits[blocks - 1 :]:
        last = dp_add(last, bit)
    held = dp_join(held, bits[0], last)
    block_out = tie(block_out, last)
    last = dp_join(last, bits[0])

    conv = held.reshape(3, 3, CONV_ROWS, LANES)[:, :, :share, :CHANS]
    hid = up_weight.shape[1]
    g_qkv, g_proj, g_up, g_down, g_rel, *g_vec = call(
        unpack_kernel,
        None,
        [last],
        [(qkv_weight.shape[1], CHANS), (share, CHANS), (CHANS, hid), (CHANS, hid), (HEADS, RPOS)] + [(1, v.shape[0]) for v in vectors],
        limit=8,
    )

    g_vec = [g[0] for g in g_vec]
    return (
        block_out[None],
        grad_images[None],
        g_vec[PRE_GAIN],
        g_vec[PRE_SHIFT],
        g_qkv.T,
        g_vec[QV_BIAS],
        g_rel.T,
        g_proj,
        g_vec[PROJ_BIAS],
        g_vec[MID_GAIN],
        g_vec[MID_SHIFT],
        g_up,
        g_vec[UP_BIAS],
        g_down.T,
        g_vec[DOWN_BIAS],
        conv.transpose(0, 1, 3, 2),
        g_vec[CONV_BIAS],
    )


def solution(mesh):
    placed = (
        P("dp", "tp", None, None),
        P("dp"),
        P("dp", "tp", None, None),
        P("tp"),
        P("tp"),
        P(None, "tp"),
        P("tp"),
        P(),
        P("tp", None),
        P("tp"),
        P("tp"),
        P("tp"),
        P(None, "tp"),
        P("tp"),
        P("tp", None),
        P("tp"),
        P(None, None, None, "tp"),
        P("tp"),
    )
    return jax.shard_map(
        body,
        mesh=mesh,
        in_specs=placed,
        out_specs=(
            P("dp", "tp", None, None),
            P("dp", "tp", None, None),
            P("tp"),
            P("tp"),
            P(None, "tp"),
            P("tp"),
            P(),
            P("tp", None),
            P("tp"),
            P("tp"),
            P("tp"),
            P(None, "tp"),
            P("tp"),
            P("tp", None),
            P("tp"),
            P(None, None, None, "tp"),
            P("tp"),
        ),
        check_vma=False,
    )
```

```python
import functools

import jax
import jax.numpy as jnp
from jax import lax
from jax.experimental import pallas as pl
from jax.experimental.pallas import tpu as pltpu
from jax.sharding import PartitionSpec as P

WIN = 8
IMG = 96
SHIFT = 4
EPSILON = 1e-05
NEG_FILL = -1e30
CHANS = 180
HEADS = 6
HD = 30
HALF = 15
SLOT = 32
LANES = 256
INNER = 192
HID = 384
RPOS = 225
HIGH = lax.Precision.HIGH
HIGHEST = lax.Precision.HIGHEST
F32 = jnp.float32
BF16 = jnp.bfloat16
BLOCK = WIN * IMG
PAIRS = IMG // WIN // 2
PARTS = 4
MIB = 2**20
STEPS = 4

QKV_ROWS, PROJ_ROWS, VEC_ROWS = 144, 48, 16
FEED_ROWS = 96
CONV_ROWS = 48
REL_ROWS = 8
FEED_AT = 2 * QKV_ROWS
VEC_AT = FEED_AT + 3 * FEED_ROWS
REL_AT = VEC_AT + VEC_ROWS
TAIL_ROWS = REL_AT + 2 * REL_ROWS
PRE_GAIN, PRE_SHIFT, PROJ_BIAS, MID_GAIN, MID_SHIFT, DOWN_BIAS, CONV_BIAS, QV_BIAS, UP_BIAS = range(9)


def flip(axis, bit):
    return [(i, i ^ bit) for i in range(lax.axis_size(axis))]


def from_behind(block, axis, distance):
    n = lax.axis_size(axis)
    return lax.ppermute(block, axis, [((i - distance) % n, i) for i in range(n)])


def gather_tp(block, *others):
    got = {0: block}
    for bit in (2, 1):
        if others and bit == 1:
            got[2] = tie(got[2], *others)
        got.update({k | bit: lax.ppermute(b, "tp", flip("tp", bit)) for k, b in list(got.items())})
    return [got[k] for k in range(PARTS)]


def tie(value, *others):
    return lax.optimization_barrier((value, others))[0]


def dp_bits():
    n = lax.axis_size("dp")
    return [1 << b for b in range(n.bit_length() - 1)]


def dp_halve(held, bit, *others):
    half = held.shape[0] // 2
    odd = (lax.axis_index("dp") & bit) != 0
    send = jnp.where(odd, held[:half], held[half:])
    got = lax.ppermute(send, "dp", flip("dp", bit))
    if others:
        got = tie(got, *others)
    return jnp.where(odd, held[half:], held[:half]) + got


def dp_join(held, bit, *others):
    odd = (lax.axis_index("dp") & bit) != 0
    got = lax.ppermute(held, "dp", flip("dp", bit))
    if others:
        got = tie(got, *others)
    return jnp.concatenate([jnp.where(odd, got, held), jnp.where(odd, held, got)], 0)


def dp_add(held, bit, *others):
    got = lax.ppermute(held, "dp", flip("dp", bit))
    if others:
        got = tie(got, *others)
    return held + got


def dot(left, right, left_dim, right_dim, precision=None):
    return lax.dot_general(
        left,
        right,
        (((left_dim,), (right_dim,)), ((), ())),
        precision=precision,
        preferred_element_type=F32,
    )


def nn(left, right):
    return dot(left, right, 1, 0, HIGH)


def nt(left, right):
    return dot(left, right, 1, 1, HIGH)


def turn(value):
    return value.T[:184]


def iota(shape, dim):
    return lax.broadcasted_iota(jnp.int32, shape, dim)


def wrapped(position):
    return jnp.where(position >= IMG, position - IMG, position)


def frame_mask(size, first, rows=WIN):
    shape = (rows, IMG, LANES)
    row = wrapped(first + iota(shape, 0))
    col = wrapped(iota(shape, 1) + SHIFT)
    return ((row < size) & (col < size) & (iota(shape, 2) < CHANS)).astype(F32)


def plain_mask(size, first, rows):
    shape = (rows, IMG, LANES)
    row = wrapped(first + iota(shape, 0))
    return ((row < size) & (iota(shape, 1) < size) & (iota(shape, 2) < CHANS)).astype(F32)


def is_channel(shape):
    return iota(shape, len(shape) - 1) < CHANS


def mean(value):
    return jnp.sum(value, axis=-1, keepdims=True) * (1.0 / CHANS)


def normalize(value):
    centre = jnp.where(is_channel(value.shape), value - mean(value), 0.0)
    scale = lax.rsqrt(mean(centre * centre) + EPSILON)
    return centre * scale, scale


def normalize_back(grad, unit, scale):
    value = scale * (grad - mean(grad) - unit * mean(grad * unit))
    return jnp.where(is_channel(value.shape), value, 0.0)


def upper(value):
    return value.astype(BF16).astype(F32)


def parted(value):
    high = upper(value)
    return jnp.where(iota(value.shape, 1) < 64, high, value - high)


def doubled(first, second):
    left = iota(first.shape, 1) < 64
    turned0 = pltpu.roll(first, 64, 1)
    turned1 = pltpu.roll(second, 64, 1)
    return (
        jnp.where(left, first, turned0),
        jnp.where(left, turned0, first),
        jnp.where(left, second, turned1),
    )


def head_products(rows, cols):
    lanes = iota((128, 128), 1)
    even = (lanes & 63) < SLOT
    outs = []
    for moving, fixed in zip(doubled(*rows), doubled(*cols)):
        high = fixed.astype(BF16)
        low = (fixed - high.astype(F32)).astype(BF16)
        held = jnp.concatenate([high, low], 1)
        pieces = parted(moving)
        ones = jnp.where(even, pieces, 0.0).astype(BF16)
        twos = jnp.where(even, 0.0, pieces).astype(BF16)
        both = []
        for w in range(2):
            part = slice(64 * w, 64 * w + 64)
            stream = jnp.concatenate([ones[part], twos[part]], 0)
            both.append(dot(jnp.concatenate([stream, stream], 1), held, 1, 1))
        outs.append(jnp.where(lanes < 64, both[0], both[1]))
    return jnp.concatenate(outs, 0)


def mix(tiles, first, second):
    n = tiles[0].shape[0]
    lanes = iota((n, 128), 1)

    def product(part, block):
        high = block.astype(BF16)
        low = (block - high.astype(F32)).astype(BF16)
        held = jnp.concatenate([high, high, low, low], 0)
        stream = jnp.concatenate(part, 0)
        return dot(jnp.concatenate([stream, stream], 1), held, 1, 0)

    a = product(tiles[:4], first)
    b = product(tiles[4:], second)
    one = jnp.where(
        lanes < 64,
        jnp.where(lanes < 32, a[:n], a[n : 2 * n]),
        jnp.where(lanes < 96, a[2 * n : 3 * n], a[3 * n :]),
    )
    two = jnp.where(lanes < 32, b[:n], b[n:])
    return one, two


def straight_tiles(table):
    left = iota(table.shape, 1) < 64
    turned = pltpu.roll(table, 64, 1)
    outs = []
    for w in range(2):
        one = jnp.where(left, table, turned) if w == 0 else jnp.where(left, turned, table)
        both = parted(one).astype(BF16)
        outs.append([both[64 * h : 64 * h + 64] for h in range(HEADS)])
    return outs


def turned_tiles(table):
    high = upper(table)
    low = table - high
    outs = [[], []]
    for h in range(HEADS):
        part = slice(64 * h, 64 * h + 64)
        both = jnp.concatenate([high[part], low[part]], 0).astype(BF16).T
        for w in range(2):
            outs[w].append(both[64 * w : 64 * w + 64])
    return outs


def window_pair(ref, pair, start):
    cols = pl.ds(pl.multiple_of(pair * 2 * WIN, 2 * WIN), 2 * WIN)
    tiles = []
    for tile in range(2):
        block = ref[:, cols, start + 128 * tile : start + 128 * tile + 128]
        tiles.append(
            jnp.concatenate(
                [block[:, :WIN].reshape(64, 128), block[:, WIN:].reshape(64, 128)], 0
            )
        )
    return tiles


def put_window(ref, pair, w, start, tiles):
    cols = pl.ds(pl.multiple_of(pair * 2 * WIN + w * WIN, WIN), WIN)
    rows = tiles[0].shape[0] // WIN
    for tile in range(2):
        ref[WIN - rows :, cols, start + 128 * tile : start + 128 * tile + 128] = tiles[
            tile
        ].reshape(rows, WIN, 128)


def pair_fill(size, first, pair):
    shape = (64, 128)
    j, lane = iota(shape, 0), iota(shape, 1)
    i, window = lane & 63, 2 * pair + (lane >> 6)
    rows = wrapped(first + (j >> 3))
    cols = wrapped(window * WIN + (j & 7) + SHIFT)
    apart_rows = (first == IMG - WIN + SHIFT) & ((j >> 5) != (i >> 5))
    apart_cols = (window == IMG // WIN - 1) & (((j & 7) >> 2) != ((i & 7) >> 2))
    keep = (rows < size) & (cols < size)
    return jnp.where(apart_rows | apart_cols | jnp.logical_not(keep), NEG_FILL, 0.0)


def block_first(scal, k):
    return wrapped(scal[1] + WIN * k)


def block_of(ref, k):
    return ref.at[pl.ds(WIN * k, WIN)]


def put_part(keep, send, part, me, store):
    place = part ^ me
    pl.when((place & 1) == 0)(lambda: store(keep.at[place >> 1]))
    pl.when((place & 1) == 1)(lambda: store(send.at[place >> 1]))


def gelu_parts(hidden):
    return 0.5 * (1.0 + lax.erf(hidden * 0.5**0.5))


def pack_kernel(qkv, proj, up, down, *refs):
    vectors, (first, second) = refs[:9], refs[9:]
    first[...] = jnp.zeros_like(first)
    second[...] = jnp.zeros_like(second)
    for n in range(9):
        first[16 * n : 16 * n + HALF, :CHANS] = qkv[HALF * n : HALF * n + HALF]
    for n in range(3):
        at = QKV_ROWS + 16 * n
        first[at : at + HALF, :CHANS] = proj[HALF * n : HALF * n + HALF]
    share, hid = CHANS // PARTS, up.shape[1]
    second[:hid, :CHANS] = up[...].T
    second[FEED_ROWS : FEED_ROWS + hid, :CHANS] = down[...].T
    at = QKV_ROWS + PROJ_ROWS
    for n, ref in enumerate(vectors):
        if n != QV_BIAS:
            first[at + n : at + n + 1, : ref.shape[1]] = ref[...]
    for n in range(6):
        first[at + QV_BIAS : at + QV_BIAS + 1, 16 * n : 16 * n + HALF] = vectors[QV_BIAS][
            :, HALF * n : HALF * n + HALF
        ]


def rims_kernel(cot, *refs):
    first, last = refs[-2:]
    height, n = cot.shape[1], first.shape[0]
    for row in range(n):
        first[row] = cot[:, row, :].T
        last[row] = cot[:, height - n + row, :].T


def prepare_kernel(scal, p0, p1, p2, p3, rel, qkv, proj, vec, table, spread):
    me = scal[2]
    for ref in (qkv, vec, spread):
        ref[...] = jnp.zeros_like(ref)
    proj[INNER:] = jnp.zeros_like(proj[INNER:])
    lanes = iota((VEC_ROWS, 3 * LANES), 1)
    row = iota((VEC_ROWS, 3 * LANES), 0)
    for k, piece in enumerate((p0, p1, p2, p3)):
        owner = me ^ k
        for m in range(3):
            at = owner * 3 + m
            start = pl.multiple_of((at // 4) * LANES + (at % 4) * 48, 16)
            qkv[pl.ds(start, 48)] = piece[48 * m : 48 * m + 48]
        proj[pl.ds(pl.multiple_of(owner * PROJ_ROWS, 16), PROJ_ROWS)] = piece[
            QKV_ROWS : QKV_ROWS + PROJ_ROWS
        ]
        spread[:VEC_ROWS, :LANES] = piece[QKV_ROWS + PROJ_ROWS :]
        value = spread[:VEC_ROWS]
        vec[...] += jnp.where(
            row < QV_BIAS,
            pltpu.roll(value, owner * (CHANS // PARTS), 1),
            jnp.where(
                row == QV_BIAS,
                pltpu.roll(value, (owner // 2) * 2 * LANES + (owner % 2) * 96, 1),
                pltpu.roll(value, owner * 96, 1),
            ),
        )
    spread[...] = jnp.zeros_like(spread)
    spread[:HEADS, :RPOS] = rel[...]
    pieces = []
    for h in range(HEADS):
        line = jnp.broadcast_to(spread[h : h + 1, :LANES], (WIN, LANES))
        for y in range(WIN):
            pieces.append(
                pltpu.roll(line, (15 * y - 112) % LANES, 1, stride=1, stride_axis=0)
            )
    lines = jnp.concatenate(pieces, 0)
    u, lane = iota((LANES, 128), 0), iota((LANES, 128), 1) & 63
    pick = (u == (lane >> 3) * 15 + (lane & 7)).astype(F32)
    table[...] = dot(lines, pick, 1, 0, HIGHEST)


def attend_kernel(edges, scal, *refs):
    m = pl.program_id(0)
    if edges:
        above, image, below, qkv, vec, table, proj = refs[:7]
        k = m * (STEPS - 1)
    else:
        image, qkv, vec, table, proj = refs[:5]
        k = m + 1
    mixed, probs, attended, after, start, wide = refs[-6:]
    height = image.shape[0]

    @pl.when(m == 0)
    def _():
        wide[...] = jnp.zeros_like(wide)
        if edges:
            wide[:SHIFT, :, :CHANS] = above[...]
            wide[SHIFT:, :, :CHANS] = image[:SHIFT]

    if edges:

        @pl.when(m == 1)
        def _():
            wide[:SHIFT, :, :CHANS] = image[height - SHIFT :]
            wide[SHIFT:, :, :CHANS] = below[...]

    else:
        wide[:, :, :CHANS] = image[pl.ds(WIN * k - SHIFT, WIN)]
    size, first = scal[0], block_first(scal, k)
    rows = pl.ds(WIN * k, WIN)
    mask = frame_mask(size, first)
    begin = mask * pltpu.roll(wide[...], IMG - SHIFT, 1)
    start[rows] = begin
    unit, _ = normalize(begin)
    normed = unit * vec[PRE_GAIN, :LANES] + vec[PRE_SHIFT, :LANES]
    mixed[...] = (
        nt(normed.reshape(BLOCK, LANES), qkv[...]) + vec[QV_BIAS : QV_BIAS + 1]
    ).reshape(WIN, IMG, 3 * LANES)
    out_here = block_of(attended, k)
    for pair in range(PAIRS):
        query = window_pair(mixed, pair, 0)
        keys = window_pair(mixed, pair, LANES)
        values = window_pair(mixed, pair, 2 * LANES)
        scores = head_products(keys, [q * HD**-0.5 for q in query]) + table[...]
        scores = scores.reshape(HEADS, 64, 128) + pair_fill(size, first, pair)[None]
        scores = jnp.exp(scores - jnp.max(scores, 1, keepdims=True))
        prob = (scores * (1.0 / jnp.sum(scores, 1, keepdims=True))).reshape(HEADS * 64, 128)
        probs[0, pair] = prob
        for w, tiles in enumerate(turned_tiles(prob)):
            part = slice(64 * w, 64 * w + 64)
            put_window(out_here, pair, w, 0, mix(tiles, values[0][part], values[1][part]))
    out = nn(out_here[...].reshape(BLOCK, LANES), proj[...]) + vec[PROJ_BIAS : PROJ_BIAS + 1, :LANES]
    after[rows] = begin + mask * out.reshape(WIN, IMG, LANES)


def feed_kernel(scal, value, vec, p0, p1, p2, p3, pre, after, up, down):
    for k, piece in enumerate((p0, p1, p2, p3)):
        rows = pl.ds(pl.multiple_of((scal[2] ^ k) * FEED_ROWS, 32), FEED_ROWS)
        up[rows] = piece[:FEED_ROWS]
        down[rows] = piece[FEED_ROWS:]

    def block(k, carry):
        rows = pl.ds(WIN * k, WIN)
        mask = frame_mask(scal[0], block_first(scal, k))
        here = value[rows]
        unit, _ = normalize(here)
        normed = unit * vec[MID_GAIN, :LANES] + vec[MID_SHIFT, :LANES]
        hidden = nt(normed.reshape(BLOCK, LANES), up[...]) + vec[UP_BIAS : UP_BIAS + 1, :HID]
        pre[rows] = hidden.reshape(WIN, IMG, HID)
        act = hidden * gelu_parts(hidden)
        out = nn(act, down[...]) + vec[DOWN_BIAS : DOWN_BIAS + 1, :LANES]
        after[rows] = here + mask * out.reshape(here.shape)
        return carry

    lax.fori_loop(0, STEPS, block, 0)


def put_shifted(ref, value):
    cols = iota(value.shape, 1)
    ref[:, :, LANES : 2 * LANES] = value
    ref[:, :, :LANES] = jnp.where(cols == 0, 0.0, pltpu.roll(value, 1, 1))
    ref[:, :, 2 * LANES :] = jnp.where(cols == IMG - 1, 0.0, pltpu.roll(value, IMG - 1, 1))


def conv_back_kernel(
    scal,
    after,
    cot,
    cot_above,
    cot_below,
    p0,
    p1,
    p2,
    p3,
    d_mid,
    keep,
    send,
    vec,
    wide,
    padded,
    d_spread,
    tall,
    gathered,
    grad,
    taps,
):
    height = cot.shape[1]
    share = CHANS // PARTS
    size, base, me = scal[0], scal[1], scal[2]
    for ref in (wide, tall, padded, grad, vec):
        ref[...] = jnp.zeros_like(ref)
    for n, piece in enumerate((p0, p1, p2, p3)):
        gathered[me ^ n] = piece[...]
    for s in range(PARTS):
        rows = slice(share * s, share * s + share)
        for i in range(3):
            for j in range(3):
                part = gathered[s, 3 * i + j]
                wide[i, rows, LANES * j : LANES * j + CHANS] = part
                at = LANES * (2 - j) + share * s
                tall[i, at : at + share, :CHANS] = part
    edge = SHIFT + 1
    padded[:edge, :, :CHANS] = cot_above[...]
    for row in range(height):
        padded[edge + row, :, :CHANS] = cot[:, row, :].T
    padded[edge + height :, :, :CHANS] = cot_below[...]
    shape = (WIN, IMG, LANES)

    def block(k, own):
        tall_shape = (WIN + 2, IMG, LANES)
        row = wrapped(wrapped(wrapped(base + IMG - 1 + WIN * k) + iota(tall_shape, 0)))
        inside = (row < size) & (iota(tall_shape, 1) < size)
        put_shifted(d_spread, jnp.where(inside, padded[pl.ds(WIN * k, WIN + 2)], 0.0))
        rows = wrapped(wrapped(base + WIN * k) + iota(shape, 0))
        rows_all = wrapped(wrapped(base + WIN * k) + iota((WIN, IMG, 3 * LANES), 0))
        total = jnp.zeros(shape, F32)
        here = pltpu.roll(after[pl.ds(WIN * k, WIN)], SHIFT, 1)[own]
        turned = turn(here.reshape(-1, LANES))
        for i in range(3):
            around = d_spread[2 - i : 2 - i + WIN]
            part = nn(around.reshape(BLOCK, 3 * LANES), tall[i]).reshape(shape)
            if i == 0:
                part = jnp.where(rows == IMG - 1, 0.0, part)
                around = jnp.where(rows_all == IMG - 1, 0.0, around)
            if i == 2:
                part = jnp.where(rows == 0, 0.0, part)
                around = jnp.where(rows_all == 0, 0.0, around)
            total = total + part
            grad[i, :184] += nn(turned, around[own].reshape(-1, 3 * LANES))
        d_mid[pl.ds(WIN * k, WIN)] = pltpu.roll(total, IMG - SHIFT, 1)
        centre = d_spread[1 : 1 + WIN, :, LANES : 2 * LANES][own]
        vec[CONV_BIAS : CONV_BIAS + 1, :LANES] += jnp.sum(
            centre.reshape(-1, LANES), 0, keepdims=True
        )

    block(0, slice(SHIFT, WIN))

    def inner(k, carry):
        block(k, slice(0, WIN))
        return carry

    lax.fori_loop(1, STEPS - 1, inner, 0)
    block(STEPS - 1, slice(0, SHIFT))
    for i in range(3):
        for j in range(3):
            taps[3 * i + j] = grad[i, :, LANES * (2 - j) : LANES * (3 - j)].T[:CHANS]
    for s in range(PARTS):

        def store(ref, s=s):
            for n in range(9):
                ref[CONV_ROWS * n : CONV_ROWS * n + share] = taps[n, share * s : share * s + share]

        put_part(keep, send, s, me, store)


def conv_kernel_body(k, blocks, scal, after, start, wide, vec, *refs):
    copies = []
    if k == blocks - 1:
        out, spread, ready, done = refs[-4:]
        for n in range(k):
            copies.append(
                pltpu.make_async_copy(refs[n], out.at[WIN * n : WIN * n + WIN], done.at[n])
            )
            copies[-1].start()
    else:
        ready, spread = refs[-2:]
    tall_shape = (WIN + 2, IMG, LANES)
    first = wrapped(scal[1] + SHIFT) + WIN * k
    row = first - 1 + iota(tall_shape, 0)
    value = pltpu.roll(after[pl.ds(WIN * k + SHIFT - 1, WIN + 2)], SHIFT, 1)
    put_shifted(spread, jnp.where((row < 0) | (row >= IMG), 0.0, value))
    total = jnp.zeros((BLOCK, LANES), F32)
    for i in range(3):
        total = total + nt(spread[i : i + WIN].reshape(BLOCK, 3 * LANES), wide[i])
    mask = plain_mask(scal[0], first, WIN)
    conv = (total + vec[CONV_BIAS : CONV_BIAS + 1, :LANES]).reshape(mask.shape)
    here = pltpu.roll(start[pl.ds(WIN * k + SHIFT, WIN)], SHIFT, 1)
    ready[...] = (here + mask * conv)[:, :, :CHANS]
    if k == blocks - 1:
        copies.append(pltpu.make_async_copy(ready, out.at[WIN * k : WIN * k + WIN], done.at[k]))
        copies[-1].start()
    for copy in copies:
        copy.wait()


def feed_back_kernel(
    scal, d_mid, value, pre, attended, up, down, proj, vec, *refs
):
    d_attn, d_att, grads, g_proj, g_vec, g_up, g_down = refs[-7:]
    for ref in (g_up, g_down, g_proj, g_vec):
        ref[...] = jnp.zeros_like(ref)
    size = scal[0]

    def block(k, rows, part, counted):
        here = pl.ds(WIN * k, WIN)
        mask = frame_mask(size, block_first(scal, k))
        mid = d_mid[here]
        d_ff = (mask * mid).reshape(BLOCK, LANES)
        hidden = pre[here].reshape(BLOCK, HID)
        phi = gelu_parts(hidden)
        act = hidden * phi
        slope = phi + hidden * (jnp.exp(-0.5 * hidden * hidden) * 0.3989422804014327)
        d_pre = nt(d_ff, down[...]) * slope
        d_normed = nn(d_pre, up[...])
        unit3, scale = normalize(value[here])
        unit = unit3.reshape(BLOCK, LANES)
        gain = vec[MID_GAIN : MID_GAIN + 1, :LANES]
        normed = unit * gain + vec[MID_SHIFT : MID_SHIFT + 1, :LANES]
        grad = (d_normed * gain).reshape(mid.shape)
        d_out = mid + normalize_back(grad, unit3, scale)
        d_attn[here] = d_out
        d_proj = (mask * d_out).reshape(BLOCK, LANES)
        d_att[here] = nt(d_proj, proj[...]).reshape(mid.shape)
        d_ff_own, d_pre_own, d_normed_own = d_ff[part], d_pre[part], d_normed[part]
        g_down[:184] += nn(turn(d_ff_own), act[part])
        g_up[:184] += nn(turn(normed[part]), d_pre_own)
        g_vec[UP_BIAS : UP_BIAS + 1, :HID] += jnp.sum(d_pre_own, 0, keepdims=True)
        for at, v in (
            (MID_GAIN, d_normed_own * unit[part]),
            (MID_SHIFT, d_normed_own),
            (DOWN_BIAS, d_ff_own),
        ):
            g_vec[at : at + 1, :LANES] += jnp.sum(v, 0, keepdims=True)
        if counted:
            g_proj[:184] += nn(turn(d_proj), attended[here].reshape(BLOCK, LANES))
            g_vec[PROJ_BIAS : PROJ_BIAS + 1, :LANES] += jnp.sum(d_proj, 0, keepdims=True)

    block(0, None, slice(SHIFT * IMG, BLOCK), False)

    def inner(k, carry):
        block(k, None, slice(0, BLOCK), True)
        return carry

    lax.fori_loop(1, STEPS - 1, inner, 0)
    block(STEPS - 1, None, slice(0, SHIFT * IMG), True)
    for s in range(PARTS):
        rows = slice(FEED_ROWS * s, FEED_ROWS * s + FEED_ROWS)
        grads[s, :, :] = jnp.zeros_like(grads[s])
    turned_up = g_up[...].T
    turned_down = g_down[...].T
    for s in range(PARTS):
        rows = slice(FEED_ROWS * s, FEED_ROWS * s + FEED_ROWS)
        below = pltpu.roll(turned_down[rows], 64, 1)
        lanes = iota((FEED_ROWS, 128), 1)
        grads[s, :, :128] = turned_up[rows, :128]
        grads[s, :, 128:256] = jnp.where(lanes < 64, turned_up[rows, 128:], below[:, :128])
        grads[s, :, 256:] = below[:, 128:]


def attend_back_kernel(begin, end, scal, start, mixed, probs, d_att, *refs):
    refs = list(refs)
    first_call, last_call = begin == 0, end == STEPS
    if last_call:
        vec, qkv, vec_conv, vec_feed, feed, g_proj = refs[:6]
        d_mixed, keep, send, g_qkv, g_table, g_mixed, lines, proj_turned, turned_qkv = refs[-9:]
    else:
        d_mixed, g_qkv, g_table, g_mixed = refs[-4:]
    before = refs[6 if last_call else 0 :][:3]
    m = pl.program_id(0)
    k = m + begin

    @pl.when(m == 0)
    def _():
        for n, ref in enumerate((g_qkv, g_table, g_mixed)):
            ref[...] = jnp.zeros_like(ref) if first_call else before[n][...]

    att_here = block_of(d_att, k)
    out_here = block_of(d_mixed, m)

    def work(begin_at):
        for pair in range(PAIRS):
            query = [q * HD**-0.5 for q in window_pair(mixed, pair, 0)]
            keys = window_pair(mixed, pair, LANES)
            values = window_pair(mixed, pair, 2 * LANES)
            d_rows = window_pair(att_here, pair, 0)
            prob = probs[0, pair]
            d_prob = head_products(values, d_rows).reshape(HEADS, 64, 128)
            prob3 = prob.reshape(HEADS, 64, 128)
            d_score = prob3 * (d_prob - jnp.sum(prob3 * d_prob, 1, keepdims=True))
            d_score = d_score.reshape(HEADS * 64, 128)
            if begin_at == 0:
                g_table[...] += d_score
            prob_tiles = straight_tiles(prob)
            score_tiles = straight_tiles(d_score)
            turned = turned_tiles(d_score)
            for w in range(2):
                part = slice(64 * w, 64 * w + 64)

                def mixed_of(tiles, pieces):
                    return mix([t[begin_at:] for t in tiles], pieces[0][part], pieces[1][part])

                d_query = mixed_of(turned[w], keys)
                put_window(out_here, pair, w, 0, [d * HD**-0.5 for d in d_query])
                put_window(out_here, pair, w, LANES, mixed_of(score_tiles[w], query))
                put_window(out_here, pair, w, 2 * LANES, mixed_of(prob_tiles[w], d_rows))
        if begin_at == 0:
            unit, _ = normalize(start[pl.ds(WIN * k, WIN)])
            d_all = out_here[...].reshape(BLOCK, 3 * LANES)
            g_qkv[:184] += nn(turn(unit.reshape(BLOCK, LANES)), d_all)
            g_mixed[0:1] += jnp.sum(d_all, 0, keepdims=True)

    if first_call:
        pl.when(k == 0)(lambda: work(SHIFT * WIN))
        pl.when(k > 0)(lambda: work(0))
    else:
        work(0)
    if last_call:

        @pl.when(m == pl.num_programs(0) - 1)
        def _():
            finish(
                scal[2], vec, qkv, vec_conv, vec_feed, feed, g_proj, keep, send, g_qkv, g_table,
                g_mixed, lines, proj_turned, turned_qkv,
            )


def finish(
    me, vec, qkv, vec_conv, vec_feed, feed, g_proj, keep, send, g_qkv, g_table, g_mixed, lines,
    proj_turned, turned_qkv,
):
    sums = g_mixed[...]
    cross = g_qkv[...].T
    lines[...] = vec_conv[...] + vec_feed[...]
    lines[PRE_GAIN : PRE_GAIN + 1, :LANES] = jnp.sum(cross * qkv[...], 0, keepdims=True)
    lines[PRE_SHIFT : PRE_SHIFT + 1, :LANES] = nn(sums, qkv[...])[0:1]
    lines[QV_BIAS : QV_BIAS + 1] = sums[0:1]
    turned_qkv[...] = cross * vec[PRE_GAIN : PRE_GAIN + 1, :LANES] + sums.T[:, 0:1] * vec[
        PRE_SHIFT : PRE_SHIFT + 1, :LANES
    ]
    folded = g_table[...]
    lane, u = iota((128, LANES), 0) & 63, iota((128, LANES), 1)
    pick = (u == 112 - 15 * (lane >> 3) - (lane & 7)).astype(F32)
    spread = dot(folded, pick, 1, 0, HIGHEST).reshape(HEADS, WIN, WIN, LANES)
    rel = []
    for h in range(HEADS):
        line = jnp.zeros((WIN, LANES), F32)
        for y in range(WIN):
            line = line + pltpu.roll(spread[h, y], 15 * y, 1, stride=1, stride_axis=0)
        rel.append(jnp.sum(line, 0, keepdims=True))
    rel = jnp.concatenate(rel + [jnp.zeros((REL_ROWS - HEADS, LANES), F32)], 0)
    share = CHANS // PARTS
    proj_turned[...] = g_proj[...].T
    lanes = iota((PROJ_ROWS, 128), 1)
    row = iota((VEC_ROWS, LANES), 0)
    for s in range(PARTS):

        def store(ref, s=s):
            ours = proj_turned[PROJ_ROWS * s : PROJ_ROWS * s + PROJ_ROWS]
            for m in range(3):
                at = s * 3 + m
                at = (at // 4) * LANES + (at % 4) * 48
                ref[48 * m : 48 * m + 48] = turned_qkv[at : at + 48, :128]
                piece = pltpu.roll(ours, (64 - 60 * m) % LANES, 1)[:, :128]
                ref[QKV_ROWS + 48 * m : QKV_ROWS + 48 * m + 48] = jnp.where(
                    lanes < 64, turned_qkv[at : at + 48, 128:], piece
                )
            for m in range(3):
                at = FEED_AT + FEED_ROWS * m
                ref[at : at + FEED_ROWS] = feed[s, :, 128 * m : 128 * m + 128]
            value = lines[...]

            def back(amount):
                return pltpu.roll(value, (3 * LANES - amount) % (3 * LANES), 1)[:, :LANES]

            vectors = jnp.where(
                row < QV_BIAS,
                back(share * s),
                jnp.where(
                    row == QV_BIAS, back((s // 2) * 2 * LANES + (s % 2) * 96), back(96 * s)
                ),
            )
            ref[VEC_AT : VEC_AT + VEC_ROWS] = vectors[:, :128]
            for m in range(2):
                at = REL_AT + REL_ROWS * m
                ref[at : at + REL_ROWS] = rel[:, 128 * m : 128 * m + 128]

        put_part(keep, send, s, me, store)


def image_back_kernel(parts, scal, *refs):
    d_mixed = refs[:parts]
    start, d_attn, cot, qkv, vec = refs[parts : parts + 5]
    out, ready, done = refs[-3:]
    size = scal[0]
    copies = []
    per = STEPS * WIN // parts
    for k in range(STEPS - 1):
        pieces = []
        for row in (WIN * k + SHIFT, WIN * k + WIN):
            pieces.append(d_mixed[row // per][row % per : row % per + SHIFT])
        here = slice(WIN * k + SHIFT, WIN * k + SHIFT + WIN)
        own = slice(WIN * k, WIN * k + WIN)
        unit3, scale = normalize(start[here])
        d_all = jnp.concatenate(pieces, 0).reshape(BLOCK, 3 * LANES)
        d_normed = nn(d_all, qkv[...])
        grad = (d_normed * vec[PRE_GAIN : PRE_GAIN + 1, :LANES]).reshape(unit3.shape)
        value = d_attn[here] + normalize_back(grad, unit3, scale)
        near = cot[WIN * k + SHIFT + 1 : WIN * k + SHIFT + 1 + WIN]
        mask = plain_mask(size, wrapped(scal[1] + SHIFT) + WIN * k, WIN)
        ready[own] = (mask * (near + pltpu.roll(value, SHIFT, 1)))[:, :, :CHANS]
        copies.append(pltpu.make_async_copy(ready.at[own], out.at[own], done.at[k]))
        copies[-1].start()
    for copy in copies:
        copy.wait()


def unpack_kernel(last, qkv, proj, up, down, rel, *vectors):
    share = CHANS // PARTS
    for n in range(9):
        rows = slice(16 * n, 16 * n + HALF)
        qkv[HALF * n : HALF * n + HALF, :128] = last[rows]
        second = slice(QKV_ROWS + 16 * n, QKV_ROWS + 16 * n + HALF)
        qkv[HALF * n : HALF * n + HALF, 128:] = last[second][:, : CHANS - 128]
    pieces = [last[QKV_ROWS + 48 * m : QKV_ROWS + 48 * m + 48] for m in range(3)]
    pieces = [jnp.concatenate([p, jnp.zeros_like(p)], 1) for p in pieces]
    whole = [pltpu.roll(p, (60 * m - 64) % LANES, 1) for m, p in enumerate(pieces)]
    lanes = iota((PROJ_ROWS, LANES), 1)
    value = jnp.where(lanes < 60, whole[0], jnp.where(lanes < 120, whole[1], whole[2]))
    for n in range(3):
        proj[HALF * n : HALF * n + HALF] = value[16 * n : 16 * n + HALF, :CHANS]
    tiles = [last[FEED_AT + FEED_ROWS * m : FEED_AT + FEED_ROWS * (m + 1)] for m in range(3)]
    hid = up.shape[1]
    up[...] = jnp.concatenate(tiles[:2], 1).T[:CHANS, :hid]
    below = pltpu.roll(jnp.concatenate([tiles[1], tiles[2]], 1), LANES - 64, 1)
    down[...] = below.T[:CHANS, :hid]
    lines = jnp.concatenate([last[REL_AT : REL_AT + REL_ROWS], last[REL_AT + REL_ROWS : TAIL_ROWS]], 1)
    a, b = iota((LANES, LANES), 0), iota((LANES, LANES), 1)
    rel[...] = dot(lines, (a + b == RPOS - 1).astype(F32), 1, 0, HIGHEST)[:HEADS, :RPOS]
    for n, ref in enumerate(vectors):
        if n != QV_BIAS:
            ref[...] = last[VEC_AT + n : VEC_AT + n + 1, : ref.shape[1]]
    for n in range(6):
        vectors[QV_BIAS][:, HALF * n : HALF * n + HALF] = last[
            VEC_AT + QV_BIAS : VEC_AT + QV_BIAS + 1, 16 * n : 16 * n + HALF
        ]


def blocked(rows, place):
    def make(shape):
        rest = tuple(shape[1:])
        return pl.BlockSpec((rows,) + rest, lambda m: (place(m),) + (0,) * len(rest))

    return make


def resident(shape):
    return pl.BlockSpec(memory_space=pltpu.VMEM)


def untouched(shape):
    return pl.BlockSpec(memory_space=pl.ANY)


def call(kernel, scal, ins, outs, scratch=(), after=(), limit=10, flops=0, steps=None, keep=None):
    ins = [i if isinstance(i, tuple) else (i, resident) for i in ins]
    outs = [o if callable(o[-1]) else (o, resident) for o in outs]
    ins = [(a if f is resident else pltpu.with_memory_space_constraint(a, pltpu.HBM), f) for a, f in ins]
    ins += [(a, untouched) for a in after]
    first = [] if scal is None else [scal]
    specs = [pl.BlockSpec(memory_space=pltpu.SMEM)] * len(first) + [f(a.shape) for a, f in ins]
    size = sum(4 * a.size for a, f in ins if f is not untouched)
    size += sum(4 * functools.reduce(lambda p, q: p * q, s) for s, _ in outs)
    return pl.pallas_call(
        kernel,
        grid=() if steps is None else (steps,),
        in_specs=specs,
        out_specs=[f(s) for s, f in outs],
        scratch_shapes=[pltpu.VMEM(s, F32) if isinstance(s, tuple) else s for s in scratch],
        out_shape=[
            jax.ShapeDtypeStruct(tuple(s), F32) if f is resident else pltpu.HBM(tuple(s), F32)
            for s, f in outs
        ],
        input_output_aliases={i + len(first): o for i, o in (keep or {}).items()},
        compiler_params=pltpu.CompilerParams(vmem_limit_bytes=limit * MIB),
        cost_estimate=pl.CostEstimate(flops=flops, bytes_accessed=size, transcendentals=0),
    )(*first, *[a for a, _ in ins])


def body(
    images,
    item_sizes,
    cotangent,
    pre_gain,
    pre_shift,
    qkv_weight,
    qv_bias,
    rel_table,
    proj_weight,
    proj_bias,
    mid_gain,
    mid_shift,
    up_weight,
    up_bias,
    down_weight,
    down_bias,
    conv_kernel,
    conv_bias,
):
    height, breadth = images.shape[1:3]
    me = lax.axis_index("tp")
    strip = height + 2 * SHIFT
    image = images[0]
    cot = cotangent[0].transpose(2, 0, 1)
    share = CHANS // PARTS

    def frame(lanes):
        return (strip, breadth, lanes)

    vectors = [pre_gain, pre_shift, proj_bias, mid_gain, mid_shift, down_bias, conv_bias, qv_bias, up_bias]
    at_once = lambda shape: pl.BlockSpec(tuple(shape), lambda m: (0,) * len(shape))
    mine1, mine2 = call(
        pack_kernel,
        None,
        [(a, at_once) for a in (qkv_weight.T, proj_weight, up_weight, down_weight.T, *[v[None] for v in vectors])],
        [(QKV_ROWS + PROJ_ROWS + VEC_ROWS, LANES), (2 * FEED_ROWS, LANES)],
        limit=8,
        steps=1,
    )
    mine3 = conv_kernel.transpose(0, 1, 3, 2).reshape(9, share, CHANS)
    scal = jnp.stack([item_sizes[0], (me * height + IMG - SHIFT) % IMG, me]).astype(jnp.int32)
    x_first, x_last = tie((image[:SHIFT], image[-SHIFT:]), mine1)
    x_above = from_behind(x_last, "tp", 1)
    x_below = from_behind(x_first, "tp", -1)
    all1 = gather_tp(mine1, x_first, x_last)

    qkv, proj, vec, table = call(
        prepare_kernel,
        scal,
        [*all1, rel_table.T],
        [(3 * LANES, LANES), (LANES, LANES), (VEC_ROWS, 3 * LANES), (HEADS * 64, 128)],
        [(VEC_ROWS, 3 * LANES)],
        limit=8,
        flops=10**8,
    )

    def attend(edges, arrays, old):
        place = (lambda m: m * (STEPS - 1)) if edges else (lambda m: m + 1)
        ins = [*arrays, qkv, vec, table, proj]
        keep = {len(ins) + n: n for n in range(len(old))}
        ins += [(o, untouched) for o in old[:2]] + list(old[2:])
        return call(
            functools.partial(attend_kernel, edges),
            scal,
            ins,
            [
                (frame(3 * LANES), blocked(WIN, place)),
                ((STEPS, PAIRS, HEADS * 64, 128), blocked(1, place)),
                frame(LANES),
                frame(LANES),
                frame(LANES),
            ],
            [(WIN, breadth, LANES)],
            flops=5 * 10**9,
            limit=16,
            steps=2,
            keep=keep,
        )

    old = attend(False, [image], [])
    all2 = gather_tp(mine2, old[2])
    c_first, c_last = call(
        rims_kernel, None, [cot], [(SHIFT + 1, breadth, CHANS)] * 2, after=[old[2]], limit=8
    )
    c_above = from_behind(c_last, "tp", 1)
    c_below = from_behind(c_first, "tp", -1)
    mixed, probs, attended, after_attn, start = attend(True, [x_above, image, x_below], old)
    all3 = gather_tp(tie(mine3, old[2]), after_attn)
    pre, after_mlp, up, down = call(
        feed_kernel,
        scal,
        [after_attn, vec, *all2],
        [frame(HID), frame(LANES), (HID, LANES), (HID, LANES)],
        flops=5 * 10**9,
    )
    d_mid, conv_keep, conv_send, vec_conv, wide, cot_rows = call(
        conv_back_kernel,
        scal,
        [after_mlp, cot, c_above, c_below, *all3],
        [
            frame(LANES),
            (2, 9 * CONV_ROWS, LANES),
            (2, 9 * CONV_ROWS, LANES),
            (VEC_ROWS, 3 * LANES),
            (3, LANES, 3 * LANES),
            (strip + 2, breadth, LANES),
        ],
        [
            (WIN + 2, breadth, 3 * LANES),
            (3, 3 * LANES, LANES),
            (PARTS, 9, share, CHANS),
            (3, LANES, 3 * LANES),
            (9, CHANS, LANES),
        ],
        flops=2 * 10**10,
        limit=20,
    )
    got_a = lax.ppermute(conv_send, "tp", flip("tp", 1))
    d_attn, d_att, g_feed, g_proj, vec_feed = call(
        feed_back_kernel,
        scal,
        [d_mid, after_attn, pre, attended, up, down, proj, vec],
        [frame(LANES), frame(LANES), (PARTS, FEED_ROWS, HID), (LANES, LANES), (VEC_ROWS, 3 * LANES)],
        [(LANES, HID), (LANES, HID)],
        after=[conv_send],
        flops=10**10,
        limit=14,
    )
    got_a = tie(got_a, d_att)
    send_b = conv_keep[1] + got_a[1]
    got_b = lax.ppermute(send_b, "tp", flip("tp", 2))

    g_shapes = [(LANES, 3 * LANES), (HEADS * 64, 128), (8, 3 * LANES)]

    def attend_back(begin, end, old, after):
        place = lambda m: m + begin
        ins = [start, (mixed, blocked(WIN, place)), (probs, blocked(1, place)), d_att]
        outs = [((end - begin) * WIN, breadth, 3 * LANES)]
        scratch = []
        if end == STEPS:
            ins += [vec, qkv, vec_conv, vec_feed, g_feed, g_proj]
            outs += [(2, TAIL_ROWS, 128)] * 2
            scratch = g_shapes + [(VEC_ROWS, 3 * LANES), (LANES, LANES), (3 * LANES, LANES)]
        else:
            outs += g_shapes
        return call(
            functools.partial(attend_back_kernel, begin, end),
            scal,
            ins + list(old),
            outs,
            scratch,
            after=after,
            flops=5 * 10**9 * (end - begin),
            limit=16 if begin else 20,
            steps=end - begin,
        )

    d_mixed0, *sums = attend_back(0, 2, [], [send_b])
    got_b = tie(got_b, d_mixed0)
    held = conv_keep[0] + got_a[0] + got_b
    bits = dp_bits()
    d_mixed1, tail_keep, tail_send = attend_back(2, STEPS, sums, [held])
    held = dp_halve(held, bits[0], d_mixed1)

    blocks = height // WIN

    def convolve(k, old, after):
        final = k == blocks - 1
        block = (WIN, breadth, CHANS)
        scratch = [(WIN + 2, breadth, 3 * LANES)]
        if final:
            scratch += [block, pltpu.SemaphoreType.DMA((blocks,))]
        (out,) = call(
            functools.partial(conv_kernel_body, k, blocks),
            scal,
            [after_mlp, start, wide, vec] + (old if final else []),
            [((height, breadth, CHANS), untouched) if final else block],
            scratch,
            after=after,
            flops=4 * 10**9,
        )
        return out if final else old + [out]

    last_a = lax.ppermute(tail_send, "tp", flip("tp", 1))
    block_out = convolve(0, [], [tail_send, held])
    last_a = tie(last_a, block_out)
    last_send = tail_keep[1] + last_a[1]
    last_b = lax.ppermute(last_send, "tp", flip("tp", 2))
    (grad_images,) = call(
        functools.partial(image_back_kernel, 2),
        scal,
        [d_mixed0, d_mixed1, start, d_attn, cot_rows, qkv, vec],
        [((height, breadth, CHANS), untouched)],
        [(height, breadth, CHANS), pltpu.SemaphoreType.DMA((STEPS - 1,))],
        after=[last_send],
        flops=4 * 10**9,
    )
    if len(bits) > 1:
        held = dp_add(held, bits[1], grad_images)
    last_b = tie(last_b, grad_images)
    last = tail_keep[0] + last_a[0] + last_b
    for k in range(1, blocks):
        if k == 1:
            block_out = convolve(k, block_out, [last])
            last = dp_halve(last, bits[0], block_out)
        elif k <= len(bits):
            block_out = convolve(k, block_out, [last])
            last = dp_add(last, bits[k - 1], block_out)
    grad_images = tie(grad_images, last)
    for bit in bits[2:]:
        held = dp_add(held, bit, grad_images)
    for bit in bits[blocks - 1 :]:
        last = dp_add(last, bit)
    held = dp_join(held, bits[0], last)
    block_out = tie(block_out, last)
    last = dp_join(last, bits[0])

    conv = held.reshape(3, 3, CONV_ROWS, LANES)[:, :, :share, :CHANS]
    hid = up_weight.shape[1]
    g_qkv, g_proj, g_up, g_down, g_rel, *g_vec = call(
        unpack_kernel,
        None,
        [last],
        [(qkv_weight.shape[1], CHANS), (share, CHANS), (CHANS, hid), (CHANS, hid), (HEADS, RPOS)] + [(1, v.shape[0]) for v in vectors],
        limit=8,
    )

    g_vec = [g[0] for g in g_vec]
    return (
        block_out[None],
        grad_images[None],
        g_vec[PRE_GAIN],
        g_vec[PRE_SHIFT],
        g_qkv.T,
        g_vec[QV_BIAS],
        g_rel.T,
        g_proj,
        g_vec[PROJ_BIAS],
        g_vec[MID_GAIN],
        g_vec[MID_SHIFT],
        g_up,
        g_vec[UP_BIAS],
        g_down.T,
        g_vec[DOWN_BIAS],
        conv.transpose(0, 1, 3, 2),
        g_vec[CONV_BIAS],
    )


def solution(mesh):
    placed = (
        P("dp", "tp", None, None),
        P("dp"),
        P("dp", "tp", None, None),
        P("tp"),
        P("tp"),
        P(None, "tp"),
        P("tp"),
        P(),
        P("tp", None),
        P("tp"),
        P("tp"),
        P("tp"),
        P(None, "tp"),
        P("tp"),
        P("tp", None),
        P("tp"),
        P(None, None, None, "tp"),
        P("tp"),
    )
    return jax.shard_map(
        body,
        mesh=mesh,
        in_specs=placed,
        out_specs=(
            P("dp", "tp", None, None),
            P("dp", "tp", None, None),
            P("tp"),
            P("tp"),
            P(None, "tp"),
            P("tp"),
            P(),
            P("tp", None),
            P("tp"),
            P("tp"),
            P("tp"),
            P(None, "tp"),
            P("tp"),
            P("tp", None),
            P("tp"),
            P(None, None, None, "tp"),
            P("tp"),
        ),
        check_vma=False,
    )
```

```python
import functools

import jax
import jax.numpy as jnp
from jax import lax
from jax.experimental import pallas as pl
from jax.experimental.pallas import tpu as pltpu
from jax.sharding import PartitionSpec as P

WIN = 8
IMG = 96
SHIFT = 4
EPSILON = 1e-05
NEG_FILL = -1e30
CHANS = 180
HEADS = 6
HD = 30
HALF = 15
SLOT = 32
LANES = 256
INNER = 192
HID = 384
RPOS = 225
HIGH = lax.Precision.HIGH
HIGHEST = lax.Precision.HIGHEST
F32 = jnp.float32
BF16 = jnp.bfloat16
BLOCK = WIN * IMG
PAIRS = IMG // WIN // 2
PARTS = 4
MIB = 2**20
STEPS = 4

QKV_ROWS, PROJ_ROWS, VEC_ROWS = 144, 48, 16
FEED_ROWS = 96
CONV_ROWS = 48
REL_ROWS = 8
FEED_AT = 2 * QKV_ROWS
VEC_AT = FEED_AT + 3 * FEED_ROWS
REL_AT = VEC_AT + VEC_ROWS
TAIL_ROWS = REL_AT + 2 * REL_ROWS
PRE_GAIN, PRE_SHIFT, PROJ_BIAS, MID_GAIN, MID_SHIFT, DOWN_BIAS, CONV_BIAS, QV_BIAS, UP_BIAS = range(9)


def flip(axis, bit):
    return [(i, i ^ bit) for i in range(lax.axis_size(axis))]


def from_behind(block, axis, distance):
    n = lax.axis_size(axis)
    return lax.ppermute(block, axis, [((i - distance) % n, i) for i in range(n)])


def gather_tp(block, *others):
    got = {0: block}
    for bit in (2, 1):
        if others and bit == 1:
            got[2] = tie(got[2], *others)
        got.update({k | bit: lax.ppermute(b, "tp", flip("tp", bit)) for k, b in list(got.items())})
    return [got[k] for k in range(PARTS)]


def tie(value, *others):
    return lax.optimization_barrier((value, others))[0]


def dp_bits():
    n = lax.axis_size("dp")
    return [1 << b for b in range(n.bit_length() - 1)]


def dp_halve(held, bit, *others):
    half = held.shape[0] // 2
    odd = (lax.axis_index("dp") & bit) != 0
    send = jnp.where(odd, held[:half], held[half:])
    got = lax.ppermute(send, "dp", flip("dp", bit))
    if others:
        got = tie(got, *others)
    return jnp.where(odd, held[half:], held[:half]) + got


def dp_join(held, bit, *others):
    odd = (lax.axis_index("dp") & bit) != 0
    got = lax.ppermute(held, "dp", flip("dp", bit))
    if others:
        got = tie(got, *others)
    return jnp.concatenate([jnp.where(odd, got, held), jnp.where(odd, held, got)], 0)


def dp_add(held, bit, *others):
    got = lax.ppermute(held, "dp", flip("dp", bit))
    if others:
        got = tie(got, *others)
    return held + got


def dot(left, right, left_dim, right_dim, precision=None):
    return lax.dot_general(
        left,
        right,
        (((left_dim,), (right_dim,)), ((), ())),
        precision=precision,
        preferred_element_type=F32,
    )


def nn(left, right):
    return dot(left, right, 1, 0, HIGH)


def nt(left, right):
    return dot(left, right, 1, 1, HIGH)


def turn(value):
    return value.T[:184]


def iota(shape, dim):
    return lax.broadcasted_iota(jnp.int32, shape, dim)


def wrapped(position):
    return jnp.where(position >= IMG, position - IMG, position)


def frame_mask(size, first, rows=WIN):
    shape = (rows, IMG, LANES)
    row = wrapped(first + iota(shape, 0))
    col = wrapped(iota(shape, 1) + SHIFT)
    return ((row < size) & (col < size) & (iota(shape, 2) < CHANS)).astype(F32)


def plain_mask(size, first, rows):
    shape = (rows, IMG, LANES)
    row = wrapped(first + iota(shape, 0))
    return ((row < size) & (iota(shape, 1) < size) & (iota(shape, 2) < CHANS)).astype(F32)


def is_channel(shape):
    return iota(shape, len(shape) - 1) < CHANS


def mean(value):
    return jnp.sum(value, axis=-1, keepdims=True) * (1.0 / CHANS)


def normalize(value):
    centre = jnp.where(is_channel(value.shape), value - mean(value), 0.0)
    scale = lax.rsqrt(mean(centre * centre) + EPSILON)
    return centre * scale, scale


def normalize_back(grad, unit, scale):
    value = scale * (grad - mean(grad) - unit * mean(grad * unit))
    return jnp.where(is_channel(value.shape), value, 0.0)


def upper(value):
    return value.astype(BF16).astype(F32)


def parted(value):
    high = upper(value)
    return jnp.where(iota(value.shape, 1) < 64, high, value - high)


def doubled(first, second):
    left = iota(first.shape, 1) < 64
    turned0 = pltpu.roll(first, 64, 1)
    turned1 = pltpu.roll(second, 64, 1)
    return (
        jnp.where(left, first, turned0),
        jnp.where(left, turned0, first),
        jnp.where(left, second, turned1),
    )


def head_products(rows, cols):
    lanes = iota((128, 128), 1)
    even = (lanes & 63) < SLOT
    outs = []
    for moving, fixed in zip(doubled(*rows), doubled(*cols)):
        high = fixed.astype(BF16)
        low = (fixed - high.astype(F32)).astype(BF16)
        held = jnp.concatenate([high, low], 1)
        pieces = parted(moving)
        ones = jnp.where(even, pieces, 0.0).astype(BF16)
        twos = jnp.where(even, 0.0, pieces).astype(BF16)
        both = []
        for w in range(2):
            part = slice(64 * w, 64 * w + 64)
            stream = jnp.concatenate([ones[part], twos[part]], 0)
            both.append(dot(jnp.concatenate([stream, stream], 1), held, 1, 1))
        outs.append(jnp.where(lanes < 64, both[0], both[1]))
    return jnp.concatenate(outs, 0)


def mix(tiles, first, second):
    n = tiles[0].shape[0]
    lanes = iota((n, 128), 1)

    def product(part, block):
        high = block.astype(BF16)
        low = (block - high.astype(F32)).astype(BF16)
        held = jnp.concatenate([high, high, low, low], 0)
        stream = jnp.concatenate(part, 0)
        return dot(jnp.concatenate([stream, stream], 1), held, 1, 0)

    a = product(tiles[:4], first)
    b = product(tiles[4:], second)
    one = jnp.where(
        lanes < 64,
        jnp.where(lanes < 32, a[:n], a[n : 2 * n]),
        jnp.where(lanes < 96, a[2 * n : 3 * n], a[3 * n :]),
    )
    two = jnp.where(lanes < 32, b[:n], b[n:])
    return one, two


def straight_tiles(table):
    left = iota(table.shape, 1) < 64
    turned = pltpu.roll(table, 64, 1)
    outs = []
    for w in range(2):
        one = jnp.where(left, table, turned) if w == 0 else jnp.where(left, turned, table)
        both = parted(one).astype(BF16)
        outs.append([both[64 * h : 64 * h + 64] for h in range(HEADS)])
    return outs


def turned_tiles(table):
    high = upper(table)
    low = table - high
    outs = [[], []]
    for h in range(HEADS):
        part = slice(64 * h, 64 * h + 64)
        both = jnp.concatenate([high[part], low[part]], 0).astype(BF16).T
        for w in range(2):
            outs[w].append(both[64 * w : 64 * w + 64])
    return outs


def window_pair(ref, pair, start):
    cols = pl.ds(pl.multiple_of(pair * 2 * WIN, 2 * WIN), 2 * WIN)
    tiles = []
    for tile in range(2):
        block = ref[:, cols, start + 128 * tile : start + 128 * tile + 128]
        tiles.append(
            jnp.concatenate(
                [block[:, :WIN].reshape(64, 128), block[:, WIN:].reshape(64, 128)], 0
            )
        )
    return tiles


def put_window(ref, pair, w, start, tiles):
    cols = pl.ds(pl.multiple_of(pair * 2 * WIN + w * WIN, WIN), WIN)
    rows = tiles[0].shape[0] // WIN
    for tile in range(2):
        ref[WIN - rows :, cols, start + 128 * tile : start + 128 * tile + 128] = tiles[
            tile
        ].reshape(rows, WIN, 128)


def pair_fill(size, first, pair):
    shape = (64, 128)
    j, lane = iota(shape, 0), iota(shape, 1)
    i, window = lane & 63, 2 * pair + (lane >> 6)
    rows = wrapped(first + (j >> 3))
    cols = wrapped(window * WIN + (j & 7) + SHIFT)
    apart_rows = (first == IMG - WIN + SHIFT) & ((j >> 5) != (i >> 5))
    apart_cols = (window == IMG // WIN - 1) & (((j & 7) >> 2) != ((i & 7) >> 2))
    keep = (rows < size) & (cols < size)
    return jnp.where(apart_rows | apart_cols | jnp.logical_not(keep), NEG_FILL, 0.0)


def block_first(scal, k):
    return wrapped(scal[1] + WIN * k)


def block_of(ref, k):
    return ref.at[pl.ds(WIN * k, WIN)]


def put_part(keep, send, part, me, store):
    place = part ^ me
    pl.when((place & 1) == 0)(lambda: store(keep.at[place >> 1]))
    pl.when((place & 1) == 1)(lambda: store(send.at[place >> 1]))


def gelu_parts(hidden):
    return 0.5 * (1.0 + lax.erf(hidden * 0.5**0.5))


def pack_kernel(qkv, proj, up, down, *refs):
    vectors, (first, second) = refs[:9], refs[9:]
    first[...] = jnp.zeros_like(first)
    second[...] = jnp.zeros_like(second)
    for n in range(9):
        first[16 * n : 16 * n + HALF, :CHANS] = qkv[HALF * n : HALF * n + HALF]
    for n in range(3):
        at = QKV_ROWS + 16 * n
        first[at : at + HALF, :CHANS] = proj[HALF * n : HALF * n + HALF]
    share, hid = CHANS // PARTS, up.shape[1]
    second[:hid, :CHANS] = up[...].T
    second[FEED_ROWS : FEED_ROWS + hid, :CHANS] = down[...].T
    at = QKV_ROWS + PROJ_ROWS
    for n, ref in enumerate(vectors):
        if n != QV_BIAS:
            first[at + n : at + n + 1, : ref.shape[1]] = ref[...]
    for n in range(6):
        first[at + QV_BIAS : at + QV_BIAS + 1, 16 * n : 16 * n + HALF] = vectors[QV_BIAS][
            :, HALF * n : HALF * n + HALF
        ]


def rims_kernel(cot, *refs):
    first, last = refs[-2:]
    height, n = cot.shape[1], first.shape[0]
    for row in range(n):
        first[row] = cot[:, row, :].T
        last[row] = cot[:, height - n + row, :].T


def prepare_kernel(scal, p0, p1, p2, p3, rel, qkv, proj, vec, table, spread):
    me = scal[2]
    for ref in (qkv, vec, spread):
        ref[...] = jnp.zeros_like(ref)
    proj[INNER:] = jnp.zeros_like(proj[INNER:])
    lanes = iota((VEC_ROWS, 3 * LANES), 1)
    row = iota((VEC_ROWS, 3 * LANES), 0)
    for k, piece in enumerate((p0, p1, p2, p3)):
        owner = me ^ k
        for m in range(3):
            at = owner * 3 + m
            start = pl.multiple_of((at // 4) * LANES + (at % 4) * 48, 16)
            qkv[pl.ds(start, 48)] = piece[48 * m : 48 * m + 48]
        proj[pl.ds(pl.multiple_of(owner * PROJ_ROWS, 16), PROJ_ROWS)] = piece[
            QKV_ROWS : QKV_ROWS + PROJ_ROWS
        ]
        spread[:VEC_ROWS, :LANES] = piece[QKV_ROWS + PROJ_ROWS :]
        value = spread[:VEC_ROWS]
        vec[...] += jnp.where(
            row < QV_BIAS,
            pltpu.roll(value, owner * (CHANS // PARTS), 1),
            jnp.where(
                row == QV_BIAS,
                pltpu.roll(value, (owner // 2) * 2 * LANES + (owner % 2) * 96, 1),
                pltpu.roll(value, owner * 96, 1),
            ),
        )
    spread[...] = jnp.zeros_like(spread)
    spread[:HEADS, :RPOS] = rel[...]
    pieces = []
    for h in range(HEADS):
        line = jnp.broadcast_to(spread[h : h + 1, :LANES], (WIN, LANES))
        for y in range(WIN):
            pieces.append(
                pltpu.roll(line, (15 * y - 112) % LANES, 1, stride=1, stride_axis=0)
            )
    lines = jnp.concatenate(pieces, 0)
    u, lane = iota((LANES, 128), 0), iota((LANES, 128), 1) & 63
    pick = (u == (lane >> 3) * 15 + (lane & 7)).astype(F32)
    table[...] = dot(lines, pick, 1, 0, HIGHEST)


def attend_kernel(edges, scal, *refs):
    m = pl.program_id(0)
    if edges:
        above, image, below, qkv, vec, table, proj = refs[:7]
        k = m * (STEPS - 1)
    else:
        image, qkv, vec, table, proj = refs[:5]
        k = m + 1
    mixed, probs, attended, after, start, wide = refs[-6:]
    height = image.shape[0]

    @pl.when(m == 0)
    def _():
        wide[...] = jnp.zeros_like(wide)
        if edges:
            wide[:SHIFT, :, :CHANS] = above[...]
            wide[SHIFT:, :, :CHANS] = image[:SHIFT]

    if edges:

        @pl.when(m == 1)
        def _():
            wide[:SHIFT, :, :CHANS] = image[height - SHIFT :]
            wide[SHIFT:, :, :CHANS] = below[...]

    else:
        wide[:, :, :CHANS] = image[pl.ds(WIN * k - SHIFT, WIN)]
    size, first = scal[0], block_first(scal, k)
    rows = pl.ds(WIN * k, WIN)
    mask = frame_mask(size, first)
    begin = mask * pltpu.roll(wide[...], IMG - SHIFT, 1)
    start[rows] = begin
    unit, _ = normalize(begin)
    normed = unit * vec[PRE_GAIN, :LANES] + vec[PRE_SHIFT, :LANES]
    mixed[...] = (
        nt(normed.reshape(BLOCK, LANES), qkv[...]) + vec[QV_BIAS : QV_BIAS + 1]
    ).reshape(WIN, IMG, 3 * LANES)
    out_here = block_of(attended, k)
    for pair in range(PAIRS):
        query = window_pair(mixed, pair, 0)
        keys = window_pair(mixed, pair, LANES)
        values = window_pair(mixed, pair, 2 * LANES)
        scores = head_products(keys, [q * HD**-0.5 for q in query]) + table[...]
        scores = scores.reshape(HEADS, 64, 128) + pair_fill(size, first, pair)[None]
        scores = jnp.exp(scores - jnp.max(scores, 1, keepdims=True))
        prob = (scores * (1.0 / jnp.sum(scores, 1, keepdims=True))).reshape(HEADS * 64, 128)
        probs[0, pair] = prob
        for w, tiles in enumerate(turned_tiles(prob)):
            part = slice(64 * w, 64 * w + 64)
            put_window(out_here, pair, w, 0, mix(tiles, values[0][part], values[1][part]))
    out = nn(out_here[...].reshape(BLOCK, LANES), proj[...]) + vec[PROJ_BIAS : PROJ_BIAS + 1, :LANES]
    after[rows] = begin + mask * out.reshape(WIN, IMG, LANES)


def feed_kernel(scal, value, vec, p0, p1, p2, p3, pre, after, up, down):
    for k, piece in enumerate((p0, p1, p2, p3)):
        rows = pl.ds(pl.multiple_of((scal[2] ^ k) * FEED_ROWS, 32), FEED_ROWS)
        up[rows] = piece[:FEED_ROWS]
        down[rows] = piece[FEED_ROWS:]

    def block(k, carry):
        rows = pl.ds(WIN * k, WIN)
        mask = frame_mask(scal[0], block_first(scal, k))
        here = value[rows]
        unit, _ = normalize(here)
        normed = unit * vec[MID_GAIN, :LANES] + vec[MID_SHIFT, :LANES]
        hidden = nt(normed.reshape(BLOCK, LANES), up[...]) + vec[UP_BIAS : UP_BIAS + 1, :HID]
        pre[rows] = hidden.reshape(WIN, IMG, HID)
        act = hidden * gelu_parts(hidden)
        out = nn(act, down[...]) + vec[DOWN_BIAS : DOWN_BIAS + 1, :LANES]
        after[rows] = here + mask * out.reshape(here.shape)
        return carry

    lax.fori_loop(0, STEPS, block, 0)


def put_shifted(ref, value):
    cols = iota(value.shape, 1)
    ref[:, :, LANES : 2 * LANES] = value
    ref[:, :, :LANES] = jnp.where(cols == 0, 0.0, pltpu.roll(value, 1, 1))
    ref[:, :, 2 * LANES :] = jnp.where(cols == IMG - 1, 0.0, pltpu.roll(value, IMG - 1, 1))


def conv_back_kernel(
    scal,
    after,
    cot,
    cot_above,
    cot_below,
    p0,
    p1,
    p2,
    p3,
    d_mid,
    keep,
    send,
    vec,
    wide,
    padded,
    d_spread,
    tall,
    gathered,
    grad,
    taps,
):
    height = cot.shape[1]
    share = CHANS // PARTS
    size, base, me = scal[0], scal[1], scal[2]
    for ref in (wide, tall, padded, grad, vec):
        ref[...] = jnp.zeros_like(ref)
    for n, piece in enumerate((p0, p1, p2, p3)):
        gathered[me ^ n] = piece[...]
    for s in range(PARTS):
        rows = slice(share * s, share * s + share)
        for i in range(3):
            for j in range(3):
                part = gathered[s, 3 * i + j]
                wide[i, rows, LANES * j : LANES * j + CHANS] = part
                at = LANES * (2 - j) + share * s
                tall[i, at : at + share, :CHANS] = part
    edge = SHIFT + 1
    padded[:edge, :, :CHANS] = cot_above[...]
    for row in range(height):
        padded[edge + row, :, :CHANS] = cot[:, row, :].T
    padded[edge + height :, :, :CHANS] = cot_below[...]
    shape = (WIN, IMG, LANES)

    def block(k, own):
        tall_shape = (WIN + 2, IMG, LANES)
        row = wrapped(wrapped(wrapped(base + IMG - 1 + WIN * k) + iota(tall_shape, 0)))
        inside = (row < size) & (iota(tall_shape, 1) < size)
        put_shifted(d_spread, jnp.where(inside, padded[pl.ds(WIN * k, WIN + 2)], 0.0))
        rows = wrapped(wrapped(base + WIN * k) + iota(shape, 0))
        rows_all = wrapped(wrapped(base + WIN * k) + iota((WIN, IMG, 3 * LANES), 0))
        total = jnp.zeros(shape, F32)
        here = pltpu.roll(after[pl.ds(WIN * k, WIN)], SHIFT, 1)[own]
        turned = turn(here.reshape(-1, LANES))
        for i in range(3):
            around = d_spread[2 - i : 2 - i + WIN]
            part = nn(around.reshape(BLOCK, 3 * LANES), tall[i]).reshape(shape)
            if i == 0:
                part = jnp.where(rows == IMG - 1, 0.0, part)
                around = jnp.where(rows_all == IMG - 1, 0.0, around)
            if i == 2:
                part = jnp.where(rows == 0, 0.0, part)
                around = jnp.where(rows_all == 0, 0.0, around)
            total = total + part
            grad[i, :184] += nn(turned, around[own].reshape(-1, 3 * LANES))
        d_mid[pl.ds(WIN * k, WIN)] = pltpu.roll(total, IMG - SHIFT, 1)
        centre = d_spread[1 : 1 + WIN, :, LANES : 2 * LANES][own]
        vec[CONV_BIAS : CONV_BIAS + 1, :LANES] += jnp.sum(
            centre.reshape(-1, LANES), 0, keepdims=True
        )

    block(0, slice(SHIFT, WIN))

    def inner(k, carry):
        block(k, slice(0, WIN))
        return carry

    lax.fori_loop(1, STEPS - 1, inner, 0)
    block(STEPS - 1, slice(0, SHIFT))
    for i in range(3):
        for j in range(3):
            taps[3 * i + j] = grad[i, :, LANES * (2 - j) : LANES * (3 - j)].T[:CHANS]
    for s in range(PARTS):

        def store(ref, s=s):
            for n in range(9):
                ref[CONV_ROWS * n : CONV_ROWS * n + share] = taps[n, share * s : share * s + share]

        put_part(keep, send, s, me, store)


def conv_kernel_body(k, blocks, scal, after, start, wide, vec, *refs):
    copies = []
    if k == blocks - 1:
        out, spread, ready, done = refs[-4:]
        for n in range(k):
            copies.append(
                pltpu.make_async_copy(refs[n], out.at[WIN * n : WIN * n + WIN], done.at[n])
            )
            copies[-1].start()
    else:
        ready, spread = refs[-2:]
    tall_shape = (WIN + 2, IMG, LANES)
    first = wrapped(scal[1] + SHIFT) + WIN * k
    row = first - 1 + iota(tall_shape, 0)
    value = pltpu.roll(after[pl.ds(WIN * k + SHIFT - 1, WIN + 2)], SHIFT, 1)
    put_shifted(spread, jnp.where((row < 0) | (row >= IMG), 0.0, value))
    total = jnp.zeros((BLOCK, LANES), F32)
    for i in range(3):
        total = total + nt(spread[i : i + WIN].reshape(BLOCK, 3 * LANES), wide[i])
    mask = plain_mask(scal[0], first, WIN)
    conv = (total + vec[CONV_BIAS : CONV_BIAS + 1, :LANES]).reshape(mask.shape)
    here = pltpu.roll(start[pl.ds(WIN * k + SHIFT, WIN)], SHIFT, 1)
    ready[...] = (here + mask * conv)[:, :, :CHANS]
    if k == blocks - 1:
        copies.append(pltpu.make_async_copy(ready, out.at[WIN * k : WIN * k + WIN], done.at[k]))
        copies[-1].start()
    for copy in copies:
        copy.wait()


def feed_back_kernel(
    scal, d_mid, value, pre, attended, up, down, proj, vec, *refs
):
    d_attn, d_att, grads, g_proj, g_vec, g_up, g_down = refs[-7:]
    for ref in (g_up, g_down, g_proj, g_vec):
        ref[...] = jnp.zeros_like(ref)
    size = scal[0]

    def block(k, rows, part, counted):
        here = pl.ds(WIN * k, WIN)
        mask = frame_mask(size, block_first(scal, k))
        mid = d_mid[here]
        d_ff = (mask * mid).reshape(BLOCK, LANES)
        hidden = pre[here].reshape(BLOCK, HID)
        phi = gelu_parts(hidden)
        act = hidden * phi
        slope = phi + hidden * (jnp.exp(-0.5 * hidden * hidden) * 0.3989422804014327)
        d_pre = nt(d_ff, down[...]) * slope
        d_normed = nn(d_pre, up[...])
        unit3, scale = normalize(value[here])
        unit = unit3.reshape(BLOCK, LANES)
        gain = vec[MID_GAIN : MID_GAIN + 1, :LANES]
        normed = unit * gain + vec[MID_SHIFT : MID_SHIFT + 1, :LANES]
        grad = (d_normed * gain).reshape(mid.shape)
        d_out = mid + normalize_back(grad, unit3, scale)
        d_attn[here] = d_out
        d_proj = (mask * d_out).reshape(BLOCK, LANES)
        d_att[here] = nt(d_proj, proj[...]).reshape(mid.shape)
        d_ff_own, d_pre_own, d_normed_own = d_ff[part], d_pre[part], d_normed[part]
        g_down[:184] += nn(turn(d_ff_own), act[part])
        g_up[:184] += nn(turn(normed[part]), d_pre_own)
        g_vec[UP_BIAS : UP_BIAS + 1, :HID] += jnp.sum(d_pre_own, 0, keepdims=True)
        for at, v in (
            (MID_GAIN, d_normed_own * unit[part]),
            (MID_SHIFT, d_normed_own),
            (DOWN_BIAS, d_ff_own),
        ):
            g_vec[at : at + 1, :LANES] += jnp.sum(v, 0, keepdims=True)
        if counted:
            g_proj[:184] += nn(turn(d_proj), attended[here].reshape(BLOCK, LANES))
            g_vec[PROJ_BIAS : PROJ_BIAS + 1, :LANES] += jnp.sum(d_proj, 0, keepdims=True)

    block(0, None, slice(SHIFT * IMG, BLOCK), False)

    def inner(k, carry):
        block(k, None, slice(0, BLOCK), True)
        return carry

    lax.fori_loop(1, STEPS - 1, inner, 0)
    block(STEPS - 1, None, slice(0, SHIFT * IMG), True)
    for s in range(PARTS):
        rows = slice(FEED_ROWS * s, FEED_ROWS * s + FEED_ROWS)
        grads[s, :, :] = jnp.zeros_like(grads[s])
    turned_up = g_up[...].T
    turned_down = g_down[...].T
    for s in range(PARTS):
        rows = slice(FEED_ROWS * s, FEED_ROWS * s + FEED_ROWS)
        below = pltpu.roll(turned_down[rows], 64, 1)
        lanes = iota((FEED_ROWS, 128), 1)
        grads[s, :, :128] = turned_up[rows, :128]
        grads[s, :, 128:256] = jnp.where(lanes < 64, turned_up[rows, 128:], below[:, :128])
        grads[s, :, 256:] = below[:, 128:]


def attend_back_kernel(begin, end, scal, start, mixed, probs, d_att, *refs):
    refs = list(refs)
    first_call, last_call = begin == 0, end == STEPS
    if last_call:
        vec, qkv, vec_conv, vec_feed, feed, g_proj = refs[:6]
        d_mixed, keep, send, g_qkv, g_table, g_mixed, lines, proj_turned, turned_qkv = refs[-9:]
    else:
        d_mixed, g_qkv, g_table, g_mixed = refs[-4:]
    before = refs[6 if last_call else 0 :][:3]
    m = pl.program_id(0)
    k = m + begin

    @pl.when(m == 0)
    def _():
        for n, ref in enumerate((g_qkv, g_table, g_mixed)):
            ref[...] = jnp.zeros_like(ref) if first_call else before[n][...]

    att_here = block_of(d_att, k)
    out_here = block_of(d_mixed, m)

    def work(begin_at):
        for pair in range(PAIRS):
            query = [q * HD**-0.5 for q in window_pair(mixed, pair, 0)]
            keys = window_pair(mixed, pair, LANES)
            values = window_pair(mixed, pair, 2 * LANES)
            d_rows = window_pair(att_here, pair, 0)
            prob = probs[0, pair]
            d_prob = head_products(values, d_rows).reshape(HEADS, 64, 128)
            prob3 = prob.reshape(HEADS, 64, 128)
            d_score = prob3 * (d_prob - jnp.sum(prob3 * d_prob, 1, keepdims=True))
            d_score = d_score.reshape(HEADS * 64, 128)
            if begin_at == 0:
                g_table[...] += d_score
            prob_tiles = straight_tiles(prob)
            score_tiles = straight_tiles(d_score)
            turned = turned_tiles(d_score)
            for w in range(2):
                part = slice(64 * w, 64 * w + 64)

                def mixed_of(tiles, pieces):
                    return mix([t[begin_at:] for t in tiles], pieces[0][part], pieces[1][part])

                d_query = mixed_of(turned[w], keys)
                put_window(out_here, pair, w, 0, [d * HD**-0.5 for d in d_query])
                put_window(out_here, pair, w, LANES, mixed_of(score_tiles[w], query))
                put_window(out_here, pair, w, 2 * LANES, mixed_of(prob_tiles[w], d_rows))
        if begin_at == 0:
            unit, _ = normalize(start[pl.ds(WIN * k, WIN)])
            d_all = out_here[...].reshape(BLOCK, 3 * LANES)
            g_qkv[:184] += nn(turn(unit.reshape(BLOCK, LANES)), d_all)
            g_mixed[0:1] += jnp.sum(d_all, 0, keepdims=True)

    if first_call:
        pl.when(k == 0)(lambda: work(SHIFT * WIN))
        pl.when(k > 0)(lambda: work(0))
    else:
        work(0)
    if last_call:

        @pl.when(m == pl.num_programs(0) - 1)
        def _():
            finish(
                scal[2], vec, qkv, vec_conv, vec_feed, feed, g_proj, keep, send, g_qkv, g_table,
                g_mixed, lines, proj_turned, turned_qkv,
            )


def finish(
    me, vec, qkv, vec_conv, vec_feed, feed, g_proj, keep, send, g_qkv, g_table, g_mixed, lines,
    proj_turned, turned_qkv,
):
    sums = g_mixed[...]
    cross = g_qkv[...].T
    lines[...] = vec_conv[...] + vec_feed[...]
    lines[PRE_GAIN : PRE_GAIN + 1, :LANES] = jnp.sum(cross * qkv[...], 0, keepdims=True)
    lines[PRE_SHIFT : PRE_SHIFT + 1, :LANES] = nn(sums, qkv[...])[0:1]
    lines[QV_BIAS : QV_BIAS + 1] = sums[0:1]
    turned_qkv[...] = cross * vec[PRE_GAIN : PRE_GAIN + 1, :LANES] + sums.T[:, 0:1] * vec[
        PRE_SHIFT : PRE_SHIFT + 1, :LANES
    ]
    folded = g_table[...]
    lane, u = iota((128, LANES), 0) & 63, iota((128, LANES), 1)
    pick = (u == 112 - 15 * (lane >> 3) - (lane & 7)).astype(F32)
    spread = dot(folded, pick, 1, 0, HIGHEST).reshape(HEADS, WIN, WIN, LANES)
    rel = []
    for h in range(HEADS):
        line = jnp.zeros((WIN, LANES), F32)
        for y in range(WIN):
            line = line + pltpu.roll(spread[h, y], 15 * y, 1, stride=1, stride_axis=0)
        rel.append(jnp.sum(line, 0, keepdims=True))
    rel = jnp.concatenate(rel + [jnp.zeros((REL_ROWS - HEADS, LANES), F32)], 0)
    share = CHANS // PARTS
    proj_turned[...] = g_proj[...].T
    lanes = iota((PROJ_ROWS, 128), 1)
    row = iota((VEC_ROWS, LANES), 0)
    for s in range(PARTS):

        def store(ref, s=s):
            ours = proj_turned[PROJ_ROWS * s : PROJ_ROWS * s + PROJ_ROWS]
            for m in range(3):
                at = s * 3 + m
                at = (at // 4) * LANES + (at % 4) * 48
                ref[48 * m : 48 * m + 48] = turned_qkv[at : at + 48, :128]
                piece = pltpu.roll(ours, (64 - 60 * m) % LANES, 1)[:, :128]
                ref[QKV_ROWS + 48 * m : QKV_ROWS + 48 * m + 48] = jnp.where(
                    lanes < 64, turned_qkv[at : at + 48, 128:], piece
                )
            for m in range(3):
                at = FEED_AT + FEED_ROWS * m
                ref[at : at + FEED_ROWS] = feed[s, :, 128 * m : 128 * m + 128]
            value = lines[...]

            def back(amount):
                return pltpu.roll(value, (3 * LANES - amount) % (3 * LANES), 1)[:, :LANES]

            vectors = jnp.where(
                row < QV_BIAS,
                back(share * s),
                jnp.where(
                    row == QV_BIAS, back((s // 2) * 2 * LANES + (s % 2) * 96), back(96 * s)
                ),
            )
            ref[VEC_AT : VEC_AT + VEC_ROWS] = vectors[:, :128]
            for m in range(2):
                at = REL_AT + REL_ROWS * m
                ref[at : at + REL_ROWS] = rel[:, 128 * m : 128 * m + 128]

        put_part(keep, send, s, me, store)


def image_back_kernel(parts, scal, *refs):
    d_mixed = refs[:parts]
    start, d_attn, cot, qkv, vec = refs[parts : parts + 5]
    out, ready, done = refs[-3:]
    size = scal[0]
    copies = []
    per = STEPS * WIN // parts
    for k in range(STEPS - 1):
        pieces = []
        for row in (WIN * k + SHIFT, WIN * k + WIN):
            pieces.append(d_mixed[row // per][row % per : row % per + SHIFT])
        here = slice(WIN * k + SHIFT, WIN * k + SHIFT + WIN)
        own = slice(WIN * k, WIN * k + WIN)
        unit3, scale = normalize(start[here])
        d_all = jnp.concatenate(pieces, 0).reshape(BLOCK, 3 * LANES)
        d_normed = nn(d_all, qkv[...])
        grad = (d_normed * vec[PRE_GAIN : PRE_GAIN + 1, :LANES]).reshape(unit3.shape)
        value = d_attn[here] + normalize_back(grad, unit3, scale)
        near = cot[WIN * k + SHIFT + 1 : WIN * k + SHIFT + 1 + WIN]
        mask = plain_mask(size, wrapped(scal[1] + SHIFT) + WIN * k, WIN)
        ready[own] = (mask * (near + pltpu.roll(value, SHIFT, 1)))[:, :, :CHANS]
        copies.append(pltpu.make_async_copy(ready.at[own], out.at[own], done.at[k]))
        copies[-1].start()
    for copy in copies:
        copy.wait()


def unpack_kernel(last, qkv, proj, up, down, rel, *vectors):
    share = CHANS // PARTS
    for n in range(9):
        rows = slice(16 * n, 16 * n + HALF)
        qkv[HALF * n : HALF * n + HALF, :128] = last[rows]
        second = slice(QKV_ROWS + 16 * n, QKV_ROWS + 16 * n + HALF)
        qkv[HALF * n : HALF * n + HALF, 128:] = last[second][:, : CHANS - 128]
    pieces = [last[QKV_ROWS + 48 * m : QKV_ROWS + 48 * m + 48] for m in range(3)]
    pieces = [jnp.concatenate([p, jnp.zeros_like(p)], 1) for p in pieces]
    whole = [pltpu.roll(p, (60 * m - 64) % LANES, 1) for m, p in enumerate(pieces)]
    lanes = iota((PROJ_ROWS, LANES), 1)
    value = jnp.where(lanes < 60, whole[0], jnp.where(lanes < 120, whole[1], whole[2]))
    for n in range(3):
        proj[HALF * n : HALF * n + HALF] = value[16 * n : 16 * n + HALF, :CHANS]
    tiles = [last[FEED_AT + FEED_ROWS * m : FEED_AT + FEED_ROWS * (m + 1)] for m in range(3)]
    hid = up.shape[1]
    up[...] = jnp.concatenate(tiles[:2], 1).T[:CHANS, :hid]
    below = pltpu.roll(jnp.concatenate([tiles[1], tiles[2]], 1), LANES - 64, 1)
    down[...] = below.T[:CHANS, :hid]
    lines = jnp.concatenate([last[REL_AT : REL_AT + REL_ROWS], last[REL_AT + REL_ROWS : TAIL_ROWS]], 1)
    a, b = iota((LANES, LANES), 0), iota((LANES, LANES), 1)
    rel[...] = dot(lines, (a + b == RPOS - 1).astype(F32), 1, 0, HIGHEST)[:HEADS, :RPOS]
    for n, ref in enumerate(vectors):
        if n != QV_BIAS:
            ref[...] = last[VEC_AT + n : VEC_AT + n + 1, : ref.shape[1]]
    for n in range(6):
        vectors[QV_BIAS][:, HALF * n : HALF * n + HALF] = last[
            VEC_AT + QV_BIAS : VEC_AT + QV_BIAS + 1, 16 * n : 16 * n + HALF
        ]


def blocked(rows, place):
    def make(shape):
        rest = tuple(shape[1:])
        return pl.BlockSpec((rows,) + rest, lambda m: (place(m),) + (0,) * len(rest))

    return make


def resident(shape):
    return pl.BlockSpec(memory_space=pltpu.VMEM)


def untouched(shape):
    return pl.BlockSpec(memory_space=pl.ANY)


def call(kernel, scal, ins, outs, scratch=(), after=(), limit=10, flops=0, steps=None, keep=None):
    ins = [i if isinstance(i, tuple) else (i, resident) for i in ins]
    outs = [o if callable(o[-1]) else (o, resident) for o in outs]
    ins = [(a if f is resident else pltpu.with_memory_space_constraint(a, pltpu.HBM), f) for a, f in ins]
    ins += [(a, untouched) for a in after]
    first = [] if scal is None else [scal]
    specs = [pl.BlockSpec(memory_space=pltpu.SMEM)] * len(first) + [f(a.shape) for a, f in ins]
    size = sum(4 * a.size for a, f in ins if f is not untouched)
    size += sum(4 * functools.reduce(lambda p, q: p * q, s) for s, _ in outs)
    return pl.pallas_call(
        kernel,
        grid=() if steps is None else (steps,),
        in_specs=specs,
        out_specs=[f(s) for s, f in outs],
        scratch_shapes=[pltpu.VMEM(s, F32) if isinstance(s, tuple) else s for s in scratch],
        out_shape=[
            jax.ShapeDtypeStruct(tuple(s), F32) if f is resident else pltpu.HBM(tuple(s), F32)
            for s, f in outs
        ],
        input_output_aliases={i + len(first): o for i, o in (keep or {}).items()},
        compiler_params=pltpu.CompilerParams(vmem_limit_bytes=limit * MIB),
        cost_estimate=pl.CostEstimate(flops=flops, bytes_accessed=size, transcendentals=0),
    )(*first, *[a for a, _ in ins])


def body(
    images,
    item_sizes,
    cotangent,
    pre_gain,
    pre_shift,
    qkv_weight,
    qv_bias,
    rel_table,
    proj_weight,
    proj_bias,
    mid_gain,
    mid_shift,
    up_weight,
    up_bias,
    down_weight,
    down_bias,
    conv_kernel,
    conv_bias,
):
    height, breadth = images.shape[1:3]
    me = lax.axis_index("tp")
    strip = height + 2 * SHIFT
    image = images[0]
    cot = cotangent[0].transpose(2, 0, 1)
    share = CHANS // PARTS

    def frame(lanes):
        return (strip, breadth, lanes)

    vectors = [pre_gain, pre_shift, proj_bias, mid_gain, mid_shift, down_bias, conv_bias, qv_bias, up_bias]
    at_once = lambda shape: pl.BlockSpec(tuple(shape), lambda m: (0,) * len(shape))
    mine1, mine2 = call(
        pack_kernel,
        None,
        [(a, at_once) for a in (qkv_weight.T, proj_weight, up_weight, down_weight.T, *[v[None] for v in vectors])],
        [(QKV_ROWS + PROJ_ROWS + VEC_ROWS, LANES), (2 * FEED_ROWS, LANES)],
        limit=8,
        steps=1,
    )
    mine3 = conv_kernel.transpose(0, 1, 3, 2).reshape(9, share, CHANS)
    scal = jnp.stack([item_sizes[0], (me * height + IMG - SHIFT) % IMG, me]).astype(jnp.int32)
    x_first, x_last = tie((image[:SHIFT], image[-SHIFT:]), mine1)
    x_above = from_behind(x_last, "tp", 1)
    x_below = from_behind(x_first, "tp", -1)
    all1 = gather_tp(mine1, x_first, x_last)

    qkv, proj, vec, table = call(
        prepare_kernel,
        scal,
        [*all1, rel_table.T],
        [(3 * LANES, LANES), (LANES, LANES), (VEC_ROWS, 3 * LANES), (HEADS * 64, 128)],
        [(VEC_ROWS, 3 * LANES)],
        limit=8,
        flops=10**8,
    )

    def attend(edges, arrays, old):
        place = (lambda m: m * (STEPS - 1)) if edges else (lambda m: m + 1)
        ins = [*arrays, qkv, vec, table, proj]
        keep = {len(ins) + n: n for n in range(len(old))}
        ins += [(o, untouched) for o in old[:2]] + list(old[2:])
        return call(
            functools.partial(attend_kernel, edges),
            scal,
            ins,
            [
                (frame(3 * LANES), blocked(WIN, place)),
                ((STEPS, PAIRS, HEADS * 64, 128), blocked(1, place)),
                frame(LANES),
                frame(LANES),
                frame(LANES),
            ],
            [(WIN, breadth, LANES)],
            flops=5 * 10**9,
            limit=16,
            steps=2,
            keep=keep,
        )

    old = attend(False, [image], [])
    all2 = gather_tp(mine2, old[2])
    c_first, c_last = call(
        rims_kernel, None, [cot], [(SHIFT + 1, breadth, CHANS)] * 2, after=[old[2]], limit=8
    )
    c_above = from_behind(c_last, "tp", 1)
    c_below = from_behind(c_first, "tp", -1)
    mixed, probs, attended, after_attn, start = attend(True, [x_above, image, x_below], old)
    all3 = gather_tp(tie(mine3, old[2]), after_attn)
    pre, after_mlp, up, down = call(
        feed_kernel,
        scal,
        [after_attn, vec, *all2],
        [frame(HID), frame(LANES), (HID, LANES), (HID, LANES)],
        flops=5 * 10**9,
    )
    d_mid, conv_keep, conv_send, vec_conv, wide, cot_rows = call(
        conv_back_kernel,
        scal,
        [after_mlp, cot, c_above, c_below, *all3],
        [
            frame(LANES),
            (2, 9 * CONV_ROWS, LANES),
            (2, 9 * CONV_ROWS, LANES),
            (VEC_ROWS, 3 * LANES),
            (3, LANES, 3 * LANES),
            (strip + 2, breadth, LANES),
        ],
        [
            (WIN + 2, breadth, 3 * LANES),
            (3, 3 * LANES, LANES),
            (PARTS, 9, share, CHANS),
            (3, LANES, 3 * LANES),
            (9, CHANS, LANES),
        ],
        flops=2 * 10**10,
        limit=20,
    )
    got_a = lax.ppermute(conv_send, "tp", flip("tp", 1))
    d_attn, d_att, g_feed, g_proj, vec_feed = call(
        feed_back_kernel,
        scal,
        [d_mid, after_attn, pre, attended, up, down, proj, vec],
        [frame(LANES), frame(LANES), (PARTS, FEED_ROWS, HID), (LANES, LANES), (VEC_ROWS, 3 * LANES)],
        [(LANES, HID), (LANES, HID)],
        after=[conv_send],
        flops=10**10,
        limit=14,
    )
    got_a = tie(got_a, d_att)
    send_b = conv_keep[1] + got_a[1]
    got_b = lax.ppermute(send_b, "tp", flip("tp", 2))

    g_shapes = [(LANES, 3 * LANES), (HEADS * 64, 128), (8, 3 * LANES)]

    def attend_back(begin, end, old, after):
        place = lambda m: m + begin
        ins = [start, (mixed, blocked(WIN, place)), (probs, blocked(1, place)), d_att]
        outs = [((end - begin) * WIN, breadth, 3 * LANES)]
        scratch = []
        if end == STEPS:
            ins += [vec, qkv, vec_conv, vec_feed, g_feed, g_proj]
            outs += [(2, TAIL_ROWS, 128)] * 2
            scratch = g_shapes + [(VEC_ROWS, 3 * LANES), (LANES, LANES), (3 * LANES, LANES)]
        else:
            outs += g_shapes
        return call(
            functools.partial(attend_back_kernel, begin, end),
            scal,
            ins + list(old),
            outs,
            scratch,
            after=after,
            flops=5 * 10**9 * (end - begin),
            limit=16 if begin else 20,
            steps=end - begin,
        )

    d_mixed0, *sums = attend_back(0, 2, [], [send_b])
    got_b = tie(got_b, d_mixed0)
    held = conv_keep[0] + got_a[0] + got_b
    bits = dp_bits()
    d_mixed1, tail_keep, tail_send = attend_back(2, STEPS, sums, [held])
    held = dp_halve(held, bits[0], d_mixed1)

    blocks = height // WIN

    def convolve(k, old, after):
        final = k == blocks - 1
        block = (WIN, breadth, CHANS)
        scratch = [(WIN + 2, breadth, 3 * LANES)]
        if final:
            scratch += [block, pltpu.SemaphoreType.DMA((blocks,))]
        (out,) = call(
            functools.partial(conv_kernel_body, k, blocks),
            scal,
            [after_mlp, start, wide, vec] + (old if final else []),
            [((height, breadth, CHANS), untouched) if final else block],
            scratch,
            after=after,
            flops=4 * 10**9,
        )
        return out if final else old + [out]

    last_a = lax.ppermute(tail_send, "tp", flip("tp", 1))
    block_out = convolve(0, [], [tail_send, held])
    last_a = tie(last_a, block_out)
    last_send = tail_keep[1] + last_a[1]
    last_b = lax.ppermute(last_send, "tp", flip("tp", 2))
    (grad_images,) = call(
        functools.partial(image_back_kernel, 2),
        scal,
        [d_mixed0, d_mixed1, start, d_attn, cot_rows, qkv, vec],
        [((height, breadth, CHANS), untouched)],
        [(height, breadth, CHANS), pltpu.SemaphoreType.DMA((STEPS - 1,))],
        after=[last_send],
        flops=4 * 10**9,
    )
    if len(bits) > 1:
        held = dp_add(held, bits[1], grad_images)
    last_b = tie(last_b, grad_images)
    last = tail_keep[0] + last_a[0] + last_b
    for k in range(1, blocks):
        if k == 1:
            block_out = convolve(k, block_out, [last])
            last = dp_halve(last, bits[0], block_out)
        elif k <= len(bits):
            block_out = convolve(k, block_out, [last])
            step = dp_halve if k == 2 else dp_add
            last = step(last, bits[k - 1], block_out)
    grad_images = tie(grad_images, last)
    for bit in bits[2:]:
        held = dp_add(held, bit, grad_images)
    for bit in bits[blocks - 1 :]:
        last = dp_add(last, bit)
    held = dp_join(held, bits[0], last)
    block_out = tie(block_out, last)
    for bit in reversed(bits[:2]):
        last = dp_join(last, bit)

    conv = held.reshape(3, 3, CONV_ROWS, LANES)[:, :, :share, :CHANS]
    hid = up_weight.shape[1]
    g_qkv, g_proj, g_up, g_down, g_rel, *g_vec = call(
        unpack_kernel,
        None,
        [last],
        [(qkv_weight.shape[1], CHANS), (share, CHANS), (CHANS, hid), (CHANS, hid), (HEADS, RPOS)] + [(1, v.shape[0]) for v in vectors],
        limit=8,
    )

    g_vec = [g[0] for g in g_vec]
    return (
        block_out[None],
        grad_images[None],
        g_vec[PRE_GAIN],
        g_vec[PRE_SHIFT],
        g_qkv.T,
        g_vec[QV_BIAS],
        g_rel.T,
        g_proj,
        g_vec[PROJ_BIAS],
        g_vec[MID_GAIN],
        g_vec[MID_SHIFT],
        g_up,
        g_vec[UP_BIAS],
        g_down.T,
        g_vec[DOWN_BIAS],
        conv.transpose(0, 1, 3, 2),
        g_vec[CONV_BIAS],
    )


def solution(mesh):
    placed = (
        P("dp", "tp", None, None),
        P("dp"),
        P("dp", "tp", None, None),
        P("tp"),
        P("tp"),
        P(None, "tp"),
        P("tp"),
        P(),
        P("tp", None),
        P("tp"),
        P("tp"),
        P("tp"),
        P(None, "tp"),
        P("tp"),
        P("tp", None),
        P("tp"),
        P(None, None, None, "tp"),
        P("tp"),
    )
    return jax.shard_map(
        body,
        mesh=mesh,
        in_specs=placed,
        out_specs=(
            P("dp", "tp", None, None),
            P("dp", "tp", None, None),
            P("tp"),
            P("tp"),
            P(None, "tp"),
            P("tp"),
            P(),
            P("tp", None),
            P("tp"),
            P("tp"),
            P("tp"),
            P(None, "tp"),
            P("tp"),
            P("tp", None),
            P("tp"),
            P(None, None, None, "tp"),
            P("tp"),
        ),
        check_vma=False,
    )
```
